128 devices in a mesh: gx: 8 (over x, core), gy: 16 (over z, y).
Axes of the slice: x: 4, y: 4, z: 4, core: 2. Of those that a mesh axis runs over, the one named last changes fastest.
Arguments:
- fine_atmospheric_values: float32 [4, 1536, 1536], P(None, 'gx', 'gy'), may hold values from -6 to 6
- fine_skin_heat: float32 [1536, 1536], P('gx', 'gy'), may hold values from -6 to 6
- coarse_lowest_values: bfloat16 [4, 3072, 6144], P(None, 'gx', 'gy'), may hold values from -6 to 6
- holder_flat: int32 [1], replicated, may hold values from 0 to 127
- corner_offset: int32 [2], replicated, may hold values from 0 to 146
- exchange_patch_holder: int32 [18432, 1], P(('gx', 'gy')), may hold values from 0 to 127; in each aligned block of 144 rows (0 to 143, 144 to 287, ...) at most 3 rows name the same one
- holder_patch_position: int32 [18432], P(('gx', 'gy')), may hold values from 0 to 31
- coarse_interface_exchange: float32 [4, 524288], P(None, ('gx', 'gy')), may hold values from -6 to 6
- marine_stratum_values: float32 [4, 41, 524288], P(None, None, ('gx', 'gy')), may hold values from -6 to 6
- diffusion_solver_operator: float32 [41, 41], replicated, may hold values from -0.3 to 1
Outputs:
- nest_next: float32 [4, 1536, 1536], P(None, 'gx', 'gy')
- refreshed_marine_values: float32 [4, 41, 524288], P(None, None, ('gx', 'gy'))
- fine_refreshed_skin_heat: float32 [1536, 1536], P('gx', 'gy')
The draws below stay inside these ranges and needn't reach their ends.
Inputs may be any that keep to these rules, and one draw needn't show every extreme that they name: `holder_flat`: index of the tile that holds the storm. `corner_offset`: the nest lies inside the owner tile. `exchange_patch_holder`: within the blocks of one device, no ocean owner is named more than 3 times.
All inputs are finite; a program needn't handle non-finite values.
Results may differ from the reference program's by a relative error of at most 0.0019.
Values may be sent and summed in bfloat16 or wider, within the bound.
No kernel may reach another device: no remote copies, remote signals or barrier semaphores. Data moves between devices by JAX's collectives and lax.ppermute only.
A program may use at most 64 MiB of HBM per device.

```python
import math
import jax
import jax.numpy as jnp
import numpy as np
from jax import lax

FIELDS = 4
CHIP_FINE_EAST = 192
CHIP_FINE_NORTH = 96
PC = 384
EXCHANGE_PATCH = 128
MARINE_PATCHES = 32
LAYERS = 41
STEPS = 4
FINE_EASTWARD = 1536
FINE_NORTHWARD = 1536
NB = 144
CAP = 3
TOTB = 18432
OCEAN_CELLS = 524288
WINX = 238
WINY = 238
PARX = 3072
PARY = 6144
N_GX = 8
N_GY = 16
DEVICES = 128


def draw_diffusion_solver_operator(key, part):
    first_key, second_key = jax.random.split(jax.random.fold_in(key, 11))
    diagonal = jax.random.uniform(first_key, (LAYERS,), jnp.float32, 0.6, 1.0)
    spread = 0.06 * jax.random.normal(second_key, (LAYERS, LAYERS), jnp.float32)
    spread = jnp.clip(spread, -0.3, 0.3)
    identity = jnp.eye(LAYERS, dtype=jnp.float32)
    return identity * diagonal[None, :] + (1.0 - identity) * spread


def with_ends(values, own_key, least, largest):
    spot = [jax.random.randint(jax.random.fold_in(own_key, axis), (), 0, length) for axis, length in enumerate(values.shape)]
    widest = values.shape.index(max(values.shape))
    beside = spot[:widest] + [(spot[widest] + 1) % values.shape[widest]] + spot[widest + 1:]
    return values.at[tuple(spot)].set(least).at[tuple(beside)].set(largest)


def level_of(own_key, extent, shards, smallest, largest):
    level = 1.0
    for dim, shards_of in shards:
        heights = jax.random.uniform(jax.random.fold_in(jax.random.fold_in(own_key, 6), dim), (shards_of,), jnp.float32, smallest / len(shards), largest / len(shards))
        level = level * jnp.repeat(jnp.exp(heights), extent[dim] // shards_of).reshape((-1,) + (1,) * (len(extent) - 1 - dim))
    return level


def routed_block(rng, own, number, rows, amount, top, most, skew):
    ranking = jax.random.permutation(rng, amount)
    crowded, usual = portions_of(amount, rows * top, most, skew, True), portions_of(amount, rows * top, most, skew, False)
    places = jnp.arange(amount)

    def named(tallies, offset_by):
        used = int((tallies > 0).sum())
        fixed = max(1, used // 4)
        passed = fixed + (places - fixed + offset_by * (used - fixed)) % max(1, amount - fixed)
        return jnp.zeros((amount,), jnp.int32).at[ranking[jnp.where(places < fixed, places, passed)]].set(jnp.asarray(tallies, jnp.int32))

    tallies = jnp.where(number % 4 == 0, named(crowded, number // 4), named(usual, number - number // 4 - 1))
    mixed = jax.random.permutation(jax.random.fold_in(own, 3), amount)
    source_of, receiver = mixed[0:amount // 2 * 2:2], mixed[1:amount // 2 * 2:2]
    margin = jnp.minimum(tallies[source_of] - 1, most - tallies[receiver]) // 2
    margin = jnp.where((source_of == ranking[0]) | (receiver == ranking[0]) | (tallies[receiver] == 0), 0, jnp.maximum(margin, 0))
    passed = jax.random.randint(jax.random.fold_in(own, 4), (amount // 2,), 0, 1 << 20) % (margin + 1)
    tallies = tallies.at[source_of].add(-passed).at[receiver].add(passed)
    members = jnp.searchsorted(jnp.cumsum(tallies), jnp.arange(rows * top), side="right").astype(jnp.int32)
    grid = members.reshape(top, rows).T
    grid = grid[jax.random.permutation(jax.random.fold_in(own, 1), rows)]
    offset_by = jax.random.randint(jax.random.fold_in(own, 2), (rows, 1), 0, top)
    return jnp.take_along_axis(grid, (jnp.arange(top)[None, :] + offset_by) % top, axis=1)


def portions_of(amount, total, most, lean, full):
    weights = [(1 << 20) // math.isqrt(rank ** lean) + 1 for rank in range(1, amount + 1)]
    largest = most if full else min(most, max(-(-total // amount), total * weights[0] // sum(weights)))
    least = 1 if total - largest >= amount - 1 else 0
    holding, surplus = [largest] + [least] * (amount - 1), total - largest - least * (amount - 1)
    while surplus > 0:
        free = [i for i in range(1, amount) if holding[i] < largest] or [i for i in range(1, amount) if holding[i] < most]
        whole, remaining = sum([weights[i] for i in free]), surplus
        for i in free:
            more = min(most - holding[i], max(1, remaining * weights[i] // whole), surplus)
            holding[i] = holding[i] + more
            surplus = surplus - more
    return np.array(holding)


def scatter_about(key, shape, scale, bound, cuts=(), held_as=jnp.bfloat16):
    result = jax.random.normal(key, shape, jnp.float32) * scale
    if len(cuts) > 0:
        result = level_of(key, shape, cuts, -0.22, 0.18) * result
    return jnp.clip(result, min=-bound, max=bound).astype(held_as)


def setup_inputs(seed: int = 0) -> dict:
    keys = jax.random.split(jax.random.key(seed), 11)
    fine_atmospheric_values = scatter_about(keys[0], (FIELDS, FINE_EASTWARD, FINE_NORTHWARD), 1.0, 6.0, ((1, 8), (2, 16)), jnp.float32)
    fine_skin_heat = scatter_about(keys[1], (FINE_EASTWARD, FINE_NORTHWARD), 1.0, 6.0, ((0, 8), (1, 16)), jnp.float32)
    coarse_lowest_values = scatter_about(keys[2], (FIELDS, PARX, PARY), 1.0, 6.0, ((1, 8), (2, 16)))
    holder_flat = jax.random.randint(keys[3], (1,), 0, DEVICES).astype(jnp.int32)
    corner_offset = jax.random.randint(keys[4], (2,), 0, PC - max(WINX, WINY) + 1).astype(jnp.int32)
    exchange_patch_holder_keys = jax.random.split(jax.random.fold_in(keys[5], 1), TOTB // NB)
    exchange_patch_holder_turns = jax.random.permutation(jax.random.fold_in(keys[5], 3), TOTB // NB)
    exchange_patch_holder = jax.vmap(lambda own, number: routed_block(jax.random.fold_in(keys[5], 2), own, number, NB, DEVICES, 1, CAP, 2))(exchange_patch_holder_keys, exchange_patch_holder_turns).reshape((TOTB, 1))
    holder_patch_position = with_ends(jax.random.randint(keys[6], (TOTB,), 0, MARINE_PATCHES), jax.random.fold_in(keys[6], 1), 0, MARINE_PATCHES - 1).astype(jnp.int32)
    coarse_interface_exchange = scatter_about(keys[7], (FIELDS, OCEAN_CELLS), 1.0, 6.0, ((1, 128),), jnp.float32)
    marine_stratum_values = scatter_about(keys[8], (FIELDS, LAYERS, OCEAN_CELLS), 1.0, 6.0, ((2, 128),), jnp.float32)
    diffusion_solver_operator = draw_diffusion_solver_operator(jax.random.fold_in(keys[10], 71), 0)
    return {"fine_atmospheric_values": fine_atmospheric_values, "fine_skin_heat": fine_skin_heat, "coarse_lowest_values": coarse_lowest_values, "holder_flat": holder_flat, "corner_offset": corner_offset, "exchange_patch_holder": exchange_patch_holder, "holder_patch_position": holder_patch_position, "coarse_interface_exchange": coarse_interface_exchange, "marine_stratum_values": marine_stratum_values, "diffusion_solver_operator": diffusion_solver_operator}


diffuse_coef = 0.24
relax_coef = 0.3
drag_coefficient = 0.5

def hat_weights(cell_count, first_cell, anchor_cell, base_cell, parent_cells):
    fine_cells = (jnp.arange(cell_count) + first_cell).astype(jnp.float32)
    centre = (fine_cells + 0.5) * (2.0 / 13.0) - 0.5 + anchor_cell.astype(jnp.float32)
    coarse = (jnp.arange(parent_cells) + base_cell).astype(jnp.float32)
    return jnp.maximum(0.0, 1.0 - jnp.abs(centre[:, None] - coarse[None, :])).astype(jnp.bfloat16)

def reference(fine_atmospheric_values, fine_skin_heat, coarse_lowest_values, holder_flat, corner_offset, exchange_patch_holder, holder_patch_position, coarse_interface_exchange, marine_stratum_values, diffusion_solver_operator):
    row_owner = (holder_flat[0] // N_GY).astype(jnp.int32)
    col_owner = (holder_flat[0] % N_GY).astype(jnp.int32)
    zero_index = jnp.zeros((), jnp.int32)
    parent_block = lax.dynamic_slice(coarse_lowest_values, (zero_index, row_owner * PC, col_owner * PC), (FIELDS, PC, PC))
    weight_x = hat_weights(FINE_EASTWARD, 0, corner_offset[0], 0, PC)
    weight_y = hat_weights(FINE_NORTHWARD, 0, corner_offset[1], 0, PC)
    partial_value = jnp.einsum('fpq,jq->fpj', parent_block.astype(jnp.float32), weight_y.astype(jnp.float32)).astype(jnp.bfloat16)
    forcing = jnp.einsum('ip,fpj->fij', weight_x.astype(jnp.float32), partial_value.astype(jnp.float32))
    present_fine_values = fine_atmospheric_values
    for iteration in range(STEPS):
        padded = jnp.pad(present_fine_values, ((0, 0), (1, 1), (1, 1)))
        beside = padded[:, 2:, 1:-1] + padded[:, :-2, 1:-1] + padded[:, 1:-1, 2:] + padded[:, 1:-1, :-2]
        present_fine_values = present_fine_values + diffuse_coef * (beside - 4.0 * present_fine_values) + relax_coef * (forcing - present_fine_values)
    breeze_speed = jnp.sqrt(1.0 + present_fine_values[0] * present_fine_values[0] + present_fine_values[1] * present_fine_values[1])
    interface_exchange = jnp.stack([drag_coefficient * breeze_speed * (present_fine_values[2] - fine_skin_heat), drag_coefficient * breeze_speed * (present_fine_values[3] - 0.5 * fine_skin_heat), drag_coefficient * breeze_speed * present_fine_values[0], drag_coefficient * breeze_speed * present_fine_values[1]])
    tiles = interface_exchange.reshape(FIELDS, N_GX, CHIP_FINE_EAST, N_GY, CHIP_FINE_NORTH).transpose(1, 3, 0, 2, 4)
    blocks = tiles.reshape(N_GX * N_GY, FIELDS, NB, EXCHANGE_PATCH).transpose(0, 2, 1, 3).reshape(TOTB, FIELDS, EXCHANGE_PATCH)
    target_holder = exchange_patch_holder[:, 0] * MARINE_PATCHES + holder_patch_position
    group_tags = N_GX * N_GY * MARINE_PATCHES
    block_sums = jax.ops.segment_sum(blocks, target_holder, group_tags)
    counts = jax.ops.segment_sum(jnp.ones((TOTB,), jnp.float32), target_holder, group_tags)
    coarse = coarse_interface_exchange.reshape(FIELDS, group_tags, EXCHANGE_PATCH).transpose(1, 0, 2)
    uncovered = (counts == 0.0).astype(jnp.float32)
    forcing_ocean = (block_sums + coarse * uncovered[:, None, None]) / jnp.maximum(counts, 1.0)[:, None, None]
    forcing_cells = forcing_ocean.transpose(1, 0, 2).reshape(FIELDS, OCEAN_CELLS)
    forced = marine_stratum_values.at[:, 0, :].set(marine_stratum_values[:, 0, :] + forcing_cells)
    refreshed_marine_values = jnp.einsum('lk,fkc->flc', diffusion_solver_operator, forced, precision=lax.Precision.HIGHEST)
    skin_heat_gather = refreshed_marine_values[0, 0].reshape(group_tags, EXCHANGE_PATCH)
    returned_patches = skin_heat_gather[target_holder]
    fine_refreshed_skin_heat = returned_patches.reshape(N_GX, N_GY, CHIP_FINE_EAST, CHIP_FINE_NORTH).transpose(0, 2, 1, 3).reshape(FINE_EASTWARD, FINE_NORTHWARD)
    return (present_fine_values, refreshed_marine_values, fine_refreshed_skin_heat)
```

```python
import functools

import jax
import jax.numpy as jnp
from jax import lax
from jax.experimental import pallas as pl
from jax.experimental.pallas import tpu as pltpu
from jax.sharding import PartitionSpec as P

F = 4
CELLS = 128
OCEAN = 32
STEPS = 4
TX, TY = 192, 96
GX, GY = 8, 16
DEV = GX * GY
PC = 384
CAP = 3
NB = 144
HALO = 4
ROWS_X = TX + 2 * HALO
WP = 32
WQ = 18
ROWS = 20
GROUP = 4 * ROWS
PROW = 256
LEFT = tuple(
    i for i in range(GX) if i < GX - 1 and (4 * (TX * i + TX + 2) - 11) // 26 + 1 - (4 * (TX * i - 3) - 11) // 26 >= WP
)
f32, bf16, i32 = jnp.float32, jnp.bfloat16, jnp.int32

diffuse_coef = 0.24
relax_coef = 0.3
drag_coefficient = 0.5


def iota(shape, dim):
    return lax.broadcasted_iota(i32, shape, dim)


def first_x(i):
    return (4 * (TX * i - 3) - 11) // 26


def first_y(j):
    return (4 * (TY * j - 3) - 11) // 26


def first_y_of(j):
    return ((4 * TY * j + 3) * 2521 >> 16) - 1


def first_x_of(i):
    return ((4 * TX * i + 3) * 2521 >> 16) - 1


def dot(a, b):
    return jnp.dot(a, b, preferred_element_type=f32)


def dot_nt(a, b):
    return lax.dot_general(a, b, (((1,), (1,)), ((), ())), preferred_element_type=f32)


def split3(x):
    high = x.astype(bf16)
    rest = x - high.astype(f32)
    mid = rest.astype(bf16)
    return high, mid, (rest - mid.astype(f32)).astype(bf16)


def column_of(row):
    n = row.shape[1]
    return jnp.sum(jnp.where(iota((n, n), 0) == iota((n, n), 1), row, 0), axis=1, keepdims=True)


def pack_kernel(holder_ref, corner_ref, owner_ref, place_ref, parent_ref, out_ref, z_ref):
    me = lax.axis_index("gx") * GY + lax.axis_index("gy")
    mine = me == holder_ref[0]
    cx, cy = corner_ref[0], corner_ref[1]

    @pl.when(mine)
    def _():
        base = pl.multiple_of(jnp.minimum(jnp.maximum(cx - 1, 0) // 16 * 16, PC - PROW), 16)
        row = iota((GY * ROWS, 1), 0)
        j = row * 3277 >> 16
        r = row - j * ROWS
        wanted = jnp.where(r < WQ, cy + first_y_of(j) + r, -1)
        pick_y = (wanted == iota((GY * ROWS, PC), 1)).astype(f32).astype(bf16)
        parts = [parent_ref[f, pl.ds(base, PROW), :] for f in range(F)]
        across = jnp.concatenate([dot_nt(pick_y, parts[f]).astype(bf16) for f in range(F)], axis=1)
        lane = iota((1, 2 * CELLS), 1)
        for pair in range(GX // 2):
            first = jnp.where(lane < CELLS, first_x(2 * pair), first_x(2 * pair + 1))
            p = cx - base + first + (lane & (WP - 1))
            target = jnp.where((p >= 0) & (p < PROW), (lane >> 5 & 3) * PROW + p, -1)
            pick_x = (iota((F * PROW, 2 * CELLS), 0) == target).astype(f32).astype(bf16)
            window = dot(across, pick_x)
            for k in range(2):
                i = 2 * pair + k
                z_ref[pl.ds(i * GY * ROWS, GY * ROWS), :] = window[:, k * CELLS : (k + 1) * CELLS]
        j16 = iota((GY, PC), 0)
        q = iota((GY, PC), 1) - (cy + first_y_of(j16))
        inside = (q >= 0) & (q < WQ)
        lanes = iota((GY, CELLS), 1) >> 5
        erow = iota((8, PROW), 0)
        target = jnp.full((8, PROW), -1, i32)
        for k, i in enumerate(LEFT):
            target = jnp.where(erow == k, cx - base + first_x(i) + WP, target)
        pick_row = (target == iota((8, PROW), 1)).astype(f32).astype(bf16)
        left = [jnp.zeros((GY, CELLS), f32) for _ in LEFT]
        for f in range(F):
            rows = dot(pick_row, parts[f])
            for k in range(len(LEFT)):
                kept = jnp.where(inside, rows[k : k + 1, :], 0.0)
                folded = kept[:, :128] + kept[:, 128:256] + kept[:, 256:]
                folded = folded + pltpu.roll(folded, 64, 1)
                folded = folded + pltpu.roll(folded, 32, 1)
                left[k] = jnp.where(lanes == f, folded, left[k])
        for k, i in enumerate(LEFT):
            z_ref[pl.ds(i * GY * ROWS + WQ, GY, stride=ROWS), :] = left[k]

    @pl.when(jnp.logical_not(mine))
    def _():
        z_ref[...] = jnp.zeros_like(z_ref)

    owner = owner_ref[...]
    rank = jnp.sum(
        jnp.where((column_of(owner) == owner) & (iota((NB, NB), 0) < iota((NB, NB), 1)), 1, 0), axis=0, keepdims=True
    )
    named = iota((DEV, NB), 0) == owner
    slots = jnp.zeros((DEV, CELLS), f32)
    for s in range(CAP):
        value = jnp.sum(jnp.where(named & (rank == s), place_ref[...] + 1, 0).astype(f32), axis=1, keepdims=True) - 1.0
        slots = jnp.where(iota((DEV, CELLS), 1) == s, value, slots)
    z_ref[pl.ds(ROWS - 1, DEV, stride=ROWS), :] = slots
    out_ref[...] = z_ref[...].astype(bf16)


def pack(holder, corner, owner, place, parent):
    smem = pl.BlockSpec(memory_space=pltpu.SMEM)
    vmem = pl.BlockSpec(memory_space=pltpu.VMEM)
    return pl.pallas_call(
        pack_kernel,
        out_shape=jax.ShapeDtypeStruct((DEV * ROWS, CELLS), bf16),
        in_specs=[smem, smem, vmem, vmem, vmem],
        out_specs=vmem,
        scratch_shapes=[pltpu.VMEM((DEV * ROWS, CELLS), f32)],
        compiler_params=pltpu.CompilerParams(vmem_limit_bytes=32 << 20),
    )(holder, corner, owner, place, parent)


def hat(fine, anchor, coarse):
    centre = (fine.astype(f32) + 0.5) * (2.0 / 13.0) - 0.5 + anchor.astype(f32)
    return jnp.maximum(0.0, 1.0 - jnp.abs(centre - coarse.astype(f32)))


def tables_kernel(holder_ref, corner_ref, owner_ref, owner_t_ref, wx_ref, wy_ref, wyc_ref, wlast_ref, mask_ref, send_ref, back_ref):
    ix, iy = lax.axis_index("gx"), lax.axis_index("gy")
    cx, cy = corner_ref[0], corner_ref[1]
    x0, y0 = ix * TX - HALO, iy * TY - HALO
    px, qy = cx + first_x_of(ix), cy + first_y_of(iy)
    lane = iota((ROWS_X, CELLS), 1)
    row = iota((ROWS_X, CELLS), 0)
    weight = hat(row + x0, cx, (lane & (WP - 1)) + px)
    for f in range(F):
        wx_ref[f * ROWS_X : (f + 1) * ROWS_X, :] = jnp.where(lane >> 5 == f, weight, 0.0).astype(bf16)
    wlast_ref[...] = hat(row + x0, cx, jnp.full_like(row, WP) + px).astype(bf16).astype(f32)
    inside = (row + x0 >= 0) & (row + x0 < GX * TX) & (lane + y0 >= 0) & (lane + y0 < GY * TY)
    mask_ref[...] = jnp.where(inside, 1.0, 0.0)
    at = iota((CELLS, GROUP), 1) - (holder_ref[0] & 3) * ROWS
    wy_ref[...] = jnp.where(
        (at >= 0) & (at < WQ), hat(iota((CELLS, GROUP), 0) + y0, cy, at + qy), 0.0
    ).astype(bf16)
    lane = iota((CELLS, CELLS), 1)
    wyc_ref[...] = hat(iota((CELLS, CELLS), 0) + y0, cy, qy + ((lane - qy) & (WP - 1))).astype(bf16)
    owner, owner_t = owner_ref[...], owner_t_ref[...]
    at = iota((1, NB), 1)
    third = (at >= NB // CAP).astype(i32) + (at >= 2 * (NB // CAP)).astype(i32)
    number = CAP * (at - third * (NB // CAP)) + third
    rank = jnp.sum(jnp.where((column_of(owner) == owner_t) & (iota((NB, NB), 0) < number), 1, 0), axis=0, keepdims=True)
    send_ref[...] = (iota((CAP * DEV, NB), 0) == rank * DEV + owner_t).astype(f32).astype(bf16)
    back_ref[...] = (column_of(owner_t * CAP + rank) == iota((NB, CAP * DEV), 1)).astype(f32).astype(bf16)


def tables(holder, corner, owner, owner_t):
    smem = pl.BlockSpec(memory_space=pltpu.SMEM)
    vmem = pl.BlockSpec(memory_space=pltpu.VMEM)
    shapes = (
        ((F * ROWS_X, CELLS), bf16),
        ((CELLS, GROUP), bf16),
        ((CELLS, CELLS), bf16),
        ((ROWS_X, CELLS), f32),
        ((ROWS_X, CELLS), f32),
        ((CAP * DEV, NB), bf16),
        ((NB, CAP * DEV), bf16),
    )
    return pl.pallas_call(
        tables_kernel,
        out_shape=tuple(jax.ShapeDtypeStruct(s, d) for s, d in shapes),
        in_specs=[smem, smem, vmem, vmem],
        out_specs=tuple(vmem for _ in shapes),
    )(holder, corner, owner, owner_t)


def columns_kernel(s_ref, low_ref, high_ref):
    for f in range(F):
        turned = jnp.swapaxes(s_ref[f], 0, 1)
        low_ref[f * HALO : (f + 1) * HALO, :] = turned[:HALO, :]
        high_ref[f * HALO : (f + 1) * HALO, :] = turned[TY - HALO :, :]


def widen_kernel(s_ref, left_ref, right_ref, out_ref, low_ref, high_ref):
    n = F * HALO
    both = jnp.concatenate([left_ref[...], right_ref[...], jnp.zeros((CELLS - 2 * n, TX), f32)], axis=0)
    turned = jnp.swapaxes(both, 0, 1)
    lane = iota((TX, CELLS), 1)
    for f in range(F):
        out_ref[f] = jnp.zeros((TX, CELLS), f32)
        out_ref[f, :, HALO : HALO + TY] = s_ref[f]
        before = turned if f == 0 else pltpu.roll(turned, CELLS - HALO * f, 1)
        after = pltpu.roll(turned, TY + HALO - n - HALO * f, 1)
        wide = jnp.where(lane < HALO, before, jnp.where((lane >= TY + HALO) & (lane < TY + 2 * HALO), after, out_ref[f]))
        out_ref[f] = wide
        low_ref[f * HALO : (f + 1) * HALO, :] = wide[:HALO]
        high_ref[f * HALO : (f + 1) * HALO, :] = wide[TX - HALO :]


def nest_kernel(
    holder_ref, got_ref, wx_ref, wy_ref, wyc_ref, wlast_ref, mask_ref, s_ref, before_ref, after_ref, skin_ref, send_ref,
    next_ref, out_ref, state_ref, force_ref, flux_ref, z_ref,
):
    got = got_ref[...]
    partial = dot(wy_ref[...], got).astype(bf16)
    last = jnp.sum(
        jnp.where(iota((GROUP, CELLS), 0) == (holder_ref[0] & 3) * ROWS + WQ, got.astype(f32), 0.0), axis=0, keepdims=True
    )
    field = iota((8, CELLS), 0)
    last = jnp.where(iota((8, CELLS), 1) >> 5 == field, last, 0.0).astype(bf16)
    partial_last = dot_nt(last, wyc_ref[...]).astype(bf16).astype(f32)
    force_ref[...] = dot_nt(wx_ref[...], partial)
    mask = mask_ref[...]
    for f in range(F):
        force = force_ref[f * ROWS_X : (f + 1) * ROWS_X, :] + wlast_ref[...] * partial_last[f : f + 1, :]
        force = relax_coef * force
        state_ref[:HALO, :] = before_ref[f * HALO : (f + 1) * HALO, :]
        state_ref[HALO : HALO + TX, :] = s_ref[f]
        state_ref[HALO + TX :, :] = after_ref[f * HALO : (f + 1) * HALO, :]
        s = state_ref[...]
        for _ in range(STEPS):
            beside = (
                pltpu.roll(s, 1, 0) + pltpu.roll(s, ROWS_X - 1, 0) + pltpu.roll(s, 1, 1) + pltpu.roll(s, CELLS - 1, 1)
            )
            s = mask * ((1.0 - 4.0 * diffuse_coef - relax_coef) * s + diffuse_coef * beside + force)
        state_ref[...] = pltpu.roll(s, CELLS - HALO, 1)
        next_ref[f] = state_ref[HALO : HALO + TX, :TY]
    u, v, ta, qa = next_ref[0], next_ref[1], next_ref[2], next_ref[3]
    half = drag_coefficient * jnp.sqrt(1.0 + u * u + v * v)
    skin = skin_ref[...]
    flux = (half * (ta - skin), half * (qa - 0.5 * skin), half * u, half * v)
    rows = NB // CAP
    lane = iota((rows, CELLS), 1)
    blocks = []
    for f in range(F):
        flux_ref[:, :TY] = flux[f]
        m = [flux_ref[pl.ds(k, rows, stride=4), :] for k in range(4)]
        r1, r2, r3 = pltpu.roll(m[1], 96, 1), pltpu.roll(m[2], 64, 1), pltpu.roll(m[3], 32, 1)
        blocks.append(
            jnp.concatenate(
                [jnp.where(lane < 96, m[0], r1), jnp.where(lane < 64, r1, r2), jnp.where(lane < 32, r2, r3)], axis=0
            ).astype(bf16)
        )
    sent = dot(send_ref[...], jnp.concatenate(blocks, axis=1))
    for slot in range(CAP):
        for f in range(F):
            z_ref[pl.ds(slot * F + f, DEV, stride=CAP * F), :] = sent[
                slot * DEV : (slot + 1) * DEV, f * CELLS : (f + 1) * CELLS
            ]
    out_ref[...] = z_ref[...].astype(bf16)


def nest(holder, got, wx, wy, wyc, wlast, mask, s, before, after, skin, send):
    def whole(shape):
        return pl.BlockSpec(shape, lambda _, h: (0,) * len(shape))

    rest = (wx, wy, wyc, wlast, mask, s, before, after, skin, send)
    return pl.pallas_call(
        nest_kernel,
        out_shape=(
            jax.ShapeDtypeStruct((F, TX, TY), f32),
            jax.ShapeDtypeStruct((DEV * CAP * F, CELLS), bf16),
        ),
        grid_spec=pltpu.PrefetchScalarGridSpec(
            num_scalar_prefetch=1,
            grid=(1,),
            in_specs=[pl.BlockSpec((GROUP, CELLS), lambda _, h: (h[0] >> 2, 0))] + [whole(a.shape) for a in rest],
            out_specs=(whole((F, TX, TY)), whole((DEV * CAP * F, CELLS))),
            scratch_shapes=[
                pltpu.VMEM((ROWS_X, CELLS), f32),
                pltpu.VMEM((F * ROWS_X, CELLS), f32),
                pltpu.VMEM((TX, CELLS), f32),
                pltpu.VMEM((DEV * CAP * F, CELLS), f32),
            ],
        ),
        compiler_params=pltpu.CompilerParams(vmem_limit_bytes=32 << 20),
    )(holder, got, *rest)


def ocean_kernel(scale_ref, got_ref, hot_ref, inverse_ref, kept_ref, base_ref, give_ref, forcing_ref, out_ref):
    forcing = dot(hot_ref[...], got_ref[...]) * inverse_ref[...] + kept_ref[...]
    forcing_ref[...] = forcing
    top = base_ref[...] + scale_ref[0, 0] * forcing
    back = dot(give_ref[...], jnp.concatenate(split3(top), axis=1))
    out_ref[...] = back[:, :CELLS] + back[:, CELLS : 2 * CELLS] + back[:, 2 * CELLS :]


def skin_kernel(got_ref, back_ref, out_ref, tile_ref):
    x = dot(back_ref[...], jnp.concatenate(split3(got_ref[...]), axis=1))
    x = x[:, :CELLS] + x[:, CELLS : 2 * CELLS] + x[:, 2 * CELLS :]
    rows = NB // CAP
    t0, t1, t2 = x[:rows], x[rows : 2 * rows], x[2 * rows :]
    lane = iota((rows, CELLS), 1)
    tile_ref[pl.ds(0, rows, stride=4), :] = t0
    tile_ref[pl.ds(1, rows, stride=4), :] = pltpu.roll(jnp.where(lane < 64, t1, t0), 32, 1)
    tile_ref[pl.ds(2, rows, stride=4), :] = pltpu.roll(jnp.where(lane < 32, t2, t1), 64, 1)
    tile_ref[pl.ds(3, rows, stride=4), :] = pltpu.roll(t2, 96, 1)
    out_ref[...] = tile_ref[:, :TY]


def call(kernel, outs, *args, smem=(), scratch=()):
    vmem = pl.BlockSpec(memory_space=pltpu.VMEM)
    return pl.pallas_call(
        kernel,
        out_shape=outs,
        in_specs=[pl.BlockSpec(memory_space=pltpu.SMEM) if k in smem else vmem for k in range(len(args))],
        out_specs=jax.tree.map(lambda _: vmem, outs),
        scratch_shapes=scratch,
    )(*args)


def shift(value, axis, by):
    n = lax.axis_size(axis)
    return lax.ppermute(value, axis, [(i, i + by) for i in range(n) if 0 <= i + by < n])


def exchange(value, rows):
    split = value.reshape(rows)
    return lax.all_to_all(split, ("gx", "gy"), split_axis=0, concat_axis=0, tiled=True).reshape(value.shape)


def by_block(value):
    return value.reshape(F, OCEAN, CELLS).transpose(1, 0, 2).reshape(OCEAN * F, CELLS)


def on_device(
    fine_atmospheric_values,
    fine_skin_heat,
    coarse_lowest_values,
    holder_flat,
    corner_offset,
    exchange_patch_holder,
    holder_patch_position,
    coarse_interface_exchange,
    marine_stratum_values,
    diffusion_solver_operator,
):
    sds = jax.ShapeDtypeStruct
    owner = exchange_patch_holder.reshape(1, NB)
    owner_t = owner.reshape(NB // CAP, CAP).T.reshape(1, NB)
    place = holder_patch_position.reshape(1, NB)
    windows = pack(holder_flat, corner_offset, owner, place, coarse_lowest_values)
    got = exchange(windows, (DEV, ROWS // 4, 4, CELLS))
    strip = sds((F * HALO, TX), f32)
    low, high = call(columns_kernel, (strip, strip), fine_atmospheric_values)
    left, right = shift(high, "gy", 1), shift(low, "gy", -1)
    strip = sds((F * HALO, CELLS), f32)
    wide, low, high = call(
        widen_kernel, (sds((F, TX, CELLS), f32), strip, strip), fine_atmospheric_values, left, right
    )
    before, after = shift(high, "gx", 1), shift(low, "gx", -1)
    *weights, send, back = tables(holder_flat, corner_offset, owner, owner_t)
    nest_next, flux = nest(holder_flat, got, *weights, wide, before, after, fine_skin_heat, send)
    got_flux = exchange(flux, (DEV, CAP, F, CELLS))
    marine = marine_stratum_values.transpose(1, 0, 2)
    base = jnp.einsum("lk,kfc->lfc", diffusion_solver_operator, marine, precision=lax.Precision.HIGHEST)
    slot = got.reshape(DEV, ROWS, CELLS)[:, ROWS - 1, :CAP].astype(i32).reshape(DEV * CAP)
    target = jnp.where(slot >= 0, slot * F, -F)[:, None] + jnp.arange(F)[None, :]
    hot = jnp.arange(OCEAN * F)[:, None] == target.reshape(1, DEV * CAP * F)
    give = (slot[:, None] * F == jnp.arange(OCEAN * F)[None, :]).astype(bf16)
    count = jnp.sum(hot.astype(f32), axis=1, keepdims=True)
    ones = jnp.ones((1, CELLS), f32)
    inverse = ones / jnp.maximum(count, 1.0)
    kept = by_block(coarse_interface_exchange) * (count == 0.0).astype(f32)
    block = sds((OCEAN * F, CELLS), f32)
    forcing, returned = call(
        ocean_kernel, (block, sds((DEV * CAP, CELLS), f32)),
        diffusion_solver_operator, got_flux, hot.astype(bf16), inverse, kept, by_block(base[0]), give, smem=(0,),
    )
    arrived = exchange(returned, (DEV, 1, CAP * CELLS))
    cells = forcing.reshape(OCEAN, F, CELLS).transpose(1, 0, 2).reshape(F, OCEAN * CELLS)
    refreshed = base + diffusion_solver_operator[:, 0][:, None, None] * cells[None]
    skin = call(
        skin_kernel, sds((TX, TY), f32), arrived, back, scratch=[pltpu.VMEM((TX, CELLS), f32)]
    )
    return (nest_next, refreshed.transpose(1, 0, 2), skin)


def solution(mesh):
    in_specs = (
        P(None, "gx", "gy"),
        P("gx", "gy"),
        P(None, "gx", "gy"),
        P(),
        P(),
        P(("gx", "gy"), None),
        P(("gx", "gy")),
        P(None, ("gx", "gy")),
        P(None, None, ("gx", "gy")),
        P(),
    )
    out_specs = (P(None, "gx", "gy"), P(None, None, ("gx", "gy")), P("gx", "gy"))
    return jax.shard_map(
        on_device, mesh=mesh, in_specs=in_specs, out_specs=out_specs, check_vma=False
    )
```

```python
import jax
import jax.numpy as jnp
from jax import lax
from jax.experimental import pallas as pl
from jax.experimental.pallas import tpu as pltpu
from jax.sharding import PartitionSpec as P

F = 4
CELLS = 128
OCEAN = 32
STEPS = 4
TX, TY = 192, 96
GX, GY = 8, 16
DEV = GX * GY
PC = 384
CAP = 3
NB = 144
HALO = 4
ROWS_X = TX + 2 * HALO
WP = 32
WQ = 18
ROWS = 20
GROUP = 4 * ROWS
PROW = 256
LEFT = tuple(
    i for i in range(GX) if i < GX - 1 and (4 * (TX * i + TX + 2) - 11) // 26 + 1 - (4 * (TX * i - 3) - 11) // 26 >= WP
)
f32, bf16, i32 = jnp.float32, jnp.bfloat16, jnp.int32

diffuse_coef = 0.24
relax_coef = 0.3
drag_coefficient = 0.5


def iota(shape, dim):
    return lax.broadcasted_iota(i32, shape, dim)


def first_x(i):
    return (4 * (TX * i - 3) - 11) // 26


def first_y(j):
    return (4 * (TY * j - 3) - 11) // 26


def first_y_of(j):
    return ((4 * TY * j + 3) * 2521 >> 16) - 1


def first_x_of(i):
    return ((4 * TX * i + 3) * 2521 >> 16) - 1


def dot(a, b):
    return jnp.dot(a, b, preferred_element_type=f32)


def dot_nt(a, b):
    return lax.dot_general(a, b, (((1,), (1,)), ((), ())), preferred_element_type=f32)


def split3(x):
    high = x.astype(bf16)
    rest = x - high.astype(f32)
    mid = rest.astype(bf16)
    return high, mid, (rest - mid.astype(f32)).astype(bf16)


def column_of(row):
    n = row.shape[1]
    return jnp.sum(jnp.where(iota((n, n), 0) == iota((n, n), 1), row, 0), axis=1, keepdims=True)


def fetch(pairs, sems):
    copies = [pltpu.make_async_copy(src, dst, sems.at[k]) for k, (src, dst) in enumerate(pairs)]
    for copy in copies:
        copy.start()
    return copies


def rank_of(column, row, number):
    return jnp.sum(jnp.where((column == row) & (iota((NB, NB), 0) < number), 1, 0), axis=0, keepdims=True)


def by_thirds(column):
    at = iota((1, NB), 1)
    third = (at >= NB // CAP).astype(i32) + (at >= 2 * (NB // CAP)).astype(i32)
    number = CAP * (at - third * (NB // CAP)) + third
    return number, jnp.sum(jnp.where(iota((NB, NB), 0) == number, column, 0), axis=0, keepdims=True)


def pack_kernel(holder_ref, corner_ref, owner_any, place_any, parent_any, out_any, owner_ref, place_ref, parent_ref, z_ref, out_ref, sems):
    me = lax.axis_index("gx") * GY + lax.axis_index("gy")
    mine = me == holder_ref[0]
    cx, cy = corner_ref[0], corner_ref[1]
    base = pl.multiple_of(jnp.minimum(jnp.maximum(cx - 1, 0) // 16 * 16, PC - PROW), 16)
    small = fetch([(owner_any, owner_ref), (place_any, place_ref)], sems)
    tile = pltpu.make_async_copy(parent_any.at[:, pl.ds(base, PROW), :], parent_ref, sems.at[2])

    @pl.when(mine)
    def _():
        tile.start()

    for copy in small:
        copy.wait()
    owner = owner_ref[...]
    rank = rank_of(column_of(owner), owner, iota((NB, NB), 1))
    named = iota((DEV, NB), 0) == owner
    slots = jnp.zeros((DEV, CELLS), f32)
    for s in range(CAP):
        value = jnp.sum(jnp.where(named & (rank == s), place_ref[...] + 1, 0).astype(f32), axis=1, keepdims=True) - 1.0
        slots = jnp.where(iota((DEV, CELLS), 1) == s, value, slots)

    @pl.when(mine)
    def _():
        row = iota((GY * ROWS, 1), 0)
        j = row * 3277 >> 16
        r = row - j * ROWS
        wanted = jnp.where(r < WQ, cy + first_y_of(j) + r, -1)
        pick_y = (wanted == iota((GY * ROWS, PC), 1)).astype(f32).astype(bf16)
        tile.wait()
        parts = [parent_ref[f] for f in range(F)]
        across = jnp.concatenate([dot_nt(pick_y, parts[f]).astype(bf16) for f in range(F)], axis=1)
        lane = iota((1, 2 * CELLS), 1)
        for pair in range(GX // 2):
            first = jnp.where(lane < CELLS, first_x(2 * pair), first_x(2 * pair + 1))
            p = cx - base + first + (lane & (WP - 1))
            target = jnp.where((p >= 0) & (p < PROW), (lane >> 5 & 3) * PROW + p, -1)
            pick_x = (iota((F * PROW, 2 * CELLS), 0) == target).astype(f32).astype(bf16)
            window = dot(across, pick_x)
            for k in range(2):
                i = 2 * pair + k
                z_ref[pl.ds(i * GY * ROWS, GY * ROWS), :] = window[:, k * CELLS : (k + 1) * CELLS]
        j16 = iota((GY, PC), 0)
        q = iota((GY, PC), 1) - (cy + first_y_of(j16))
        inside = (q >= 0) & (q < WQ)
        lanes = iota((GY, CELLS), 1) >> 5
        erow = iota((8, PROW), 0)
        target = jnp.full((8, PROW), -1, i32)
        for k, i in enumerate(LEFT):
            target = jnp.where(erow == k, cx - base + first_x(i) + WP, target)
        pick_row = (target == iota((8, PROW), 1)).astype(f32).astype(bf16)
        left = [jnp.zeros((GY, CELLS), f32) for _ in LEFT]
        for f in range(F):
            rows = dot(pick_row, parts[f])
            for k in range(len(LEFT)):
                kept = jnp.where(inside, rows[k : k + 1, :], 0.0)
                folded = kept[:, :128] + kept[:, 128:256] + kept[:, 256:]
                folded = folded + pltpu.roll(folded, 64, 1)
                folded = folded + pltpu.roll(folded, 32, 1)
                left[k] = jnp.where(lanes == f, folded, left[k])
        for k, i in enumerate(LEFT):
            z_ref[pl.ds(i * GY * ROWS + WQ, GY, stride=ROWS), :] = left[k]

    @pl.when(jnp.logical_not(mine))
    def _():
        z_ref[...] = jnp.zeros_like(z_ref)

    z_ref[pl.ds(ROWS - 1, DEV, stride=ROWS), :] = slots
    out_ref[...] = z_ref[...].astype(bf16)
    done = pltpu.make_async_copy(out_ref, out_any, sems.at[3])
    done.start()
    done.wait()


def hat(fine, anchor, coarse):
    centre = (fine.astype(f32) + 0.5) * (2.0 / 13.0) - 0.5 + anchor.astype(f32)
    return jnp.maximum(0.0, 1.0 - jnp.abs(centre - coarse.astype(f32)))


def columns_kernel(s_ref, low_ref, high_ref, wide_ref):
    field = iota((TX, CELLS), 1) >> 2
    wide_ref[...] = jnp.zeros_like(wide_ref)
    low, high = jnp.zeros((TX, CELLS), f32), jnp.zeros((TX, CELLS), f32)
    for f in range(F):
        wide_ref[:, :TY] = s_ref[f]
        s = wide_ref[...]
        low = jnp.where(field == f, s if f == 0 else pltpu.roll(s, HALO * f, 1), low)
        high = jnp.where(field == f, pltpu.roll(s, CELLS - TY + HALO + HALO * f, 1), high)
    low_ref[...] = low
    high_ref[...] = high


def widened(s, left, right, f):
    lane = iota(s.shape, 1)
    before = left if f == 0 else pltpu.roll(left, CELLS - HALO * f, 1)
    after = pltpu.roll(right, TY + HALO - HALO * f, 1)
    wide = jnp.where(lane < TY + HALO, pltpu.roll(s, HALO, 1), after)
    return jnp.where(lane < HALO, before, jnp.where(lane < TY + 2 * HALO, wide, 0.0))


def rows_kernel(s_any, left_any, right_any, low_ref, high_ref, s_ref, left_ref, right_ref, wide_ref, sems):
    ends = ((0, 0), (8, TX - 8))
    pairs = [(s_any.at[:, pl.ds(src, 8), :], s_ref.at[:, pl.ds(dst, 8), :]) for dst, src in ends]
    pairs += [(left_any.at[pl.ds(src, 8), :], left_ref.at[pl.ds(dst, 8), :]) for dst, src in ends]
    pairs += [(right_any.at[pl.ds(src, 8), :], right_ref.at[pl.ds(dst, 8), :]) for dst, src in ends]
    for copy in fetch(pairs, sems):
        copy.wait()
    wide_ref[...] = jnp.zeros_like(wide_ref)
    for f in range(F):
        wide_ref[:, :TY] = s_ref[f]
        wide = widened(wide_ref[...], left_ref[...], right_ref[...], f)
        low_ref[f * HALO : (f + 1) * HALO, :] = wide[:HALO]
        high_ref[f * HALO : (f + 1) * HALO, :] = wide[16 - HALO :]


def nest_kernel(
    holder_ref, corner_ref, got_any, s_any, left_any, right_any, before_any, after_any, skin_any, owner_any,
    next_any, out_any,
    got_ref, s_ref, left_ref, right_ref, before_ref, after_ref, skin_ref, owner_ref, next_ref, out_ref,
    wx_ref, wide_ref, state_ref, force_ref, flux_ref, z_ref, sems,
):
    group = pl.multiple_of((holder_ref[0] >> 2) * GROUP, GROUP)
    pairs = [
        (owner_any, owner_ref), (got_any.at[pl.ds(group, GROUP), :], got_ref), (s_any, s_ref), (left_any, left_ref),
        (right_any, right_ref), (before_any, before_ref), (after_any, after_ref), (skin_any, skin_ref),
    ]
    copies = fetch(pairs, sems)
    ix, iy = lax.axis_index("gx"), lax.axis_index("gy")
    cx, cy = corner_ref[0], corner_ref[1]
    x0, y0 = ix * TX - HALO, iy * TY - HALO
    px, qy = cx + first_x_of(ix), cy + first_y_of(iy)
    lane = iota((ROWS_X, CELLS), 1)
    row = iota((ROWS_X, CELLS), 0)
    weight = hat(row + x0, cx, (lane & (WP - 1)) + px)
    for f in range(F):
        wx_ref[f * ROWS_X : (f + 1) * ROWS_X, :] = jnp.where(lane >> 5 == f, weight, 0.0).astype(bf16)
    weight_last = relax_coef * hat(row + x0, cx, jnp.full_like(row, WP) + px).astype(bf16).astype(f32)
    inside = (row + x0 >= 0) & (row + x0 < GX * TX) & (lane + y0 >= 0) & (lane + y0 < GY * TY)
    mask = jnp.where(inside, 1.0, 0.0)
    at = iota((CELLS, GROUP), 1) - (holder_ref[0] & 3) * ROWS
    weight_y = jnp.where((at >= 0) & (at < WQ), hat(iota((CELLS, GROUP), 0) + y0, cy, at + qy), 0.0).astype(bf16)
    lane = iota((CELLS, CELLS), 1)
    weight_c = hat(iota((CELLS, CELLS), 0) + y0, cy, qy + ((lane - qy) & (WP - 1))).astype(bf16)
    wide_ref[...] = jnp.zeros_like(wide_ref)
    flux_ref[...] = jnp.zeros_like(flux_ref)
    copies[0].wait()
    column = column_of(owner_ref[...])
    number, owner = by_thirds(column)
    send = (iota((CAP * DEV, NB), 0) == rank_of(column, owner, number) * DEV + owner).astype(f32).astype(bf16)
    copies[1].wait()
    got = got_ref[...]
    partial = dot(weight_y, got).astype(bf16)
    last = jnp.sum(
        jnp.where(iota((GROUP, CELLS), 0) == (holder_ref[0] & 3) * ROWS + WQ, got.astype(f32), 0.0), axis=0, keepdims=True
    )
    last = jnp.where(iota((8, CELLS), 1) >> 5 == iota((8, CELLS), 0), last, 0.0).astype(bf16)
    partial_last = dot_nt(last, weight_c).astype(bf16).astype(f32)
    force_ref[...] = dot_nt(wx_ref[...], partial)
    for copy in copies[2:]:
        copy.wait()
    left, right = left_ref[...], right_ref[...]
    written = []
    for f in range(F):
        force = relax_coef * force_ref[f * ROWS_X : (f + 1) * ROWS_X, :] + weight_last * partial_last[f : f + 1, :]
        wide_ref[:, :TY] = s_ref[f]
        state_ref[:HALO, :] = before_ref[f * HALO : (f + 1) * HALO, :]
        state_ref[HALO : HALO + TX, :] = widened(wide_ref[...], left, right, f)
        state_ref[HALO + TX :, :] = after_ref[f * HALO : (f + 1) * HALO, :]
        s = state_ref[...]
        for _ in range(STEPS):
            beside = (
                pltpu.roll(s, 1, 0) + pltpu.roll(s, ROWS_X - 1, 0) + pltpu.roll(s, 1, 1) + pltpu.roll(s, CELLS - 1, 1)
            )
            s = mask * ((1.0 - 4.0 * diffuse_coef - relax_coef) * s + diffuse_coef * beside + force)
        state_ref[...] = pltpu.roll(s, CELLS - HALO, 1)
        next_ref[f] = state_ref[HALO : HALO + TX, :TY]
        written.append(pltpu.make_async_copy(next_ref.at[f], next_any.at[f], sems.at[len(pairs) + f]))
        written[f].start()
    u, v, ta, qa = next_ref[0], next_ref[1], next_ref[2], next_ref[3]
    half = drag_coefficient * jnp.sqrt(1.0 + u * u + v * v)
    skin = skin_ref[...]
    flux = (half * (ta - skin), half * (qa - 0.5 * skin), half * u, half * v)
    rows = NB // CAP
    lane = iota((rows, CELLS), 1)
    blocks = []
    for f in range(F):
        flux_ref[:, :TY] = flux[f]
        m = [flux_ref[pl.ds(k, rows, stride=4), :] for k in range(4)]
        r1, r2, r3 = pltpu.roll(m[1], 96, 1), pltpu.roll(m[2], 64, 1), pltpu.roll(m[3], 32, 1)
        blocks.append(
            jnp.concatenate(
                [jnp.where(lane < 96, m[0], r1), jnp.where(lane < 64, r1, r2), jnp.where(lane < 32, r2, r3)], axis=0
            ).astype(bf16)
        )
    sent = dot(send, jnp.concatenate(blocks, axis=1))
    for slot in range(CAP):
        for f in range(F):
            z_ref[pl.ds(slot * F + f, DEV, stride=CAP * F), :] = sent[
                slot * DEV : (slot + 1) * DEV, f * CELLS : (f + 1) * CELLS
            ]
    out_ref[...] = z_ref[...].astype(bf16)
    written.append(pltpu.make_async_copy(out_ref, out_any, sems.at[len(pairs) + F]))
    written[F].start()
    for copy in written:
        copy.wait()


def hot_kernel(got_any, kept_any, hot_ref, give_ref, inverse_ref, cover_ref, got_ref, kept_ref, z_ref, slot_ref, row_ref, sems):
    copies = fetch([(got_any, got_ref), (kept_any, kept_ref)], sems)
    for copy in copies:
        copy.wait()
    slot_ref[...] = got_ref[...].astype(f32)
    slots = slot_ref[pl.ds(ROWS - 1, DEV, stride=ROWS), :].astype(i32)
    lane = iota((DEV, OCEAN * F), 1)
    for s in range(CAP):
        target = slots[:, s : s + 1] * F
        for f in range(F):
            z_ref[pl.ds(s * F + f, DEV, stride=CAP * F), :] = (lane == jnp.where(target < 0, -1, target + f)).astype(f32)
        row_ref[pl.ds(s, DEV, stride=CAP), :] = (lane == target).astype(f32)
    give_ref[...] = row_ref[...].astype(bf16)
    hot = jnp.swapaxes(z_ref[...], 0, 1)
    hot_ref[...] = hot.astype(bf16)
    count = jnp.sum(hot, axis=1, keepdims=True)
    inverse_ref[...] = jnp.broadcast_to(1.0 / jnp.maximum(count, 1.0), (OCEAN * F, CELLS))
    cover_ref[...] = jnp.where(count == 0.0, kept_ref[...], 0.0)


def top_kernel(scale_ref, marine_ref, out_ref):
    total = scale_ref[0, 0] * marine_ref[0]
    for k in range(1, marine_ref.shape[0]):
        total = total + scale_ref[0, k] * marine_ref[k]
    out_ref[: OCEAN * F, :] = total
    out_ref[OCEAN * F :, :] = jnp.full((8, CELLS), scale_ref[0, 0], f32)


def ocean_kernel(
    got_any, hot_any, inverse_any, cover_any, top_any, give_any, forcing_any, out_any,
    got_ref, hot_ref, inverse_ref, cover_ref, top_ref, give_ref, forcing_ref, out_ref, sems,
):
    pairs = [
        (hot_any, hot_ref), (got_any, got_ref), (inverse_any, inverse_ref), (cover_any, cover_ref), (top_any, top_ref),
        (give_any, give_ref),
    ]
    for copy in fetch(pairs, sems):
        copy.wait()
    forcing = dot(hot_ref[...], got_ref[...]) * inverse_ref[...] + cover_ref[...]
    forcing_ref[...] = forcing
    top = top_ref[: OCEAN * F, :] + top_ref[OCEAN * F : OCEAN * F + 1, :] * forcing
    back = dot(give_ref[...], jnp.concatenate(split3(top), axis=1))
    out_ref[...] = back[:, :CELLS] + back[:, CELLS : 2 * CELLS] + back[:, 2 * CELLS :]
    a = pltpu.make_async_copy(out_ref, out_any, sems.at[0])
    b = pltpu.make_async_copy(forcing_ref, forcing_any, sems.at[1])
    a.start()
    b.start()
    a.wait()
    b.wait()


def mix_kernel(scale_ref, forcing_ref, marine_ref, out_ref, high_ref, low_ref):
    layers = marine_ref.shape[0]
    n = 8 * layers

    @pl.when(pl.program_id(0) == 0)
    def _():
        spread = (iota((n, layers), 0) >> 3 == iota((n, layers), 1)).astype(f32).astype(bf16)
        same = (iota((n, n), 0) & 7) == (iota((n, n), 1) & 7)
        scale = scale_ref[...]
        high = scale.astype(bf16)
        low = (scale - high.astype(f32)).astype(bf16)
        for part, ref in ((high, high_ref), (low, low_ref)):
            wide = dot_nt(dot(spread, part).astype(bf16), spread)
            ref[...] = jnp.where(same, wide, 0.0).astype(bf16)

    groups = marine_ref.shape[1] // 8
    columns = []
    for g in range(groups):
        x = marine_ref[:, 8 * g : 8 * g + 8, :].reshape(n, CELLS)
        first = x[:8] + forcing_ref[8 * g : 8 * g + 8, :]
        columns.append(jnp.concatenate([first, x[8:]], axis=0))
    x = jnp.concatenate(columns, axis=1)
    high = x.astype(bf16)
    low = (x - high.astype(f32)).astype(bf16)
    y = dot(high_ref[...], high) + (dot(high_ref[...], low) + dot(low_ref[...], high))
    for g in range(groups):
        out_ref[:, 8 * g : 8 * g + 8, :] = y[:, g * CELLS : (g + 1) * CELLS].reshape(layers, 8, CELLS)


def skin_kernel(got_any, owner_any, out_ref, got_ref, owner_ref, tile_ref, sems):
    copies = fetch([(owner_any, owner_ref), (got_any, got_ref)], sems)
    copies[0].wait()
    column = column_of(owner_ref[...])
    number, owner = by_thirds(column)
    source = column_of(owner * CAP + rank_of(column, owner, number))
    back = (source == iota((NB, CAP * DEV), 1)).astype(f32).astype(bf16)
    copies[1].wait()
    x = dot(back, jnp.concatenate(split3(got_ref[...]), axis=1))
    x = x[:, :CELLS] + x[:, CELLS : 2 * CELLS] + x[:, 2 * CELLS :]
    rows = NB // CAP
    t0, t1, t2 = x[:rows], x[rows : 2 * rows], x[2 * rows :]
    lane = iota((rows, CELLS), 1)
    tile_ref[pl.ds(0, rows, stride=4), :] = t0
    tile_ref[pl.ds(1, rows, stride=4), :] = pltpu.roll(jnp.where(lane < 64, t1, t0), 32, 1)
    tile_ref[pl.ds(2, rows, stride=4), :] = pltpu.roll(jnp.where(lane < 32, t2, t1), 64, 1)
    tile_ref[pl.ds(3, rows, stride=4), :] = pltpu.roll(t2, 96, 1)
    out_ref[...] = tile_ref[:, :TY]


SPACES = {
    "s": pl.BlockSpec(memory_space=pltpu.SMEM),
    "v": pl.BlockSpec(memory_space=pltpu.VMEM),
    "h": pl.BlockSpec(memory_space=pltpu.HBM),
    "a": pl.BlockSpec(memory_space=pl.ANY),
}


def call(kernel, ins, outs, args, shapes, scratch=(), copies=0):
    return pl.pallas_call(
        kernel,
        out_shape=tuple(jax.ShapeDtypeStruct(s, d) for s, d in shapes),
        in_specs=[SPACES[c] for c in ins],
        out_specs=tuple(SPACES[c] for c in outs),
        scratch_shapes=[pltpu.VMEM(s, d) for s, d in scratch] + ([pltpu.SemaphoreType.DMA((copies,))] if copies else []),
        compiler_params=pltpu.CompilerParams(vmem_limit_bytes=40 << 20),
    )(*args)


def shift(value, axis, by):
    n = lax.axis_size(axis)
    return lax.ppermute(value, axis, [(i, i + by) for i in range(n) if 0 <= i + by < n])


def exchange(value, rows):
    split = value.reshape(rows)
    return lax.all_to_all(split, ("gx", "gy"), split_axis=0, concat_axis=0, tiled=True).reshape(value.shape)


def by_block(value):
    return value.reshape(F, OCEAN, CELLS).transpose(1, 0, 2).reshape(OCEAN * F, CELLS)


def on_device(
    fine_atmospheric_values,
    fine_skin_heat,
    coarse_lowest_values,
    holder_flat,
    corner_offset,
    exchange_patch_holder,
    holder_patch_position,
    coarse_interface_exchange,
    marine_stratum_values,
    diffusion_solver_operator,
):
    owner = exchange_patch_holder.reshape(1, NB)
    place = holder_patch_position.reshape(1, NB)
    names, message = ((1, NB), i32), ((DEV * ROWS, CELLS), bf16)
    (windows,) = call(
        pack_kernel, "ssaaa", "h", (holder_flat, corner_offset, owner, place, coarse_lowest_values), (message,),
        (names, names, ((F, PROW, PC), bf16), ((DEV * ROWS, CELLS), f32), message), 4,
    )
    got = exchange(windows, (DEV, ROWS // 4, 4, CELLS))
    present, windows = lax.optimization_barrier((fine_atmospheric_values, windows))
    strip = ((TX, CELLS), f32)
    low, high = call(columns_kernel, "v", "vv", (present,), (strip, strip), (strip,))
    left, right = shift(high, "gy", 1), shift(low, "gy", -1)
    ends, strip16 = ((F * HALO, CELLS), f32), ((16, CELLS), f32)
    low, high = call(
        rows_kernel, "aaa", "vv", (present, left, right), (ends, ends), (((F, 16, TY), f32), strip16, strip16, strip16), 6
    )
    before, after = shift(high, "gx", 1), shift(low, "gx", -1)
    tile, sent = ((F, TX, TY), f32), ((DEV * CAP * F, CELLS), bf16)
    nest_next, flux = call(
        nest_kernel, "ssaaaaaaaa", "hh",
        (holder_flat, corner_offset, got, present, left, right, before, after, fine_skin_heat, owner), (tile, sent),
        (
            ((GROUP, CELLS), bf16), tile, strip, strip, ends, ends, ((TX, TY), f32), names, tile, sent,
            ((F * ROWS_X, CELLS), bf16), strip, ((ROWS_X, CELLS), f32), ((F * ROWS_X, CELLS), f32), strip,
            ((DEV * CAP * F, CELLS), f32),
        ), 13,
    )
    got_flux = exchange(flux, (DEV, CAP, F, CELLS))
    layers = marine_stratum_values.shape[1]
    marine = marine_stratum_values.reshape(F, layers, OCEAN, CELLS).transpose(1, 2, 0, 3).reshape(layers, OCEAN * F, CELLS)
    marine_late, got_late, flux = lax.optimization_barrier((marine, got, flux))
    block = ((OCEAN * F, CELLS), f32)
    hot, give = ((OCEAN * F, DEV * CAP * F), bf16), ((DEV * CAP, OCEAN * F), bf16)
    hot, give, inverse, cover = call(
        hot_kernel, "aa", "vvvv", (got_late, by_block(coarse_interface_exchange)), (hot, give, block, block),
        (
            message, block, ((DEV * CAP * F, OCEAN * F), f32), ((DEV * ROWS, CELLS), f32), ((DEV * CAP, OCEAN * F), f32),
        ), 2,
    )
    (top,) = call(top_kernel, "sv", "v", (diffusion_solver_operator, marine_late), (((OCEAN * F + 8, CELLS), f32),))
    returned = ((DEV * CAP, CELLS), f32)
    forcing, back = call(
        ocean_kernel, "aaaaaa", "hh", (got_flux, hot, inverse, cover, top, give), (block, returned),
        (
            sent, ((OCEAN * F, DEV * CAP * F), bf16), block, block, ((OCEAN * F + 8, CELLS), f32),
            ((DEV * CAP, OCEAN * F), bf16), block, returned,
        ), 6,
    )
    arrived = exchange(back, (DEV, 1, CAP * CELLS))
    part = 32
    refreshed = pl.pallas_call(
        mix_kernel,
        out_shape=jax.ShapeDtypeStruct((layers, OCEAN * F, CELLS), f32),
        grid=(OCEAN * F // part,),
        in_specs=[
            pl.BlockSpec((layers, layers), lambda g: (0, 0)),
            pl.BlockSpec((part, CELLS), lambda g: (g, 0)),
            pl.BlockSpec((layers, part, CELLS), lambda g: (0, g, 0)),
        ],
        out_specs=pl.BlockSpec((layers, part, CELLS), lambda g: (0, g, 0)),
        scratch_shapes=[pltpu.VMEM((8 * layers, 8 * layers), bf16)] * 2,
        compiler_params=pltpu.CompilerParams(vmem_limit_bytes=40 << 20),
    )(diffusion_solver_operator, forcing, marine)
    refreshed = refreshed.reshape(layers, OCEAN, F, CELLS).transpose(2, 0, 1, 3).reshape(marine_stratum_values.shape)
    (skin,) = call(
        skin_kernel, "aa", "v", (arrived, owner), (((TX, TY), f32),), (returned, names, ((TX, CELLS), f32)), 2
    )
    return (nest_next, refreshed, skin)


def solution(mesh):
    in_specs = (
        P(None, "gx", "gy"),
        P("gx", "gy"),
        P(None, "gx", "gy"),
        P(),
        P(),
        P(("gx", "gy"), None),
        P(("gx", "gy")),
        P(None, ("gx", "gy")),
        P(None, None, ("gx", "gy")),
        P(),
    )
    out_specs = (P(None, "gx", "gy"), P(None, None, ("gx", "gy")), P("gx", "gy"))
    return jax.shard_map(
        on_device, mesh=mesh, in_specs=in_specs, out_specs=out_specs, check_vma=False
    )
```

```python
import jax
import jax.numpy as jnp
from jax import lax
from jax.experimental import pallas as pl
from jax.experimental.pallas import tpu as pltpu
from jax.sharding import PartitionSpec as P

F = 4
CELLS = 128
OCEAN = 32
STEPS = 4
TX, TY = 192, 96
GX, GY = 8, 16
DEV = GX * GY
PC = 384
CAP = 3
NB = 144
HALO = 4
ROWS_X = TX + 2 * HALO
WP = 32
WQ = 18
ROWS = 20
GROUP = 4 * ROWS
PROW = 256
LEFT = tuple(
    i for i in range(GX) if i < GX - 1 and (4 * (TX * i + TX + 2) - 11) // 26 + 1 - (4 * (TX * i - 3) - 11) // 26 >= WP
)
f32, bf16, i32 = jnp.float32, jnp.bfloat16, jnp.int32

diffuse_coef = 0.24
relax_coef = 0.3
drag_coefficient = 0.5


def iota(shape, dim):
    return lax.broadcasted_iota(i32, shape, dim)


def first_x(i):
    return (4 * (TX * i - 3) - 11) // 26


def first_y(j):
    return (4 * (TY * j - 3) - 11) // 26


def first_y_of(j):
    return ((4 * TY * j + 3) * 2521 >> 16) - 1


def first_x_of(i):
    return ((4 * TX * i + 3) * 2521 >> 16) - 1


def dot(a, b):
    return jnp.dot(a, b, preferred_element_type=f32)


def dot_nt(a, b):
    return lax.dot_general(a, b, (((1,), (1,)), ((), ())), preferred_element_type=f32)


def split3(x):
    high = x.astype(bf16)
    rest = x - high.astype(f32)
    mid = rest.astype(bf16)
    return high, mid, (rest - mid.astype(f32)).astype(bf16)


def column_of(row):
    n = row.shape[1]
    return jnp.sum(jnp.where(iota((n, n), 0) == iota((n, n), 1), row, 0), axis=1, keepdims=True)


def fetch(pairs, sems):
    copies = [pltpu.make_async_copy(src, dst, sems.at[k]) for k, (src, dst) in enumerate(pairs)]
    for copy in copies:
        copy.start()
    return copies


def rank_of(column, row, number):
    return jnp.sum(jnp.where((column == row) & (iota((NB, NB), 0) < number), 1, 0), axis=0, keepdims=True)


def by_thirds(column):
    at = iota((1, NB), 1)
    third = (at >= NB // CAP).astype(i32) + (at >= 2 * (NB // CAP)).astype(i32)
    number = CAP * (at - third * (NB // CAP)) + third
    return number, jnp.sum(jnp.where(iota((NB, NB), 0) == number, column, 0), axis=0, keepdims=True)


def pack_kernel(
    corner_ref, owner_ref, place_ref, parent_ref, s_ref, out_any, low_ref, high_ref, wide_ref, z_ref, out_ref, sems,
):
    wide_ref[...] = jnp.zeros_like(wide_ref)
    cx, cy = corner_ref[0], corner_ref[1]
    base = pl.multiple_of(jnp.minimum(jnp.maximum(cx - 1, 0) // 16 * 16, PC - PROW), 16)
    owner = owner_ref[...]
    rank = rank_of(column_of(owner), owner, iota((NB, NB), 1))
    named = iota((DEV, NB), 0) == owner
    slots = jnp.zeros((DEV, CELLS), f32)
    for s in range(CAP):
        value = jnp.sum(jnp.where(named & (rank == s), place_ref[...] + 1, 0).astype(f32), axis=1, keepdims=True) - 1.0
        slots = jnp.where(iota((DEV, CELLS), 1) == s, value, slots)
    columns(s_ref, low_ref, high_ref, wide_ref)

    row = iota((GY * ROWS, 1), 0)
    j = row * 3277 >> 16
    r = row - j * ROWS
    wanted = jnp.where(r < WQ, cy + first_y_of(j) + r, -1)
    pick_y = (wanted == iota((GY * ROWS, PC), 1)).astype(f32).astype(bf16)
    parts = [parent_ref[f, pl.ds(base, PROW), :] for f in range(F)]
    across = jnp.concatenate([dot_nt(pick_y, parts[f]).astype(bf16) for f in range(F)], axis=1)
    lane = iota((1, 2 * CELLS), 1)
    for pair in range(GX // 2):
        first = jnp.where(lane < CELLS, first_x(2 * pair), first_x(2 * pair + 1))
        p = cx - base + first + (lane & (WP - 1))
        target = jnp.where((p >= 0) & (p < PROW), (lane >> 5 & 3) * PROW + p, -1)
        pick_x = (iota((F * PROW, 2 * CELLS), 0) == target).astype(f32).astype(bf16)
        window = dot(across, pick_x)
        for k in range(2):
            i = 2 * pair + k
            z_ref[pl.ds(i * GY * ROWS, GY * ROWS), :] = window[:, k * CELLS : (k + 1) * CELLS]
    j16 = iota((GY, PC), 0)
    q = iota((GY, PC), 1) - (cy + first_y_of(j16))
    inside = (q >= 0) & (q < WQ)
    lanes = iota((GY, CELLS), 1) >> 5
    erow = iota((8, PROW), 0)
    target = jnp.full((8, PROW), -1, i32)
    for k, i in enumerate(LEFT):
        target = jnp.where(erow == k, cx - base + first_x(i) + WP, target)
    pick_row = (target == iota((8, PROW), 1)).astype(f32).astype(bf16)
    left = [jnp.zeros((GY, CELLS), f32) for _ in LEFT]
    for f in range(F):
        rows = dot(pick_row, parts[f])
        for k in range(len(LEFT)):
            kept = jnp.where(inside, rows[k : k + 1, :], 0.0)
            folded = kept[:, :128] + kept[:, 128:256] + kept[:, 256:]
            folded = folded + pltpu.roll(folded, 64, 1)
            folded = folded + pltpu.roll(folded, 32, 1)
            left[k] = jnp.where(lanes == f, folded, left[k])
    for k, i in enumerate(LEFT):
        z_ref[pl.ds(i * GY * ROWS + WQ, GY, stride=ROWS), :] = left[k]
    z_ref[pl.ds(ROWS - 1, DEV, stride=ROWS), :] = slots
    write(z_ref, out_ref, out_any, sems, 4)


def write(z_ref, out_ref, out_any, sems, parts):
    rows = z_ref.shape[0] // parts
    copies = []
    for k in range(parts):
        at = pl.ds(k * rows, rows)
        out_ref[at, :] = z_ref[at, :].astype(bf16)
        copies.append(pltpu.make_async_copy(out_ref.at[at, :], out_any.at[at, :], sems.at[k]))
        copies[k].start()
    for copy in copies:
        copy.wait()


def hat(fine, anchor, coarse):
    centre = (fine.astype(f32) + 0.5) * (2.0 / 13.0) - 0.5 + anchor.astype(f32)
    return jnp.maximum(0.0, 1.0 - jnp.abs(centre - coarse.astype(f32)))


def columns(s_ref, low_ref, high_ref, wide_ref):
    field = iota((TX, CELLS), 1) >> 2
    low, high = jnp.zeros((TX, CELLS), f32), jnp.zeros((TX, CELLS), f32)
    for f in range(F):
        wide_ref[:, :TY] = s_ref[f]
        s = wide_ref[...]
        low = jnp.where(field == f, s if f == 0 else pltpu.roll(s, HALO * f, 1), low)
        high = jnp.where(field == f, pltpu.roll(s, CELLS - TY + HALO + HALO * f, 1), high)
    low_ref[...] = low
    high_ref[...] = high


def widened(s, left, right, f):
    lane = iota(s.shape, 1)
    before = left if f == 0 else pltpu.roll(left, CELLS - HALO * f, 1)
    after = pltpu.roll(right, TY + HALO - HALO * f, 1)
    wide = jnp.where(lane < TY + HALO, pltpu.roll(s, HALO, 1), after)
    return jnp.where(lane < HALO, before, jnp.where(lane < TY + 2 * HALO, wide, 0.0))


def rows_kernel(s_any, left_ref, right_ref, low_ref, high_ref, s_ref, wide_ref, sems):
    ends = ((0, 0), (8, TX - 8))
    for copy in fetch([(s_any.at[:, pl.ds(src, 8), :], s_ref.at[:, pl.ds(dst, 8), :]) for dst, src in ends], sems):
        copy.wait()
    left = jnp.concatenate([left_ref[:8, :], left_ref[TX - 8 :, :]], axis=0)
    right = jnp.concatenate([right_ref[:8, :], right_ref[TX - 8 :, :]], axis=0)
    wide_ref[...] = jnp.zeros_like(wide_ref)
    for f in range(F):
        wide_ref[:, :TY] = s_ref[f]
        wide = widened(wide_ref[...], left, right, f)
        low_ref[f * HALO : (f + 1) * HALO, :] = wide[:HALO]
        high_ref[f * HALO : (f + 1) * HALO, :] = wide[16 - HALO :]


def ready_kernel(
    holder_ref, corner_ref, owner_ref, s_ref, left_ref, right_ref, before_ref, after_ref,
    wx_ref, wlast_ref, mask_ref, wy_ref, wyc_ref, send_ref, back_ref, state_ref, wide_ref,
):
    ix, iy = lax.axis_index("gx"), lax.axis_index("gy")
    cx, cy = corner_ref[0], corner_ref[1]
    x0, y0 = ix * TX - HALO, iy * TY - HALO
    px, qy = cx + first_x_of(ix), cy + first_y_of(iy)
    lane = iota((ROWS_X, CELLS), 1)
    row = iota((ROWS_X, CELLS), 0)
    weight = hat(row + x0, cx, (lane & (WP - 1)) + px)
    for f in range(F):
        wx_ref[f * ROWS_X : (f + 1) * ROWS_X, :] = jnp.where(lane >> 5 == f, weight, 0.0).astype(bf16)
    wlast_ref[...] = relax_coef * hat(row + x0, cx, jnp.full_like(row, WP) + px).astype(bf16).astype(f32)
    inside = (row + x0 >= 0) & (row + x0 < GX * TX) & (lane + y0 >= 0) & (lane + y0 < GY * TY)
    mask_ref[...] = jnp.where(inside, 1.0, 0.0)
    at = iota((CELLS, GROUP), 1) - (holder_ref[0] & 3) * ROWS
    wy_ref[...] = jnp.where((at >= 0) & (at < WQ), hat(iota((CELLS, GROUP), 0) + y0, cy, at + qy), 0.0).astype(bf16)
    lane = iota((CELLS, CELLS), 1)
    wyc_ref[...] = hat(iota((CELLS, CELLS), 0) + y0, cy, qy + ((lane - qy) & (WP - 1))).astype(bf16)
    wide_ref[...] = jnp.zeros_like(wide_ref)
    column = column_of(owner_ref[...])
    number, owner = by_thirds(column)
    rank = rank_of(column, owner, number)
    send_ref[...] = (iota((CAP * DEV, NB), 0) == rank * DEV + owner).astype(f32).astype(bf16)
    back_ref[...] = (column_of(owner * CAP + rank) == iota((NB, CAP * DEV), 1)).astype(f32).astype(bf16)
    left, right = left_ref[...], right_ref[...]
    for f in range(F):
        wide_ref[:, :TY] = s_ref[f]
        state_ref[f, :HALO, :] = before_ref[f * HALO : (f + 1) * HALO, :]
        state_ref[f, HALO : HALO + TX, :] = widened(wide_ref[...], left, right, f)
        state_ref[f, HALO + TX :, :] = after_ref[f * HALO : (f + 1) * HALO, :]


def nest_kernel(
    holder_ref, got_ref, wx_ref, wlast_ref, mask_ref, wy_ref, wyc_ref, send_ref, begin_ref, skin_ref, next_any, out_any,
    next_ref, out_ref, state_ref, force_ref, flux_ref, z_ref, sems,
):
    group = pl.multiple_of((holder_ref[0] >> 2) * GROUP, 16)
    got = got_ref[pl.ds(group, GROUP), :]
    partial = dot(wy_ref[...], got).astype(bf16)
    last = jnp.sum(
        jnp.where(iota((GROUP, CELLS), 0) == (holder_ref[0] & 3) * ROWS + WQ, got.astype(f32), 0.0), axis=0, keepdims=True
    )
    last = jnp.where(iota((8, CELLS), 1) >> 5 == iota((8, CELLS), 0), last, 0.0).astype(bf16)
    partial_last = dot_nt(last, wyc_ref[...]).astype(bf16).astype(f32)
    force_ref[...] = dot_nt(wx_ref[...], partial)
    flux_ref[...] = jnp.zeros_like(flux_ref)
    mask = mask_ref[...]
    written = []
    for f in range(F):
        force = relax_coef * force_ref[f * ROWS_X : (f + 1) * ROWS_X, :] + wlast_ref[...] * partial_last[f : f + 1, :]
        s = begin_ref[f]
        for _ in range(STEPS):
            beside = (
                pltpu.roll(s, 1, 0) + pltpu.roll(s, ROWS_X - 1, 0) + pltpu.roll(s, 1, 1) + pltpu.roll(s, CELLS - 1, 1)
            )
            s = mask * ((1.0 - 4.0 * diffuse_coef - relax_coef) * s + diffuse_coef * beside + force)
        state_ref[...] = pltpu.roll(s, CELLS - HALO, 1)
        next_ref[f] = state_ref[HALO : HALO + TX, :TY]
        written.append(pltpu.make_async_copy(next_ref.at[f], next_any.at[f], sems.at[f]))
        written[f].start()
    u, v, ta, qa = next_ref[0], next_ref[1], next_ref[2], next_ref[3]
    half = drag_coefficient * jnp.sqrt(1.0 + u * u + v * v)
    skin = skin_ref[...]
    flux = (half * (ta - skin), half * (qa - 0.5 * skin), half * u, half * v)
    rows = NB // CAP
    lane = iota((rows, CELLS), 1)
    blocks = []
    for f in range(F):
        flux_ref[:, :TY] = flux[f]
        m = [flux_ref[pl.ds(k, rows, stride=4), :] for k in range(4)]
        r1, r2, r3 = pltpu.roll(m[1], 96, 1), pltpu.roll(m[2], 64, 1), pltpu.roll(m[3], 32, 1)
        blocks.append(
            jnp.concatenate(
                [jnp.where(lane < 96, m[0], r1), jnp.where(lane < 64, r1, r2), jnp.where(lane < 32, r2, r3)], axis=0
            ).astype(bf16)
        )
    sent = dot(send_ref[...], jnp.concatenate(blocks, axis=1))
    for slot in range(CAP):
        for f in range(F):
            z_ref[pl.ds(slot * F + f, DEV, stride=CAP * F), :] = sent[
                slot * DEV : (slot + 1) * DEV, f * CELLS : (f + 1) * CELLS
            ]
    for copy in written:
        copy.wait()
    write(z_ref, out_ref, out_any, sems, 4)


def hot_kernel(got_ref, kept_ref, hot_ref, give_ref, inverse_ref, cover_ref, z_ref, slot_ref, row_ref):
    slot_ref[...] = got_ref[...].astype(f32)
    slots = slot_ref[pl.ds(ROWS - 1, DEV, stride=ROWS), :].astype(i32)
    lane = iota((DEV, OCEAN * F), 1)
    for s in range(CAP):
        target = slots[:, s : s + 1] * F
        for f in range(F):
            z_ref[pl.ds(s * F + f, DEV, stride=CAP * F), :] = (lane == jnp.where(target < 0, -1, target + f)).astype(f32)
        row_ref[pl.ds(s, DEV, stride=CAP), :] = (lane == target).astype(f32)
    give_ref[...] = row_ref[...].astype(bf16)
    hot = jnp.swapaxes(z_ref[...], 0, 1)
    hot_ref[...] = hot.astype(bf16)
    count = jnp.sum(hot, axis=1, keepdims=True)
    inverse_ref[...] = jnp.broadcast_to(1.0 / jnp.maximum(count, 1.0), (OCEAN * F, CELLS))
    cover_ref[...] = jnp.where(count == 0.0, kept_ref[...], 0.0)


def top_kernel(scale_ref, marine_ref, out_ref):
    total = scale_ref[0, 0] * marine_ref[0]
    for k in range(1, marine_ref.shape[0]):
        total = total + scale_ref[0, k] * marine_ref[k]
    out_ref[: OCEAN * F, :] = total
    out_ref[OCEAN * F :, :] = jnp.full((8, CELLS), scale_ref[0, 0], f32)


def ocean_kernel(got_ref, hot_ref, inverse_ref, cover_ref, top_ref, give_ref, forcing_ref, out_ref):
    forcing = dot(hot_ref[...], got_ref[...]) * inverse_ref[...] + cover_ref[...]
    forcing_ref[...] = forcing
    top = top_ref[: OCEAN * F, :] + top_ref[OCEAN * F : OCEAN * F + 1, :] * forcing
    back = dot(give_ref[...], jnp.concatenate(split3(top), axis=1))
    out_ref[...] = back[:, :CELLS] + back[:, CELLS : 2 * CELLS] + back[:, 2 * CELLS :]

def mix_kernel(scale_ref, forcing_ref, marine_ref, out_ref, high_ref, low_ref):
    layers = marine_ref.shape[0]
    n = 8 * layers

    @pl.when(pl.program_id(0) == 0)
    def _():
        spread = (iota((n, layers), 0) >> 3 == iota((n, layers), 1)).astype(f32).astype(bf16)
        same = (iota((n, n), 0) & 7) == (iota((n, n), 1) & 7)
        scale = scale_ref[...]
        high = scale.astype(bf16)
        low = (scale - high.astype(f32)).astype(bf16)
        for part, ref in ((high, high_ref), (low, low_ref)):
            wide = dot_nt(dot(spread, part).astype(bf16), spread)
            ref[...] = jnp.where(same, wide, 0.0).astype(bf16)

    groups = marine_ref.shape[1] // 8
    columns = []
    for g in range(groups):
        x = marine_ref[:, 8 * g : 8 * g + 8, :].reshape(n, CELLS)
        first = x[:8] + forcing_ref[8 * g : 8 * g + 8, :]
        columns.append(jnp.concatenate([first, x[8:]], axis=0))
    x = jnp.concatenate(columns, axis=1)
    high = x.astype(bf16)
    low = (x - high.astype(f32)).astype(bf16)
    y = dot(high_ref[...], high) + (dot(high_ref[...], low) + dot(low_ref[...], high))
    for g in range(groups):
        out_ref[:, 8 * g : 8 * g + 8, :] = y[:, g * CELLS : (g + 1) * CELLS].reshape(layers, 8, CELLS)


def skin_kernel(got_ref, back_ref, out_ref, tile_ref):
    x = dot(back_ref[...], jnp.concatenate(split3(got_ref[...]), axis=1))
    x = x[:, :CELLS] + x[:, CELLS : 2 * CELLS] + x[:, 2 * CELLS :]
    rows = NB // CAP
    t0, t1, t2 = x[:rows], x[rows : 2 * rows], x[2 * rows :]
    lane = iota((rows, CELLS), 1)
    tile_ref[pl.ds(0, rows, stride=4), :] = t0
    tile_ref[pl.ds(1, rows, stride=4), :] = pltpu.roll(jnp.where(lane < 64, t1, t0), 32, 1)
    tile_ref[pl.ds(2, rows, stride=4), :] = pltpu.roll(jnp.where(lane < 32, t2, t1), 64, 1)
    tile_ref[pl.ds(3, rows, stride=4), :] = pltpu.roll(t2, 96, 1)
    out_ref[...] = tile_ref[:, :TY]


MEMORY = {"h": pltpu.HBM, "v": pltpu.VMEM, "H": pltpu.HBM, "S": pltpu.HBM}
SPACES = {"h": pltpu.HBM, "v": pltpu.VMEM, "H": pltpu.HBM, "S": pltpu.HBM, "p": pltpu.VMEM, "s": pltpu.SMEM}


def call(kernel, ins, outs, args, shapes, scratch=(), copies=0):
    args = [pltpu.with_memory_space_constraint(a, MEMORY[c]) if c in MEMORY else a for c, a in zip(ins, args)]
    letters = ins + outs
    kinds = [(a.shape, a.dtype) for a in args] + list(shapes)
    moved = [k for k, c in enumerate(letters) if c in "HS"]
    own = len(scratch) + (1 if copies else 0)

    def body(*refs):
        arrays, rest = list(refs[: len(letters)]), refs[len(letters) :]
        sems = rest[-1]
        far = [arrays[k] for k in moved]
        for n, k in enumerate(moved):
            arrays[k] = rest[own + n]
        pending = [
            pltpu.make_async_copy(far[n], arrays[k], sems.at[n]) for n, k in enumerate(moved) if k < len(ins)
        ]
        for copy in pending:
            copy.start()
        for copy in pending:
            copy.wait()
        kernel(*arrays, *rest[:own])
        done = [pltpu.make_async_copy(arrays[k], far[n], sems.at[n]) for n, k in enumerate(moved) if k >= len(ins)]
        for copy in done:
            copy.start()
        for copy in done:
            copy.wait()

    return pl.pallas_call(
        body,
        out_shape=tuple(MEMORY[c](s, d) if c in MEMORY else jax.ShapeDtypeStruct(s, d) for c, (s, d) in zip(outs, shapes)),
        in_specs=[pl.BlockSpec(memory_space=SPACES[c]) for c in ins],
        out_specs=tuple(pl.BlockSpec(memory_space=SPACES[c]) for c in outs),
        scratch_shapes=[pltpu.VMEM(s, d) for s, d in scratch]
        + ([pltpu.SemaphoreType.DMA((copies,))] if copies else [])
        + [(pltpu.SMEM if letters[k] == "S" else pltpu.VMEM)(*kinds[k]) for k in moved]
        + [pltpu.SemaphoreType.DMA((max(1, len(moved)),))],
        compiler_params=pltpu.CompilerParams(vmem_limit_bytes=32 << 20),
    )(*args)


def shift(value, axis, by):
    n = lax.axis_size(axis)
    return lax.ppermute(value, axis, [(i, i + by) for i in range(n) if 0 <= i + by < n])


def exchange(value, rows):
    split = value.reshape(rows)
    return lax.all_to_all(split, ("gx", "gy"), split_axis=0, concat_axis=0, tiled=True).reshape(value.shape)


def by_block(value):
    return value.reshape(F, OCEAN, CELLS).transpose(1, 0, 2).reshape(OCEAN * F, CELLS)


def on_device(
    fine_atmospheric_values,
    fine_skin_heat,
    coarse_lowest_values,
    holder_flat,
    corner_offset,
    exchange_patch_holder,
    holder_patch_position,
    coarse_interface_exchange,
    marine_stratum_values,
    diffusion_solver_operator,
):
    owner = exchange_patch_holder.reshape(1, NB)
    place = holder_patch_position.reshape(1, NB)
    names, message, tile, strip = ((1, NB), i32), ((DEV * ROWS, CELLS), bf16), ((F, TX, TY), f32), ((TX, CELLS), f32)
    windows, low, high = call(
        pack_kernel, "SHHHH", "hvv",
        (corner_offset, owner, place, coarse_lowest_values, fine_atmospheric_values), (message, strip, strip),
        (strip, ((DEV * ROWS, CELLS), f32), message), 4,
    )
    left, right = shift(high, "gy", 1), shift(low, "gy", -1)
    got = exchange(windows, (DEV, ROWS // 4, 4, CELLS))
    ends = ((F * HALO, CELLS), f32)
    low, high = call(
        rows_kernel, "hvv", "vv", (fine_atmospheric_values, left, right), (ends, ends),
        (((F, 16, TY), f32), ((16, CELLS), f32)), 2,
    )
    before, after = shift(high, "gx", 1), shift(low, "gx", -1)
    holder, _ = lax.optimization_barrier((holder_flat, low))
    holder = jnp.minimum(holder, DEV - 1)
    wide = (ROWS_X, CELLS)
    *weights, send, back, state = call(
        ready_kernel, "sSHHvvvv", "HHHHHHHH",
        (holder, corner_offset, owner, fine_atmospheric_values, left, right, before, after),
        (
            ((F * ROWS_X, CELLS), bf16), (wide, f32), (wide, f32), ((CELLS, GROUP), bf16), ((CELLS, CELLS), bf16),
            ((CAP * DEV, NB), bf16), ((NB, CAP * DEV), bf16), ((F,) + wide, f32),
        ), (strip,),
    )
    sent = ((DEV * CAP * F, CELLS), bf16)
    nest_next, flux = call(
        nest_kernel, "svHHHHHHHH", "hh", (holder, got, *weights, send, state, fine_skin_heat), (tile, sent),
        (tile, sent, (wide, f32), ((F * ROWS_X, CELLS), f32), strip, ((DEV * CAP * F, CELLS), f32)), F,
    )
    got_flux = exchange(flux, (DEV, CAP, F, CELLS))
    layers = marine_stratum_values.shape[1]
    marine = marine_stratum_values.reshape(F, layers, OCEAN, CELLS).transpose(1, 2, 0, 3).reshape(layers, OCEAN * F, CELLS)
    marine_late, got_late, flux = lax.optimization_barrier((marine, got, flux))
    block = ((OCEAN * F, CELLS), f32)
    hot, give = ((OCEAN * F, DEV * CAP * F), bf16), ((DEV * CAP, OCEAN * F), bf16)
    hot, give, inverse, cover = call(
        hot_kernel, "vH", "HHHH", (got_late, by_block(coarse_interface_exchange)), (hot, give, block, block),
        (((DEV * CAP * F, OCEAN * F), f32), ((DEV * ROWS, CELLS), f32), ((DEV * CAP, OCEAN * F), f32)),
    )
    (top,) = call(top_kernel, "Sp", "H", (diffusion_solver_operator, marine_late), (((OCEAN * F + 8, CELLS), f32),))
    returned = ((DEV * CAP, CELLS), f32)
    forcing, skins = call(
        ocean_kernel, "HHHHHH", "HH", (got_flux, hot, inverse, cover, top, give), (block, returned)
    )
    arrived = exchange(skins, (DEV, 1, CAP * CELLS))
    part = 32
    refreshed = pl.pallas_call(
        mix_kernel,
        out_shape=jax.ShapeDtypeStruct((layers, OCEAN * F, CELLS), f32),
        grid=(OCEAN * F // part,),
        in_specs=[
            pl.BlockSpec((layers, layers), lambda g: (0, 0)),
            pl.BlockSpec((part, CELLS), lambda g: (g, 0)),
            pl.BlockSpec((layers, part, CELLS), lambda g: (0, g, 0)),
        ],
        out_specs=pl.BlockSpec((layers, part, CELLS), lambda g: (0, g, 0)),
        scratch_shapes=[pltpu.VMEM((8 * layers, 8 * layers), bf16)] * 2,
        compiler_params=pltpu.CompilerParams(vmem_limit_bytes=40 << 20),
    )(diffusion_solver_operator, forcing, marine)
    refreshed = refreshed.reshape(layers, OCEAN, F, CELLS).transpose(2, 0, 1, 3).reshape(marine_stratum_values.shape)
    (skin,) = call(skin_kernel, "vH", "p", (arrived, back), (((TX, TY), f32),), (((TX, CELLS), f32),))
    return (nest_next, refreshed, skin)


def solution(mesh):
    in_specs = (
        P(None, "gx", "gy"),
        P("gx", "gy"),
        P(None, "gx", "gy"),
        P(),
        P(),
        P(("gx", "gy"), None),
        P(("gx", "gy")),
        P(None, ("gx", "gy")),
        P(None, None, ("gx", "gy")),
        P(),
    )
    out_specs = (P(None, "gx", "gy"), P(None, None, ("gx", "gy")), P("gx", "gy"))
    return jax.shard_map(
        on_device, mesh=mesh, in_specs=in_specs, out_specs=out_specs, check_vma=False
    )
```

```python
import jax
import jax.numpy as jnp
from jax import lax
from jax.experimental import pallas as pl
from jax.experimental.pallas import tpu as pltpu
from jax.sharding import PartitionSpec as P

F = 4
CELLS = 128
OCEAN = 32
STEPS = 4
TX, TY = 192, 96
GX, GY = 8, 16
DEV = GX * GY
PC = 384
CAP = 3
NB = 144
HALO = 4
ROWS_X = TX + 2 * HALO
WP = 32
WQ = 18
ROWS = 20
GROUP = 4 * ROWS
PROW = 256
LEFT = tuple(
    i for i in range(GX) if i < GX - 1 and (4 * (TX * i + TX + 2) - 11) // 26 + 1 - (4 * (TX * i - 3) - 11) // 26 >= WP
)
f32, bf16, i32 = jnp.float32, jnp.bfloat16, jnp.int32

diffuse_coef = 0.24
relax_coef = 0.3
drag_coefficient = 0.5


def iota(shape, dim):
    return lax.broadcasted_iota(i32, shape, dim)


def first_x(i):
    return (4 * (TX * i - 3) - 11) // 26


def first_y(j):
    return (4 * (TY * j - 3) - 11) // 26


def first_y_of(j):
    return ((4 * TY * j + 3) * 2521 >> 16) - 1


def first_x_of(i):
    return ((4 * TX * i + 3) * 2521 >> 16) - 1


def dot(a, b):
    return jnp.dot(a, b, preferred_element_type=f32)


def dot_nt(a, b):
    return lax.dot_general(a, b, (((1,), (1,)), ((), ())), preferred_element_type=f32)


def split3(x):
    high = x.astype(bf16)
    rest = x - high.astype(f32)
    mid = rest.astype(bf16)
    return high, mid, (rest - mid.astype(f32)).astype(bf16)


def column_of(row):
    n = row.shape[1]
    return jnp.sum(jnp.where(iota((n, n), 0) == iota((n, n), 1), row, 0), axis=1, keepdims=True)


def fetch(pairs, sems):
    copies = [pltpu.make_async_copy(src, dst, sems.at[k]) for k, (src, dst) in enumerate(pairs)]
    for copy in copies:
        copy.start()
    return copies


def rank_of(column, row, number):
    return jnp.sum(jnp.where((column == row) & (iota((NB, NB), 0) < number), 1, 0), axis=0, keepdims=True)


def by_thirds(column):
    at = iota((1, NB), 1)
    third = (at >= NB // CAP).astype(i32) + (at >= 2 * (NB // CAP)).astype(i32)
    number = CAP * (at - third * (NB // CAP)) + third
    return number, jnp.sum(jnp.where(iota((NB, NB), 0) == number, column, 0), axis=0, keepdims=True)


PARTS = 3
EDGE = 3
CORNER = F * EDGE * EDGE
FREE = 16
CORNERS = ((-1, -1), (-1, 1), (1, -1), (1, 1))


def neighbour(step):
    x, y = lax.axis_index("gx") + step[0], lax.axis_index("gy") + step[1]
    there = (x >= 0) & (x < GX) & (y >= 0) & (y < GY)
    return jnp.where(there, x * GY + y, 0), there


def corner_rows(s_ref, wide_ref):
    lane, sub = iota((8, CELLS), 1), iota((8, CELLS), 0)
    wide_ref[...] = jnp.zeros_like(wide_ref)
    out = jnp.zeros((8, CELLS), f32)
    for f in range(F):
        wide_ref[:, :TY] = s_ref[f]
        for k, (dx, dy) in enumerate(CORNERS):
            for r in range(EDGE):
                row = r if dx < 0 else 16 - EDGE + r
                column = 0 if dy < 0 else TY - EDGE
                at = FREE + (f * EDGE + r) * EDGE
                moved = pltpu.roll(jnp.broadcast_to(wide_ref[row : row + 1, :], (8, CELLS)), (at - column) % CELLS, 1)
                out = jnp.where((sub == k) & (lane >= at) & (lane < at + EDGE), moved, out)
    high, mid, low = (x.astype(f32) for x in split3(out))
    return high + pltpu.roll(mid, CORNER, 1) + pltpu.roll(low, 2 * CORNER, 1)


def pack_kernel(
    corner_ref, owner_ref, place_ref, parent_ref, s_any, out_any, s_ref, wide_ref, z_ref, out_ref, sems,
):
    ends = fetch([(s_any.at[:, pl.ds(src, 8), :], s_ref.at[:, pl.ds(dst, 8), :]) for dst, src in ((0, 0), (8, TX - 8))], sems)
    cx, cy = corner_ref[0], corner_ref[1]
    base = pl.multiple_of(jnp.minimum(jnp.maximum(cx - 1, 0) // 16 * 16, PC - PROW), 16)
    owner = owner_ref[...]
    rank = rank_of(column_of(owner), owner, iota((NB, NB), 1))
    named = iota((DEV, NB), 0) == owner
    slots = jnp.zeros((DEV, CELLS), f32)
    for s in range(CAP):
        value = jnp.sum(jnp.where(named & (rank == s), place_ref[...] + 1, 0).astype(f32), axis=1, keepdims=True) - 1.0
        slots = jnp.where(iota((DEV, CELLS), 1) == s, value, slots)
    row = iota((GY * ROWS, 1), 0)
    j = row * 3277 >> 16
    r = row - j * ROWS
    wanted = jnp.where(r < WQ, cy + first_y_of(j) + r, -1)
    pick_y = (wanted == iota((GY * ROWS, PC), 1)).astype(f32).astype(bf16)
    parts = [parent_ref[f, pl.ds(base, PROW), :] for f in range(F)]
    across = jnp.concatenate([dot_nt(pick_y, parts[f]).astype(bf16) for f in range(F)], axis=1)
    lane = iota((1, 2 * CELLS), 1)
    for pair in range(GX // 2):
        first = jnp.where(lane < CELLS, first_x(2 * pair), first_x(2 * pair + 1))
        p = cx - base + first + (lane & (WP - 1))
        target = jnp.where((p >= 0) & (p < PROW), (lane >> 5 & 3) * PROW + p, -1)
        pick_x = (iota((F * PROW, 2 * CELLS), 0) == target).astype(f32).astype(bf16)
        window = dot(across, pick_x)
        for k in range(2):
            i = 2 * pair + k
            z_ref[pl.ds(i * GY * ROWS, GY * ROWS), :] = window[:, k * CELLS : (k + 1) * CELLS]
    j16 = iota((GY, PC), 0)
    q = iota((GY, PC), 1) - (cy + first_y_of(j16))
    inside = (q >= 0) & (q < WQ)
    lanes = iota((GY, CELLS), 1) >> 5
    erow = iota((8, PROW), 0)
    target = jnp.full((8, PROW), -1, i32)
    for k, i in enumerate(LEFT):
        target = jnp.where(erow == k, cx - base + first_x(i) + WP, target)
    pick_row = (target == iota((8, PROW), 1)).astype(f32).astype(bf16)
    left = [jnp.zeros((GY, CELLS), f32) for _ in LEFT]
    for f in range(F):
        rows = dot(pick_row, parts[f])
        for k in range(len(LEFT)):
            kept = jnp.where(inside, rows[k : k + 1, :], 0.0)
            folded = kept[:, :128] + kept[:, 128:256] + kept[:, 256:]
            folded = folded + pltpu.roll(folded, 64, 1)
            folded = folded + pltpu.roll(folded, 32, 1)
            left[k] = jnp.where(lanes == f, folded, left[k])
    for k, i in enumerate(LEFT):
        z_ref[pl.ds(i * GY * ROWS + WQ, GY, stride=ROWS), :] = left[k]
    z_ref[pl.ds(ROWS - 1, DEV, stride=ROWS), :] = slots
    for copy in ends:
        copy.wait()
    corners = corner_rows(s_ref, wide_ref)
    for k, step in enumerate(CORNERS):
        other, there = neighbour(step)
        at = pl.ds(other * ROWS + ROWS - 1, 1)

        @pl.when(there)
        def _():
            z_ref[at, :] = z_ref[at, :] + corners[k : k + 1, :]

    write(z_ref, out_ref, out_any, sems, 4)


def write(z_ref, out_ref, out_any, sems, parts):
    rows = z_ref.shape[0] // parts
    copies = []
    for k in range(parts):
        at = pl.ds(k * rows, rows)
        out_ref[at, :] = z_ref[at, :].astype(bf16)
        copies.append(pltpu.make_async_copy(out_ref.at[at, :], out_any.at[at, :], sems.at[k]))
        copies[k].start()
    for copy in copies:
        copy.wait()


def hat(fine, anchor, coarse):
    centre = (fine.astype(f32) + 0.5) * (2.0 / 13.0) - 0.5 + anchor.astype(f32)
    return jnp.maximum(0.0, 1.0 - jnp.abs(centre - coarse.astype(f32)))


def strips_kernel(s_ref, low_ref, high_ref, top_ref, bottom_ref, wide_ref):
    field = iota((TX, CELLS), 1) >> 2
    wide_ref[...] = jnp.zeros_like(wide_ref)
    low, high = jnp.zeros((TX, CELLS), f32), jnp.zeros((TX, CELLS), f32)
    for f in range(F):
        wide_ref[:, :TY] = s_ref[f]
        s = wide_ref[...]
        low = jnp.where(field == f, s if f == 0 else pltpu.roll(s, HALO * f, 1), low)
        high = jnp.where(field == f, pltpu.roll(s, CELLS - TY + HALO + HALO * f, 1), high)
        top_ref[f * HALO : (f + 1) * HALO, :] = pltpu.roll(s[:8], HALO, 1)[:HALO]
        bottom_ref[f * HALO : (f + 1) * HALO, :] = pltpu.roll(s[TX - 8 :], HALO, 1)[HALO:]
    low_ref[...] = low
    high_ref[...] = high


def widened(s, left, right, f):
    lane = iota(s.shape, 1)
    before = left if f == 0 else pltpu.roll(left, CELLS - HALO * f, 1)
    after = pltpu.roll(right, TY + HALO - HALO * f, 1)
    wide = jnp.where(lane < TY + HALO, pltpu.roll(s, HALO, 1), after)
    return jnp.where(lane < HALO, before, jnp.where(lane < TY + 2 * HALO, wide, 0.0))


def tables_kernel(
    holder_ref, corner_ref, owner_ref, wx_ref, wlast_ref, mask_ref, wy_ref, wyc_ref, send_ref, back_ref
):
    ix, iy = lax.axis_index("gx"), lax.axis_index("gy")
    cx, cy = corner_ref[0], corner_ref[1]
    x0, y0 = ix * TX - HALO, iy * TY - HALO
    px, qy = cx + first_x_of(ix), cy + first_y_of(iy)
    lane = iota((ROWS_X, CELLS), 1)
    row = iota((ROWS_X, CELLS), 0)
    weight = hat(row + x0, cx, (lane & (WP - 1)) + px)
    for f in range(F):
        wx_ref[f * ROWS_X : (f + 1) * ROWS_X, :] = jnp.where(lane >> 5 == f, weight, 0.0).astype(bf16)
    wlast_ref[...] = relax_coef * hat(row + x0, cx, jnp.full_like(row, WP) + px).astype(bf16).astype(f32)
    inside = (row + x0 >= 0) & (row + x0 < GX * TX) & (lane + y0 >= 0) & (lane + y0 < GY * TY)
    mask_ref[...] = jnp.where(inside, 1.0, 0.0)
    at = iota((CELLS, GROUP), 1) - (holder_ref[0] & 3) * ROWS
    wy_ref[...] = jnp.where((at >= 0) & (at < WQ), hat(iota((CELLS, GROUP), 0) + y0, cy, at + qy), 0.0).astype(bf16)
    lane = iota((CELLS, CELLS), 1)
    wyc_ref[...] = hat(iota((CELLS, CELLS), 0) + y0, cy, qy + ((lane - qy) & (WP - 1))).astype(bf16)
    column = column_of(owner_ref[...])
    number, owner = by_thirds(column)
    rank = rank_of(column, owner, number)
    send_ref[...] = (iota((CAP * DEV, NB), 0) == rank * DEV + owner).astype(f32).astype(bf16)
    back_ref[...] = (column_of(owner * CAP + rank) == iota((NB, CAP * DEV), 1)).astype(f32).astype(bf16)


def corner_of(got_ref, step):
    other, there = neighbour(step)
    rows = got_ref[pl.ds(pl.multiple_of((other >> 2) * GROUP, 16), GROUP), :].astype(f32)
    mine = jnp.where(there, (other & 3) * ROWS + ROWS - 1, -1)
    row = jnp.sum(jnp.where(iota((GROUP, CELLS), 0) == mine, rows, 0.0), axis=0, keepdims=True)
    row = jnp.broadcast_to(row, (8, CELLS))
    return row + pltpu.roll(row, CELLS - CORNER, 1) + pltpu.roll(row, CELLS - 2 * CORNER, 1)


def nest_kernel(
    wait, holder_ref, got_ref, wx_ref, wlast_ref, mask_ref, wy_ref, wyc_ref, send_ref, s_ref, left_ref, right_ref,
    before_ref, after_ref, skin_ref, next_any, out_any,
    wide_ref, next_ref, out_ref, state_ref, force_ref, flux_ref, z_ref, sems,
):
    wide_ref[...] = jnp.zeros_like(wide_ref)
    corners = [corner_of(got_ref, step) for step in CORNERS]
    group = pl.multiple_of((holder_ref[0] >> 2) * GROUP, 16)
    got = got_ref[pl.ds(group, GROUP), :]
    wait(5)
    partial = dot(wy_ref[...], got).astype(bf16)
    last = jnp.sum(
        jnp.where(iota((GROUP, CELLS), 0) == (holder_ref[0] & 3) * ROWS + WQ, got.astype(f32), 0.0), axis=0, keepdims=True
    )
    last = jnp.where(iota((8, CELLS), 1) >> 5 == iota((8, CELLS), 0), last, 0.0).astype(bf16)
    wait(6)
    partial_last = dot_nt(last, wyc_ref[...]).astype(bf16).astype(f32)
    wait(2)
    force_ref[...] = dot_nt(wx_ref[...], partial)
    flux_ref[...] = jnp.zeros_like(flux_ref)
    for k in (3, 4, 8):
        wait(k)
    mask = mask_ref[...]
    left, right = left_ref[...], right_ref[...]
    lane, sub = iota((8, CELLS), 1), iota((8, CELLS), 0)
    written = []
    for f in range(F):
        force = relax_coef * force_ref[f * ROWS_X : (f + 1) * ROWS_X, :] + wlast_ref[...] * partial_last[f : f + 1, :]
        wide_ref[:, :TY] = s_ref[f]
        state_ref[:HALO, :] = before_ref[f * HALO : (f + 1) * HALO, :]
        state_ref[HALO : HALO + TX, :] = widened(wide_ref[...], left, right, f)
        state_ref[HALO + TX :, :] = after_ref[f * HALO : (f + 1) * HALO, :]
        for side, base in ((-1, 0), (1, ROWS_X - 8)):
            tile = state_ref[base : base + 8, :]
            for k, (dx, dy) in enumerate(CORNERS):
                for r in range(EDGE if dx == side else 0):
                    row = HALO - EDGE + r if dx < 0 else 8 - HALO + r
                    column = HALO - EDGE if dy < 0 else HALO + TY
                    at = FREE + (f * EDGE + r) * EDGE
                    moved = pltpu.roll(corners[k], (column - at) % CELLS, 1)
                    tile = jnp.where((sub == row) & (lane >= column) & (lane < column + EDGE), moved, tile)
            state_ref[base : base + 8, :] = tile
        s = state_ref[...]
        for _ in range(STEPS):
            beside = (
                pltpu.roll(s, 1, 0) + pltpu.roll(s, ROWS_X - 1, 0) + pltpu.roll(s, 1, 1) + pltpu.roll(s, CELLS - 1, 1)
            )
            s = mask * ((1.0 - 4.0 * diffuse_coef - relax_coef) * s + diffuse_coef * beside + force)
        state_ref[...] = pltpu.roll(s, CELLS - HALO, 1)
        next_ref[f] = state_ref[HALO : HALO + TX, :TY]
        written.append(pltpu.make_async_copy(next_ref.at[f], next_any.at[f], sems.at[f]))
        written[f].start()
    u, v, ta, qa = next_ref[0], next_ref[1], next_ref[2], next_ref[3]
    half = drag_coefficient * jnp.sqrt(1.0 + u * u + v * v)
    wait(13)
    skin = skin_ref[...]
    flux = (half * (ta - skin), half * (qa - 0.5 * skin), half * u, half * v)
    rows = NB // CAP
    lane = iota((rows, CELLS), 1)
    blocks = []
    for f in range(F):
        flux_ref[:, :TY] = flux[f]
        m = [flux_ref[pl.ds(k, rows, stride=4), :] for k in range(4)]
        r1, r2, r3 = pltpu.roll(m[1], 96, 1), pltpu.roll(m[2], 64, 1), pltpu.roll(m[3], 32, 1)
        blocks.append(
            jnp.concatenate(
                [jnp.where(lane < 96, m[0], r1), jnp.where(lane < 64, r1, r2), jnp.where(lane < 32, r2, r3)], axis=0
            ).astype(bf16)
        )
    wait(7)
    sent = dot(send_ref[...], jnp.concatenate(blocks, axis=1))
    for slot in range(CAP):
        for f in range(F):
            z_ref[pl.ds(slot * F + f, DEV, stride=CAP * F), :] = sent[
                slot * DEV : (slot + 1) * DEV, f * CELLS : (f + 1) * CELLS
            ]
    for copy in written:
        copy.wait()
    write(z_ref, out_ref, out_any, sems, 4)


def hot_kernel(got_ref, kept_ref, hot_ref, give_ref, inverse_ref, cover_ref, z_ref, slot_ref, row_ref):
    slot_ref[...] = got_ref[...].astype(f32)
    slots = slot_ref[pl.ds(ROWS - 1, DEV, stride=ROWS), :].astype(i32)
    lane = iota((DEV, OCEAN * F), 1)
    for s in range(CAP):
        target = slots[:, s : s + 1] * F
        for f in range(F):
            z_ref[pl.ds(s * F + f, DEV, stride=CAP * F), :] = (lane == jnp.where(target < 0, -1, target + f)).astype(f32)
        row_ref[pl.ds(s, DEV, stride=CAP), :] = (lane == target).astype(f32)
    give_ref[...] = row_ref[...].astype(bf16)
    hot = jnp.swapaxes(z_ref[...], 0, 1)
    hot_ref[...] = hot.astype(bf16)
    count = jnp.sum(hot, axis=1, keepdims=True)
    inverse_ref[...] = jnp.broadcast_to(1.0 / jnp.maximum(count, 1.0), (OCEAN * F, CELLS))
    cover_ref[...] = jnp.where(count == 0.0, kept_ref[...], 0.0)


def top_kernel(scale_ref, marine_ref, out_ref):
    total = scale_ref[0, 0] * marine_ref[0]
    for k in range(1, marine_ref.shape[0]):
        total = total + scale_ref[0, k] * marine_ref[k]
    out_ref[: OCEAN * F, :] = total
    out_ref[OCEAN * F :, :] = jnp.full((8, CELLS), scale_ref[0, 0], f32)


def ocean_kernel(got_ref, hot_ref, inverse_ref, cover_ref, top_ref, give_ref, forcing_ref, out_ref):
    forcing = dot(hot_ref[...], got_ref[...]) * inverse_ref[...] + cover_ref[...]
    forcing_ref[...] = forcing
    top = top_ref[: OCEAN * F, :] + top_ref[OCEAN * F : OCEAN * F + 1, :] * forcing
    back = dot(give_ref[...], jnp.concatenate(split3(top), axis=1))
    out_ref[...] = back[:, :CELLS] + back[:, CELLS : 2 * CELLS] + back[:, 2 * CELLS :]

def mix_kernel(scale_ref, forcing_ref, marine_ref, out_ref, high_ref, low_ref):
    layers = marine_ref.shape[0]
    n = 8 * layers

    @pl.when(pl.program_id(0) == 0)
    def _():
        spread = (iota((n, layers), 0) >> 3 == iota((n, layers), 1)).astype(f32).astype(bf16)
        same = (iota((n, n), 0) & 7) == (iota((n, n), 1) & 7)
        scale = scale_ref[...]
        high = scale.astype(bf16)
        low = (scale - high.astype(f32)).astype(bf16)
        for part, ref in ((high, high_ref), (low, low_ref)):
            wide = dot_nt(dot(spread, part).astype(bf16), spread)
            ref[...] = jnp.where(same, wide, 0.0).astype(bf16)

    groups = marine_ref.shape[1] // 8
    columns = []
    for g in range(groups):
        x = marine_ref[:, 8 * g : 8 * g + 8, :].reshape(n, CELLS)
        first = x[:8] + forcing_ref[8 * g : 8 * g + 8, :]
        columns.append(jnp.concatenate([first, x[8:]], axis=0))
    x = jnp.concatenate(columns, axis=1)
    high = x.astype(bf16)
    low = (x - high.astype(f32)).astype(bf16)
    y = dot(high_ref[...], high) + (dot(high_ref[...], low) + dot(low_ref[...], high))
    for g in range(groups):
        out_ref[:, 8 * g : 8 * g + 8, :] = y[:, g * CELLS : (g + 1) * CELLS].reshape(layers, 8, CELLS)


def skin_kernel(got_ref, back_ref, out_ref, tile_ref):
    x = dot(back_ref[...], jnp.concatenate(split3(got_ref[...]), axis=1))
    x = x[:, :CELLS] + x[:, CELLS : 2 * CELLS] + x[:, 2 * CELLS :]
    rows = NB // CAP
    t0, t1, t2 = x[:rows], x[rows : 2 * rows], x[2 * rows :]
    lane = iota((rows, CELLS), 1)
    tile_ref[pl.ds(0, rows, stride=4), :] = t0
    tile_ref[pl.ds(1, rows, stride=4), :] = pltpu.roll(jnp.where(lane < 64, t1, t0), 32, 1)
    tile_ref[pl.ds(2, rows, stride=4), :] = pltpu.roll(jnp.where(lane < 32, t2, t1), 64, 1)
    tile_ref[pl.ds(3, rows, stride=4), :] = pltpu.roll(t2, 96, 1)
    out_ref[...] = tile_ref[:, :TY]


MEMORY = {"h": pltpu.HBM, "v": pltpu.VMEM, "H": pltpu.HBM, "S": pltpu.HBM}
SPACES = {"h": pltpu.HBM, "v": pltpu.VMEM, "H": pltpu.HBM, "S": pltpu.HBM, "p": pltpu.VMEM, "s": pltpu.SMEM}


def call(kernel, ins, outs, args, shapes, scratch=(), copies=0, lazy=False):
    args = [pltpu.with_memory_space_constraint(a, MEMORY[c]) if c in MEMORY else a for c, a in zip(ins, args)]
    letters = ins + outs
    kinds = [(a.shape, a.dtype) for a in args] + list(shapes)
    moved = [k for k, c in enumerate(letters) if c in "HS"]
    own = len(scratch) + (1 if copies else 0)

    def body(*refs):
        arrays, rest = list(refs[: len(letters)]), refs[len(letters) :]
        sems = rest[-1]
        far = [arrays[k] for k in moved]
        for n, k in enumerate(moved):
            arrays[k] = rest[own + n]
        pending = {k: pltpu.make_async_copy(far[n], arrays[k], sems.at[n]) for n, k in enumerate(moved) if k < len(ins)}
        for copy in pending.values():
            copy.start()
        if lazy:
            kernel(lambda k: pending[k].wait(), *arrays, *rest[:own])
        else:
            for copy in pending.values():
                copy.wait()
            kernel(*arrays, *rest[:own])
        done = [pltpu.make_async_copy(arrays[k], far[n], sems.at[n]) for n, k in enumerate(moved) if k >= len(ins)]
        for copy in done:
            copy.start()
        for copy in done:
            copy.wait()

    return pl.pallas_call(
        body,
        out_shape=tuple(MEMORY[c](s, d) if c in MEMORY else jax.ShapeDtypeStruct(s, d) for c, (s, d) in zip(outs, shapes)),
        in_specs=[pl.BlockSpec(memory_space=SPACES[c]) for c in ins],
        out_specs=tuple(pl.BlockSpec(memory_space=SPACES[c]) for c in outs),
        scratch_shapes=[pltpu.VMEM(s, d) for s, d in scratch]
        + ([pltpu.SemaphoreType.DMA((copies,))] if copies else [])
        + [(pltpu.SMEM if letters[k] == "S" else pltpu.VMEM)(*kinds[k]) for k in moved]
        + [pltpu.SemaphoreType.DMA((max(1, len(moved)),))],
        compiler_params=pltpu.CompilerParams(vmem_limit_bytes=32 << 20),
    )(*args)


def shift(value, axis, by):
    n = lax.axis_size(axis)
    return lax.ppermute(value, axis, [(i, i + by) for i in range(n) if 0 <= i + by < n])


def exchange(value, rows):
    split = value.reshape(rows)
    return lax.all_to_all(split, ("gx", "gy"), split_axis=0, concat_axis=0, tiled=True).reshape(value.shape)


def by_block(value):
    return value.reshape(F, OCEAN, CELLS).transpose(1, 0, 2).reshape(OCEAN * F, CELLS)


def on_device(
    fine_atmospheric_values,
    fine_skin_heat,
    coarse_lowest_values,
    holder_flat,
    corner_offset,
    exchange_patch_holder,
    holder_patch_position,
    coarse_interface_exchange,
    marine_stratum_values,
    diffusion_solver_operator,
):
    owner = exchange_patch_holder.reshape(1, NB)
    place = holder_patch_position.reshape(1, NB)
    names, message, tile, strip = ((1, NB), i32), ((DEV * ROWS, CELLS), bf16), ((F, TX, TY), f32), ((TX, CELLS), f32)
    (windows,) = call(
        pack_kernel, "SHHHh", "h", (corner_offset, owner, place, coarse_lowest_values, fine_atmospheric_values), (message,),
        (((F, 16, TY), f32), ((16, CELLS), f32), ((DEV * ROWS, CELLS), f32), message), 4,
    )
    got = exchange(windows, (DEV, ROWS // 4, 4, CELLS))
    present, _ = lax.optimization_barrier((fine_atmospheric_values, windows))
    ends = ((F * HALO, CELLS), f32)
    low, high, top, bottom = call(strips_kernel, "H", "vvvv", (present,), (strip, strip, ends, ends), (strip,))
    left, right = shift(high, "gy", 1), shift(low, "gy", -1)
    before, after = shift(bottom, "gx", 1), shift(top, "gx", -1)
    holder, corner, _ = lax.optimization_barrier((holder_flat, corner_offset, windows))
    holder = jnp.minimum(holder, DEV - 1)
    wide = (ROWS_X, CELLS)
    *weights, send, back = call(
        tables_kernel, "sSH", "HHHHHHH", (holder, corner, owner),
        (
            ((F * ROWS_X, CELLS), bf16), (wide, f32), (wide, f32), ((CELLS, GROUP), bf16), ((CELLS, CELLS), bf16),
            ((CAP * DEV, NB), bf16), ((NB, CAP * DEV), bf16),
        ),
    )
    sent = ((DEV * CAP * F, CELLS), bf16)
    nest_next, flux = call(
        nest_kernel, "svHHHHHHHvvvvH", "hh",
        (holder, got, *weights, send, fine_atmospheric_values, left, right, before, after, fine_skin_heat), (tile, sent),
        (strip, tile, sent, (wide, f32), ((F * ROWS_X, CELLS), f32), strip, ((DEV * CAP * F, CELLS), f32)), F, True,
    )
    got_flux = exchange(flux, (DEV, CAP, F, CELLS))
    layers = marine_stratum_values.shape[1]
    marine = marine_stratum_values.reshape(F, layers, OCEAN, CELLS).transpose(1, 2, 0, 3).reshape(layers, OCEAN * F, CELLS)
    marine_late, got_late, flux = lax.optimization_barrier((marine, got, flux))
    block = ((OCEAN * F, CELLS), f32)
    hot, give = ((OCEAN * F, DEV * CAP * F), bf16), ((DEV * CAP, OCEAN * F), bf16)
    hot, give, inverse, cover = call(
        hot_kernel, "vH", "HHHH", (got_late, by_block(coarse_interface_exchange)), (hot, give, block, block),
        (((DEV * CAP * F, OCEAN * F), f32), ((DEV * ROWS, CELLS), f32), ((DEV * CAP, OCEAN * F), f32)),
    )
    (layer0,) = call(top_kernel, "Sp", "H", (diffusion_solver_operator, marine_late), (((OCEAN * F + 8, CELLS), f32),))
    returned = ((DEV * CAP, CELLS), f32)
    forcing, skins = call(
        ocean_kernel, "HHHHHH", "HH", (got_flux, hot, inverse, cover, layer0, give), (block, returned)
    )
    arrived = exchange(skins, (DEV, 1, CAP * CELLS))
    part = 32
    refreshed = pl.pallas_call(
        mix_kernel,
        out_shape=jax.ShapeDtypeStruct((layers, OCEAN * F, CELLS), f32),
        grid=(OCEAN * F // part,),
        in_specs=[
            pl.BlockSpec((layers, layers), lambda g: (0, 0)),
            pl.BlockSpec((part, CELLS), lambda g: (g, 0)),
            pl.BlockSpec((layers, part, CELLS), lambda g: (0, g, 0)),
        ],
        out_specs=pl.BlockSpec((layers, part, CELLS), lambda g: (0, g, 0)),
        scratch_shapes=[pltpu.VMEM((8 * layers, 8 * layers), bf16)] * 2,
        compiler_params=pltpu.CompilerParams(vmem_limit_bytes=40 << 20),
    )(diffusion_solver_operator, forcing, marine)
    refreshed = refreshed.reshape(layers, OCEAN, F, CELLS).transpose(2, 0, 1, 3).reshape(marine_stratum_values.shape)
    (skin,) = call(skin_kernel, "vH", "p", (arrived, back), (((TX, TY), f32),), (((TX, CELLS), f32),))
    return (nest_next, refreshed, skin)


def solution(mesh):
    in_specs = (
        P(None, "gx", "gy"),
        P("gx", "gy"),
        P(None, "gx", "gy"),
        P(),
        P(),
        P(("gx", "gy"), None),
        P(("gx", "gy")),
        P(None, ("gx", "gy")),
        P(None, None, ("gx", "gy")),
        P(),
    )
    out_specs = (P(None, "gx", "gy"), P(None, None, ("gx", "gy")), P("gx", "gy"))
    return jax.shard_map(
        on_device, mesh=mesh, in_specs=in_specs, out_specs=out_specs, check_vma=False
    )
```

```python
import jax
import jax.numpy as jnp
from jax import lax
from jax.experimental import pallas as pl
from jax.experimental.pallas import tpu as pltpu
from jax.sharding import PartitionSpec as P

F = 4
CELLS = 128
OCEAN = 32
STEPS = 4
TX, TY = 192, 96
GX, GY = 8, 16
DEV = GX * GY
PC = 384
CAP = 3
NB = 144
HALO = 4
ROWS_X = TX + 2 * HALO
PAD = 8
WP = 32
WQ = 18
ROWS = 20
GROUP = 4 * ROWS
PROW = 256
LEFT = tuple(
    i for i in range(GX) if i < GX - 1 and (4 * (TX * i + TX + 2) - 11) // 26 + 1 - (4 * (TX * i - 3) - 11) // 26 >= WP
)
f32, bf16, i32 = jnp.float32, jnp.bfloat16, jnp.int32

diffuse_coef = 0.24
relax_coef = 0.3
drag_coefficient = 0.5


def iota(shape, dim):
    return lax.broadcasted_iota(i32, shape, dim)


def first_x(i):
    return (4 * (TX * i - 3) - 11) // 26


def first_y(j):
    return (4 * (TY * j - 3) - 11) // 26


def first_y_of(j):
    return ((4 * TY * j + 3) * 2521 >> 16) - 1


def first_x_of(i):
    return ((4 * TX * i + 3) * 2521 >> 16) - 1


def dot(a, b):
    return jnp.dot(a, b, preferred_element_type=f32)


def dot_nt(a, b):
    return lax.dot_general(a, b, (((1,), (1,)), ((), ())), preferred_element_type=f32)


def split3(x):
    high = x.astype(bf16)
    rest = x - high.astype(f32)
    mid = rest.astype(bf16)
    return high, mid, (rest - mid.astype(f32)).astype(bf16)


def column_of(row):
    n = row.shape[1]
    return jnp.sum(jnp.where(iota((n, n), 0) == iota((n, n), 1), row, 0), axis=1, keepdims=True)


def fetch(pairs, sems):
    copies = [pltpu.make_async_copy(src, dst, sems.at[k]) for k, (src, dst) in enumerate(pairs)]
    for copy in copies:
        copy.start()
    return copies


def rank_of(column, row, number):
    return jnp.sum(jnp.where((column == row) & (iota((NB, NB), 0) < number), 1, 0), axis=0, keepdims=True)


def by_thirds(column):
    at = iota((1, NB), 1)
    third = (at >= NB // CAP).astype(i32) + (at >= 2 * (NB // CAP)).astype(i32)
    number = CAP * (at - third * (NB // CAP)) + third
    return number, jnp.sum(jnp.where(iota((NB, NB), 0) == number, column, 0), axis=0, keepdims=True)


PARTS = 3
EDGE = 3
CORNER = F * EDGE * EDGE
FREE = 16
CORNERS = ((-1, -1), (-1, 1), (1, -1), (1, 1))


def neighbour(step):
    x, y = lax.axis_index("gx") + step[0], lax.axis_index("gy") + step[1]
    there = (x >= 0) & (x < GX) & (y >= 0) & (y < GY)
    return jnp.where(there, x * GY + y, 0), there


def corner_rows(s_ref, wide_ref):
    lane, sub = iota((8, CELLS), 1), iota((8, CELLS), 0)
    wide_ref[...] = jnp.zeros_like(wide_ref)
    out = jnp.zeros((8, CELLS), f32)
    for f in range(F):
        wide_ref[:, :TY] = s_ref[f]
        for k, (dx, dy) in enumerate(CORNERS):
            for r in range(EDGE):
                row = r if dx < 0 else 16 - EDGE + r
                column = 0 if dy < 0 else TY - EDGE
                at = FREE + (f * EDGE + r) * EDGE
                moved = pltpu.roll(jnp.broadcast_to(wide_ref[row : row + 1, :], (8, CELLS)), (at - column) % CELLS, 1)
                out = jnp.where((sub == k) & (lane >= at) & (lane < at + EDGE), moved, out)
    high, mid, low = (x.astype(f32) for x in split3(out))
    return high + pltpu.roll(mid, CORNER, 1) + pltpu.roll(low, 2 * CORNER, 1)


def pack_kernel(
    wait, corner_ref, owner_ref, place_ref, parent_ref, s_any, out_any, s_ref, wide_ref, pick_ref, z_ref, out_ref, sems,
):
    ends = fetch([(s_any.at[:, pl.ds(src, 8), :], s_ref.at[:, pl.ds(dst, 8), :]) for dst, src in ((0, 0), (8, TX - 8))], sems)
    wait(0)
    cx, cy = corner_ref[0], corner_ref[1]
    base = pl.multiple_of(jnp.minimum(jnp.maximum(cx - 1, 0) // 16 * 16, PC - PROW), 16)
    row = iota((GY * ROWS, 1), 0)
    j = row * 3277 >> 16
    r = row - j * ROWS
    wanted = jnp.where(r < WQ, cy + first_y_of(j) + r, -1)
    pick_y = (wanted == iota((GY * ROWS, PC), 1)).astype(f32).astype(bf16)
    lane = iota((1, 2 * CELLS), 1)
    for f in range(F):
        i = (lane >> 7) * F + (((lane >> 5) - f) & 3)
        p = cx - base + first_x_of(i) + (lane & (WP - 1))
        pick_ref[f] = (iota((PROW, 2 * CELLS), 0) == p).astype(f32).astype(bf16)
    wait(1)
    wait(2)
    owner = owner_ref[...]
    rank = rank_of(column_of(owner), owner, iota((NB, NB), 1))
    named = iota((DEV, NB), 0) == owner
    slots = jnp.zeros((DEV, CELLS), f32)
    for s in range(CAP):
        value = jnp.sum(jnp.where(named & (rank == s), place_ref[...] + 1, 0).astype(f32), axis=1, keepdims=True) - 1.0
        slots = jnp.where(iota((DEV, CELLS), 1) == s, value, slots)
    for copy in ends:
        copy.wait()
    corners = corner_rows(s_ref, wide_ref)
    for k, step in enumerate(CORNERS):
        other, there = neighbour(step)
        slots = slots + jnp.where(iota((DEV, CELLS), 0) == jnp.where(there, other, -1), corners[k : k + 1, :], 0.0)
    wait(3)
    parts = [parent_ref[f, pl.ds(base, PROW), :] for f in range(F)]
    windows = [dot(dot_nt(pick_y, parts[f]).astype(bf16), pick_ref[f]) for f in range(F)]
    j16 = iota((GY, PC), 0)
    q = iota((GY, PC), 1) - (cy + first_y_of(j16))
    inside = (q >= 0) & (q < WQ)
    lanes = iota((GY, CELLS), 1) >> 5
    erow = iota((8, PROW), 0)
    target = jnp.full((8, PROW), -1, i32)
    for k, i in enumerate(LEFT):
        target = jnp.where(erow == k, cx - base + first_x(i) + WP, target)
    pick_row = (target == iota((8, PROW), 1)).astype(f32).astype(bf16)
    left = [jnp.zeros((GY, CELLS), f32) for _ in LEFT]
    for f in range(F):
        rows = dot(pick_row, parts[f])
        for k in range(len(LEFT)):
            kept = jnp.where(inside, rows[k : k + 1, :], 0.0)
            folded = kept[:, :128] + kept[:, 128:256] + kept[:, 256:]
            folded = folded + pltpu.roll(folded, 64, 1)
            folded = folded + pltpu.roll(folded, 32, 1)
            left[k] = jnp.where(lanes == f, folded, left[k])
    copies = []
    size = 2 * GY * ROWS
    quarter = iota((GY * ROWS, CELLS), 1) >> 5
    for pair in range(GX // 2):
        for i in (2 * pair, 2 * pair + 1):
            tile = slice(i // F * CELLS, i // F * CELLS + CELLS)
            message = windows[0][:, tile]
            for f in range(1, F):
                message = jnp.where(quarter == (f + i) % F, windows[f][:, tile], message)
            z_ref[pl.ds(i * GY * ROWS, GY * ROWS), :] = message
            if i in LEFT:
                z_ref[pl.ds(i * GY * ROWS + WQ, GY, stride=ROWS), :] = left[LEFT.index(i)]
        z_ref[pl.ds(pair * size + ROWS - 1, 2 * GY, stride=ROWS), :] = slots[2 * GY * pair : 2 * GY * (pair + 1)]
        copies.append(write(z_ref, out_ref, out_any, sems.at[pair], pl.ds(pair * size, size)))
    for copy in copies:
        copy.wait()


def write(z_ref, out_ref, out_any, sem, at):
    out_ref[at, :] = z_ref[at, :].astype(bf16)
    copy = pltpu.make_async_copy(out_ref.at[at, :], out_any.at[at, :], sem)
    copy.start()
    return copy


def hat(fine, anchor, coarse):
    centre = (fine.astype(f32) + 0.5) * (2.0 / 13.0) - 0.5 + anchor.astype(f32)
    return jnp.maximum(0.0, 1.0 - jnp.abs(centre - coarse.astype(f32)))


FOLD = TX // (CELLS // (F * HALO))


def strips_kernel(s_ref, low_ref, high_ref, top_ref, bottom_ref, wide_ref):
    field = iota((TX, CELLS), 1) >> 2
    wide_ref[...] = jnp.zeros_like(wide_ref)
    low, high = jnp.zeros((TX, CELLS), f32), jnp.zeros((TX, CELLS), f32)
    for f in range(F):
        wide_ref[:, :TY] = s_ref[f]
        s = wide_ref[...]
        low = jnp.where(field == f, s if f == 0 else pltpu.roll(s, HALO * f, 1), low)
        high = jnp.where(field == f, pltpu.roll(s, CELLS - TY + HALO + HALO * f, 1), high)
        top_ref[f * HALO : (f + 1) * HALO, :] = pltpu.roll(s[:8], HALO, 1)[:HALO]
        bottom_ref[f * HALO : (f + 1) * HALO, :] = pltpu.roll(s[TX - 8 :], HALO, 1)[HALO:]
    for strip, ref in ((low, low_ref), (high, high_ref)):
        packed = strip[:FOLD]
        for g in range(1, TX // FOLD):
            packed = packed + pltpu.roll(strip[g * FOLD : (g + 1) * FOLD], g * F * HALO, 1)
        ref[...] = packed


def unfolded(packed):
    n = F * HALO
    return jnp.concatenate([packed] + [pltpu.roll(packed, CELLS - g * n, 1) for g in range(1, TX // FOLD)], axis=0)


def widened(s, left, right, f):
    lane = iota(s.shape, 1)
    before = left if f == 0 else pltpu.roll(left, CELLS - HALO * f, 1)
    after = pltpu.roll(right, TY + HALO - HALO * f, 1)
    wide = jnp.where(lane < TY + HALO, pltpu.roll(s, HALO, 1), after)
    return jnp.where(lane < HALO, before, jnp.where(lane < TY + 2 * HALO, wide, 0.0))


def corner_of(got_ref, step):
    other, there = neighbour(step)
    rows = got_ref[pl.ds(pl.multiple_of((other >> 2) * GROUP, 16), GROUP), :].astype(f32)
    mine = jnp.where(there, (other & 3) * ROWS + ROWS - 1, -1)
    row = jnp.sum(jnp.where(iota((GROUP, CELLS), 0) == mine, rows, 0.0), axis=0, keepdims=True)
    row = jnp.broadcast_to(row, (8, CELLS))
    return row + pltpu.roll(row, CELLS - CORNER, 1) + pltpu.roll(row, CELLS - 2 * CORNER, 1)


def nest_kernel(
    wait, holder_ref, corner_ref, owner_ref, got_ref, s_ref, left_ref, right_ref, before_ref, after_ref, skin_ref,
    next_any, out_any, wx_ref, wide_ref, next_ref, out_ref, state_ref, force_ref, flux_ref, z_ref, sems,
):
    wide_ref[...] = jnp.zeros_like(wide_ref)
    flux_ref[...] = jnp.zeros_like(flux_ref)
    corners = [corner_of(got_ref, step) for step in CORNERS]
    group = pl.multiple_of((holder_ref[0] >> 2) * GROUP, 16)
    got = got_ref[pl.ds(group, GROUP), :]
    wait(1)
    ix, iy = lax.axis_index("gx"), lax.axis_index("gy")
    cx, cy = corner_ref[0], corner_ref[1]
    x0, y0 = ix * TX - HALO, iy * TY - HALO
    px, qy = cx + first_x_of(ix), cy + first_y_of(iy)
    lane = iota((ROWS_X, CELLS), 1)
    row = iota((ROWS_X, CELLS), 0)
    weight = hat(row + x0, cx, (lane & (WP - 1)) + px)
    for f in range(F):
        wx_ref[f * ROWS_X : (f + 1) * ROWS_X, :] = jnp.where(lane >> 5 == ((f + ix) & 3), weight, 0.0).astype(bf16)
    weight_last = relax_coef / diffuse_coef * hat(row + x0, cx, jnp.full_like(row, WP) + px).astype(bf16).astype(f32)
    inside = (row + x0 >= 0) & (row + x0 < GX * TX) & (lane + y0 >= 0) & (lane + y0 < GY * TY)
    mask = jnp.where(inside, diffuse_coef, 0.0)
    for now in range(2):
        state_ref[:, now, :PAD, :] = jnp.zeros((F, PAD, CELLS), f32)
        state_ref[:, now, PAD + ROWS_X :, :] = jnp.zeros((F, PAD, CELLS), f32)
    at = iota((CELLS, GROUP), 1) - (holder_ref[0] & 3) * ROWS
    weight_y = jnp.where((at >= 0) & (at < WQ), hat(iota((CELLS, GROUP), 0) + y0, cy, at + qy), 0.0).astype(bf16)
    lane = iota((CELLS, CELLS), 1)
    weight_c = hat(iota((CELLS, CELLS), 0) + y0, cy, qy + ((lane - qy) & (WP - 1))).astype(bf16)
    partial = dot(weight_y, got).astype(bf16)
    last = jnp.sum(
        jnp.where(iota((GROUP, CELLS), 0) == (holder_ref[0] & 3) * ROWS + WQ, got.astype(f32), 0.0), axis=0, keepdims=True
    )
    last = jnp.where(iota((8, CELLS), 1) >> 5 == iota((8, CELLS), 0), last, 0.0).astype(bf16)
    partial_last = dot_nt(last, weight_c).astype(bf16).astype(f32)
    force_ref[...] = dot_nt(wx_ref[...], partial)
    wait(2)
    column = column_of(owner_ref[...])
    number, owner = by_thirds(column)
    send = (iota((CAP * DEV, NB), 0) == rank_of(column, owner, number) * DEV + owner).astype(f32).astype(bf16)
    wait(4)
    left, right = unfolded(left_ref[...]), unfolded(right_ref[...])
    lane, sub = iota((8, CELLS), 1), iota((8, CELLS), 0)
    written = []
    for f in range(F):
        force = relax_coef / diffuse_coef * force_ref[f * ROWS_X : (f + 1) * ROWS_X, :] + weight_last * partial_last[f : f + 1, :]
        wide_ref[f, :, :TY] = s_ref[f]
        state_ref[f, 0, PAD : PAD + HALO, :] = before_ref[f * HALO : (f + 1) * HALO, :]
        state_ref[f, 0, PAD + HALO : PAD + HALO + TX, :] = widened(wide_ref[f], left, right, f)
        state_ref[f, 0, PAD + HALO + TX : PAD + ROWS_X, :] = after_ref[f * HALO : (f + 1) * HALO, :]
        for side, base in ((-1, PAD), (1, PAD + ROWS_X - 8)):
            tile = state_ref[f, 0, base : base + 8, :]
            for k, (dx, dy) in enumerate(CORNERS):
                for r in range(EDGE if dx == side else 0):
                    row = HALO - EDGE + r if dx < 0 else 8 - HALO + r
                    column = HALO - EDGE if dy < 0 else HALO + TY
                    at = FREE + (f * EDGE + r) * EDGE
                    moved = pltpu.roll(corners[k], (column - at) % CELLS, 1)
                    tile = jnp.where((sub == row) & (lane >= column) & (lane < column + EDGE), moved, tile)
            state_ref[f, 0, base : base + 8, :] = tile
        s = state_ref[f, 0, PAD : PAD + ROWS_X, :]
        for step in range(STEPS):
            now = step % 2
            beside = state_ref[f, now, PAD - 1 : PAD - 1 + ROWS_X, :] + state_ref[f, now, PAD + 1 : PAD + 1 + ROWS_X, :]
            beside = beside + (pltpu.roll(s, 1, 1) + pltpu.roll(s, CELLS - 1, 1))
            s = mask * ((1.0 - 4.0 * diffuse_coef - relax_coef) / diffuse_coef * s + beside + force)
            state_ref[f, 1 - now, PAD : PAD + ROWS_X, :] = s if step < STEPS - 1 else pltpu.roll(s, CELLS - HALO, 1)
        last_state = state_ref.at[f, STEPS % 2]
        next_ref[f] = last_state[PAD + HALO : PAD + HALO + TX, :TY]
    u, v, ta, qa = next_ref[0], next_ref[1], next_ref[2], next_ref[3]
    half = drag_coefficient * jnp.sqrt(1.0 + u * u + v * v)
    written.append(pltpu.make_async_copy(next_ref, next_any, sems.at[4]))
    written[0].start()
    wait(9)
    skin = skin_ref[...]
    flux = (half * (ta - skin), half * (qa - 0.5 * skin), half * u, half * v)
    rows = NB // CAP
    lane = iota((rows, CELLS), 1)
    blocks = []
    for f in range(F):
        flux_ref[f, :, :TY] = flux[f]
        m = [flux_ref[f, pl.ds(k, rows, stride=4), :] for k in range(4)]
        r1, r2, r3 = pltpu.roll(m[1], 96, 1), pltpu.roll(m[2], 64, 1), pltpu.roll(m[3], 32, 1)
        blocks.append(
            jnp.concatenate(
                [jnp.where(lane < 96, m[0], r1), jnp.where(lane < 64, r1, r2), jnp.where(lane < 32, r2, r3)], axis=0
            ).astype(bf16)
        )
    sent = dot(send, jnp.concatenate(blocks, axis=1))
    part = DEV // 4
    for c in range(4):
        for slot in range(CAP):
            for f in range(F):
                z_ref[pl.ds(c * part * CAP * F + slot * F + f, part, stride=CAP * F), :] = sent[
                    slot * DEV + c * part : slot * DEV + (c + 1) * part, f * CELLS : (f + 1) * CELLS
                ]
        written.append(write(z_ref, out_ref, out_any, sems.at[c], pl.ds(c * part * CAP * F, part * CAP * F)))
    for copy in written:
        copy.wait()


def hot_kernel(
    got_ref, kept_ref, owner_ref, hot_ref, give_ref, inverse_ref, cover_ref, back_ref, z_ref, slot_ref, row_ref
):
    column = column_of(owner_ref[...])
    number, owner = by_thirds(column)
    source = column_of(owner * CAP + rank_of(column, owner, number))
    back_ref[...] = (source == iota((NB, CAP * DEV), 1)).astype(f32).astype(bf16)
    slot_ref[...] = got_ref[...].astype(f32)
    slots = slot_ref[pl.ds(ROWS - 1, DEV, stride=ROWS), :].astype(i32)
    lane = iota((DEV, OCEAN * F), 1)
    for s in range(CAP):
        target = slots[:, s : s + 1] * F
        for f in range(F):
            z_ref[pl.ds(s * F + f, DEV, stride=CAP * F), :] = (lane == jnp.where(target < 0, -1, target + f)).astype(f32)
        row_ref[pl.ds(s, DEV, stride=CAP), :] = (lane == target).astype(f32)
    give_ref[...] = row_ref[...].astype(bf16)
    hot = jnp.swapaxes(z_ref[...], 0, 1)
    hot_ref[...] = hot.astype(bf16)
    count = jnp.sum(hot, axis=1, keepdims=True)
    inverse_ref[...] = jnp.broadcast_to(1.0 / jnp.maximum(count, 1.0), (OCEAN * F, CELLS))
    cover_ref[...] = jnp.where(count == 0.0, kept_ref[...], 0.0)


def top_kernel(scale_ref, marine_ref, out_ref):
    total = scale_ref[0, 0] * marine_ref[0]
    for k in range(1, marine_ref.shape[0]):
        total = total + scale_ref[0, k] * marine_ref[k]
    out_ref[: OCEAN * F, :] = total
    out_ref[OCEAN * F :, :] = jnp.full((8, CELLS), scale_ref[0, 0], f32)


def ocean_kernel(wait, got_ref, hot_ref, inverse_ref, cover_ref, top_ref, give_ref, forcing_ref, out_ref):
    wait(1)
    wait(0)
    sums = dot(hot_ref[...], got_ref[...])
    for k in (2, 3, 4, 5):
        wait(k)
    forcing = sums * inverse_ref[...] + cover_ref[...]
    forcing_ref[...] = forcing
    top = top_ref[: OCEAN * F, :] + top_ref[OCEAN * F : OCEAN * F + 1, :] * forcing
    back = dot(give_ref[...], jnp.concatenate(split3(top), axis=1))
    out_ref[...] = back[:, :CELLS] + back[:, CELLS : 2 * CELLS] + back[:, 2 * CELLS :]

def mix_kernel(scale_ref, forcing_ref, marine_ref, out_ref, high_ref, low_ref):
    layers = marine_ref.shape[0]
    n = 8 * layers

    @pl.when(pl.program_id(0) == 0)
    def _():
        spread = (iota((n, layers), 0) >> 3 == iota((n, layers), 1)).astype(f32).astype(bf16)
        same = (iota((n, n), 0) & 7) == (iota((n, n), 1) & 7)
        scale = scale_ref[...]
        high = scale.astype(bf16)
        low = (scale - high.astype(f32)).astype(bf16)
        for part, ref in ((high, high_ref), (low, low_ref)):
            wide = dot_nt(dot(spread, part).astype(bf16), spread)
            ref[...] = jnp.where(same, wide, 0.0).astype(bf16)

    groups = marine_ref.shape[1] // 8
    columns = []
    for g in range(groups):
        x = marine_ref[:, 8 * g : 8 * g + 8, :].reshape(n, CELLS)
        first = x[:8] + forcing_ref[8 * g : 8 * g + 8, :]
        columns.append(jnp.concatenate([first, x[8:]], axis=0))
    x = jnp.concatenate(columns, axis=1)
    high = x.astype(bf16)
    low = (x - high.astype(f32)).astype(bf16)
    y = dot(high_ref[...], high) + (dot(high_ref[...], low) + dot(low_ref[...], high))
    for g in range(groups):
        out_ref[:, 8 * g : 8 * g + 8, :] = y[:, g * CELLS : (g + 1) * CELLS].reshape(layers, 8, CELLS)


def skin_kernel(got_ref, back_ref, out_ref, tile_ref):
    x = dot(back_ref[...], jnp.concatenate(split3(got_ref[...]), axis=1))
    x = x[:, :CELLS] + x[:, CELLS : 2 * CELLS] + x[:, 2 * CELLS :]
    rows = NB // CAP
    t0, t1, t2 = x[:rows], x[rows : 2 * rows], x[2 * rows :]
    lane = iota((rows, CELLS), 1)
    tile_ref[pl.ds(0, rows, stride=4), :] = t0
    tile_ref[pl.ds(1, rows, stride=4), :] = pltpu.roll(jnp.where(lane < 64, t1, t0), 32, 1)
    tile_ref[pl.ds(2, rows, stride=4), :] = pltpu.roll(jnp.where(lane < 32, t2, t1), 64, 1)
    tile_ref[pl.ds(3, rows, stride=4), :] = pltpu.roll(t2, 96, 1)
    out_ref[...] = tile_ref[:, :TY]


MEMORY = {"h": pltpu.HBM, "v": pltpu.VMEM, "H": pltpu.HBM, "S": pltpu.HBM}
SPACES = {"h": pltpu.HBM, "v": pltpu.VMEM, "H": pltpu.HBM, "S": pltpu.HBM, "p": pltpu.VMEM, "s": pltpu.SMEM}


def call(kernel, ins, outs, args, shapes, scratch=(), copies=0, lazy=False):
    args = [pltpu.with_memory_space_constraint(a, MEMORY[c]) if c in MEMORY else a for c, a in zip(ins, args)]
    letters = ins + outs
    kinds = [(a.shape, a.dtype) for a in args] + list(shapes)
    moved = [k for k, c in enumerate(letters) if c in "HS"]
    own = len(scratch) + (1 if copies else 0)

    def body(*refs):
        arrays, rest = list(refs[: len(letters)]), refs[len(letters) :]
        sems = rest[-1]
        far = [arrays[k] for k in moved]
        for n, k in enumerate(moved):
            arrays[k] = rest[own + n]
        pending = {k: pltpu.make_async_copy(far[n], arrays[k], sems.at[n]) for n, k in enumerate(moved) if k < len(ins)}
        for copy in pending.values():
            copy.start()
        if lazy:
            kernel(lambda k: pending[k].wait(), *arrays, *rest[:own])
        else:
            for copy in pending.values():
                copy.wait()
            kernel(*arrays, *rest[:own])
        done = [pltpu.make_async_copy(arrays[k], far[n], sems.at[n]) for n, k in enumerate(moved) if k >= len(ins)]
        for copy in done:
            copy.start()
        for copy in done:
            copy.wait()

    return pl.pallas_call(
        body,
        out_shape=tuple(MEMORY[c](s, d) if c in MEMORY else jax.ShapeDtypeStruct(s, d) for c, (s, d) in zip(outs, shapes)),
        in_specs=[pl.BlockSpec(memory_space=SPACES[c]) for c in ins],
        out_specs=tuple(pl.BlockSpec(memory_space=SPACES[c]) for c in outs),
        scratch_shapes=[pltpu.VMEM(s, d) for s, d in scratch]
        + ([pltpu.SemaphoreType.DMA((copies,))] if copies else [])
        + [(pltpu.SMEM if letters[k] == "S" else pltpu.VMEM)(*kinds[k]) for k in moved]
        + [pltpu.SemaphoreType.DMA((max(1, len(moved)),))],
        compiler_params=pltpu.CompilerParams(vmem_limit_bytes=32 << 20),
    )(*args)


def shift(value, axis, by):
    n = lax.axis_size(axis)
    return lax.ppermute(value, axis, [(i, i + by) for i in range(n) if 0 <= i + by < n])


def exchange(value, rows):
    split = value.reshape(rows)
    return lax.all_to_all(split, ("gx", "gy"), split_axis=0, concat_axis=0, tiled=True).reshape(value.shape)


def by_block(value):
    return value.reshape(F, OCEAN, CELLS).transpose(1, 0, 2).reshape(OCEAN * F, CELLS)


def on_device(
    fine_atmospheric_values,
    fine_skin_heat,
    coarse_lowest_values,
    holder_flat,
    corner_offset,
    exchange_patch_holder,
    holder_patch_position,
    coarse_interface_exchange,
    marine_stratum_values,
    diffusion_solver_operator,
):
    owner = exchange_patch_holder.reshape(1, NB)
    place = holder_patch_position.reshape(1, NB)
    names, message, tile, strip = ((1, NB), i32), ((DEV * ROWS, CELLS), bf16), ((F, TX, TY), f32), ((TX, CELLS), f32)
    (windows,) = call(
        pack_kernel, "SHHHh", "h", (corner_offset, owner, place, coarse_lowest_values, fine_atmospheric_values), (message,),
        (
            ((F, 16, TY), f32), ((16, CELLS), f32), ((F, PROW, 2 * CELLS), bf16), ((DEV * ROWS, CELLS), f32),
            message,
        ), 4, True,
    )
    got = exchange(windows, (DEV, ROWS // 4, 4, CELLS))
    present, _ = lax.optimization_barrier((fine_atmospheric_values, windows))
    ends, fold = ((F * HALO, CELLS), f32), ((FOLD, CELLS), f32)
    low, high, top, bottom = call(strips_kernel, "H", "vvvv", (present,), (fold, fold, ends, ends), (strip,))
    left, right = shift(high, "gy", 1), shift(low, "gy", -1)
    before, after = shift(bottom, "gx", 1), shift(top, "gx", -1)
    holder, _ = lax.optimization_barrier((holder_flat, windows))
    holder = jnp.minimum(holder, DEV - 1)
    sent, strips = ((DEV * CAP * F, CELLS), bf16), ((F, TX, CELLS), f32)
    nest_next, flux = call(
        nest_kernel, "sSHvHvvvvH", "hh",
        (holder, corner_offset, owner, got, fine_atmospheric_values, left, right, before, after, fine_skin_heat), (tile, sent),
        (
            ((F * ROWS_X, CELLS), bf16), strips, tile, sent, ((F, 2, ROWS_X + 2 * PAD, CELLS), f32),
            ((F * ROWS_X, CELLS), f32), strips, ((DEV * CAP * F, CELLS), f32),
        ), 5, True,
    )
    got_flux = exchange(flux, (DEV, CAP, F, CELLS))
    layers = marine_stratum_values.shape[1]
    marine = marine_stratum_values.reshape(F, layers, OCEAN, CELLS).transpose(1, 2, 0, 3).reshape(layers, OCEAN * F, CELLS)
    marine_late, got_late, flux = lax.optimization_barrier((marine, got, flux))
    block = ((OCEAN * F, CELLS), f32)
    hot, give = ((OCEAN * F, DEV * CAP * F), bf16), ((DEV * CAP, OCEAN * F), bf16)
    hot, give, inverse, cover, back = call(
        hot_kernel, "vHH", "HHHHv", (got_late, by_block(coarse_interface_exchange), owner),
        (hot, give, block, block, ((NB, CAP * DEV), bf16)),
        (((DEV * CAP * F, OCEAN * F), f32), ((DEV * ROWS, CELLS), f32), ((DEV * CAP, OCEAN * F), f32)),
    )
    (layer0,) = call(top_kernel, "Sp", "H", (diffusion_solver_operator, marine_late), (((OCEAN * F + 8, CELLS), f32),))
    returned = ((DEV * CAP, CELLS), f32)
    forcing, skins = call(
        ocean_kernel, "HHHHHH", "HH", (got_flux, hot, inverse, cover, layer0, give), (block, returned),
        lazy=True,
    )
    arrived = exchange(skins, (DEV, 1, CAP * CELLS))
    part = 32
    refreshed = pl.pallas_call(
        mix_kernel,
        out_shape=jax.ShapeDtypeStruct((layers, OCEAN * F, CELLS), f32),
        grid=(OCEAN * F // part,),
        in_specs=[
            pl.BlockSpec((layers, layers), lambda g: (0, 0)),
            pl.BlockSpec((part, CELLS), lambda g: (g, 0)),
            pl.BlockSpec((layers, part, CELLS), lambda g: (0, g, 0)),
        ],
        out_specs=pl.BlockSpec((layers, part, CELLS), lambda g: (0, g, 0)),
        scratch_shapes=[pltpu.VMEM((8 * layers, 8 * layers), bf16)] * 2,
        compiler_params=pltpu.CompilerParams(vmem_limit_bytes=40 << 20),
    )(diffusion_solver_operator, forcing, marine)
    refreshed = refreshed.reshape(layers, OCEAN, F, CELLS).transpose(2, 0, 1, 3).reshape(marine_stratum_values.shape)
    (skin,) = call(skin_kernel, "vv", "p", (arrived, back), (((TX, TY), f32),), (((TX, CELLS), f32),))
    return (nest_next, refreshed, skin)


def solution(mesh):
    in_specs = (
        P(None, "gx", "gy"),
        P("gx", "gy"),
        P(None, "gx", "gy"),
        P(),
        P(),
        P(("gx", "gy"), None),
        P(("gx", "gy")),
        P(None, ("gx", "gy")),
        P(None, None, ("gx", "gy")),
        P(),
    )
    out_specs = (P(None, "gx", "gy"), P(None, None, ("gx", "gy")), P("gx", "gy"))
    return jax.shard_map(
        on_device, mesh=mesh, in_specs=in_specs, out_specs=out_specs, check_vma=False
    )
```

```python
import jax
import jax.numpy as jnp
from jax import lax
from jax.experimental import pallas as pl
from jax.experimental.pallas import tpu as pltpu
from jax.sharding import PartitionSpec as P

F = 4
CELLS = 128
OCEAN = 32
STEPS = 4
TX, TY = 192, 96
GX, GY = 8, 16
DEV = GX * GY
PC = 384
CAP = 3
NB = 144
HALO = 4
ROWS_X = TX + 2 * HALO
PAD = 8
WP = 32
WQ = 18
ROWS = 20
GROUP = 4 * ROWS
PROW = 256
LEFT = tuple(
    i for i in range(GX) if i < GX - 1 and (4 * (TX * i + TX + 2) - 11) // 26 + 1 - (4 * (TX * i - 3) - 11) // 26 >= WP
)
f32, bf16, i32 = jnp.float32, jnp.bfloat16, jnp.int32

diffuse_coef = 0.24
relax_coef = 0.3
drag_coefficient = 0.5


def iota(shape, dim):
    return lax.broadcasted_iota(i32, shape, dim)


def first_x(i):
    return (4 * (TX * i - 3) - 11) // 26


def first_y(j):
    return (4 * (TY * j - 3) - 11) // 26


def first_y_of(j):
    return ((4 * TY * j + 3) * 2521 >> 16) - 1


def first_x_of(i):
    return ((4 * TX * i + 3) * 2521 >> 16) - 1


def dot(a, b):
    return jnp.dot(a, b, preferred_element_type=f32)


def dot_nt(a, b):
    return lax.dot_general(a, b, (((1,), (1,)), ((), ())), preferred_element_type=f32)


def split3(x):
    high = x.astype(bf16)
    rest = x - high.astype(f32)
    mid = rest.astype(bf16)
    return high, mid, (rest - mid.astype(f32)).astype(bf16)


def column_of(row):
    n = row.shape[1]
    return jnp.sum(jnp.where(iota((n, n), 0) == iota((n, n), 1), row, 0), axis=1, keepdims=True)


def fetch(pairs, sems):
    copies = [pltpu.make_async_copy(src, dst, sems.at[k]) for k, (src, dst) in enumerate(pairs)]
    for copy in copies:
        copy.start()
    return copies


def rank_of(column, row, number):
    return jnp.sum(jnp.where((column == row) & (iota((NB, NB), 0) < number), 1, 0), axis=0, keepdims=True)


def by_thirds(column):
    at = iota((1, NB), 1)
    third = (at >= NB // CAP).astype(i32) + (at >= 2 * (NB // CAP)).astype(i32)
    number = CAP * (at - third * (NB // CAP)) + third
    return number, jnp.sum(jnp.where(iota((NB, NB), 0) == number, column, 0), axis=0, keepdims=True)


PARTS = 3
EDGE = 3
CORNER = F * EDGE * EDGE
FREE = 16
CORNERS = ((-1, -1), (-1, 1), (1, -1), (1, 1))


def neighbour(step):
    x, y = lax.axis_index("gx") + step[0], lax.axis_index("gy") + step[1]
    there = (x >= 0) & (x < GX) & (y >= 0) & (y < GY)
    return jnp.where(there, x * GY + y, 0), there


def corner_rows(wide_ref):
    lane, sub = iota((8, CELLS), 1), iota((8, CELLS), 0)
    out = jnp.zeros((8, CELLS), f32)
    for f in range(F):
        for k, (dx, dy) in enumerate(CORNERS):
            for r in range(EDGE):
                row = r if dx < 0 else TX - EDGE + r
                column = 0 if dy < 0 else TY - EDGE
                at = FREE + (f * EDGE + r) * EDGE
                moved = pltpu.roll(jnp.broadcast_to(wide_ref[f, row : row + 1, :], (8, CELLS)), (at - column) % CELLS, 1)
                out = jnp.where((sub == k) & (lane >= at) & (lane < at + EDGE), moved, out)
    high, mid, low = (x.astype(f32) for x in split3(out))
    return high + pltpu.roll(mid, CORNER, 1) + pltpu.roll(low, 2 * CORNER, 1)


def pack_kernel(
    wait, corner_ref, owner_ref, place_ref, parent_ref, s_ref, out_any, low_ref, high_ref, top_ref, bottom_ref,
    wide_ref, pick_ref, z_ref, out_ref, sems,
):
    wait(0)
    cx, cy = corner_ref[0], corner_ref[1]
    base = pl.multiple_of(jnp.minimum(jnp.maximum(cx - 1, 0) // 16 * 16, PC - PROW), 16)
    row = iota((GY * ROWS, 1), 0)
    j = row * 3277 >> 16
    r = row - j * ROWS
    wanted = jnp.where(r < WQ, cy + first_y_of(j) + r, -1)
    pick_y = (wanted == iota((GY * ROWS, PC), 1)).astype(f32).astype(bf16)
    lane = iota((1, 2 * CELLS), 1)
    for f in range(F):
        i = (lane >> 7) * F + (((lane >> 5) - f) & 3)
        p = cx - base + first_x_of(i) + (lane & (WP - 1))
        pick_ref[f] = (iota((PROW, 2 * CELLS), 0) == p).astype(f32).astype(bf16)
    wait(1)
    wait(2)
    owner = owner_ref[...]
    rank = rank_of(column_of(owner), owner, iota((NB, NB), 1))
    named = iota((DEV, NB), 0) == owner
    slots = jnp.zeros((DEV, CELLS), f32)
    for s in range(CAP):
        value = jnp.sum(jnp.where(named & (rank == s), place_ref[...] + 1, 0).astype(f32), axis=1, keepdims=True) - 1.0
        slots = jnp.where(iota((DEV, CELLS), 1) == s, value, slots)
    wait(4)
    wide_ref[...] = jnp.zeros_like(wide_ref)
    for f in range(F):
        wide_ref[f, :, :TY] = s_ref[f]
    strips(wide_ref, low_ref, high_ref, top_ref, bottom_ref)
    corners = corner_rows(wide_ref)
    for k, step in enumerate(CORNERS):
        other, there = neighbour(step)
        slots = slots + jnp.where(iota((DEV, CELLS), 0) == jnp.where(there, other, -1), corners[k : k + 1, :], 0.0)
    wait(3)
    parts = [parent_ref[f, pl.ds(base, PROW), :] for f in range(F)]
    windows = [dot(dot_nt(pick_y, parts[f]).astype(bf16), pick_ref[f]) for f in range(F)]
    j16 = iota((GY, PC), 0)
    q = iota((GY, PC), 1) - (cy + first_y_of(j16))
    inside = (q >= 0) & (q < WQ)
    lanes = iota((GY, CELLS), 1) >> 5
    erow = iota((8, PROW), 0)
    target = jnp.full((8, PROW), -1, i32)
    for k, i in enumerate(LEFT):
        target = jnp.where(erow == k, cx - base + first_x(i) + WP, target)
    pick_row = (target == iota((8, PROW), 1)).astype(f32).astype(bf16)
    left = [jnp.zeros((GY, CELLS), f32) for _ in LEFT]
    for f in range(F):
        rows = dot(pick_row, parts[f])
        for k in range(len(LEFT)):
            kept = jnp.where(inside, rows[k : k + 1, :], 0.0)
            folded = kept[:, :128] + kept[:, 128:256] + kept[:, 256:]
            folded = folded + pltpu.roll(folded, 64, 1)
            folded = folded + pltpu.roll(folded, 32, 1)
            left[k] = jnp.where(lanes == f, folded, left[k])
    copies = []
    size = 2 * GY * ROWS
    quarter = iota((GY * ROWS, CELLS), 1) >> 5
    for pair in range(GX // 2):
        for i in (2 * pair, 2 * pair + 1):
            tile = slice(i // F * CELLS, i // F * CELLS + CELLS)
            message = windows[0][:, tile]
            for f in range(1, F):
                message = jnp.where(quarter == (f + i) % F, windows[f][:, tile], message)
            z_ref[pl.ds(i * GY * ROWS, GY * ROWS), :] = message
            if i in LEFT:
                z_ref[pl.ds(i * GY * ROWS + WQ, GY, stride=ROWS), :] = left[LEFT.index(i)]
        z_ref[pl.ds(pair * size + ROWS - 1, 2 * GY, stride=ROWS), :] = slots[2 * GY * pair : 2 * GY * (pair + 1)]
        copies.append(write(z_ref, out_ref, out_any, sems.at[pair], pl.ds(pair * size, size)))
    for copy in copies:
        copy.wait()


def write(z_ref, out_ref, out_any, sem, at):
    out_ref[at, :] = z_ref[at, :].astype(bf16)
    copy = pltpu.make_async_copy(out_ref.at[at, :], out_any.at[at, :], sem)
    copy.start()
    return copy


def hat(fine, anchor, coarse):
    centre = (fine.astype(f32) + 0.5) * (2.0 / 13.0) - 0.5 + anchor.astype(f32)
    return jnp.maximum(0.0, 1.0 - jnp.abs(centre - coarse.astype(f32)))


FOLD = TX // (CELLS // (F * HALO))


def strips(wide_ref, low_ref, high_ref, top_ref, bottom_ref):
    field = iota((TX, CELLS), 1) >> 2
    low, high = jnp.zeros((TX, CELLS), f32), jnp.zeros((TX, CELLS), f32)
    for f in range(F):
        s = wide_ref[f]
        low = jnp.where(field == f, s if f == 0 else pltpu.roll(s, HALO * f, 1), low)
        high = jnp.where(field == f, pltpu.roll(s, CELLS - TY + HALO + HALO * f, 1), high)
        top_ref[f * HALO : (f + 1) * HALO, :] = pltpu.roll(s[:8], HALO, 1)[:HALO]
        bottom_ref[f * HALO : (f + 1) * HALO, :] = pltpu.roll(s[TX - 8 :], HALO, 1)[HALO:]
    for strip, ref in ((low, low_ref), (high, high_ref)):
        packed = strip[:FOLD]
        for g in range(1, TX // FOLD):
            packed = packed + pltpu.roll(strip[g * FOLD : (g + 1) * FOLD], g * F * HALO, 1)
        ref[...] = packed


def unfolded(packed):
    n = F * HALO
    return jnp.concatenate([packed] + [pltpu.roll(packed, CELLS - g * n, 1) for g in range(1, TX // FOLD)], axis=0)


def widened(s, left, right, f):
    lane = iota(s.shape, 1)
    before = left if f == 0 else pltpu.roll(left, CELLS - HALO * f, 1)
    after = pltpu.roll(right, TY + HALO - HALO * f, 1)
    wide = jnp.where(lane < TY + HALO, pltpu.roll(s, HALO, 1), after)
    return jnp.where(lane < HALO, before, jnp.where(lane < TY + 2 * HALO, wide, 0.0))


def corner_of(got_ref, step):
    other, there = neighbour(step)
    rows = got_ref[pl.ds(pl.multiple_of((other >> 2) * GROUP, 16), GROUP), :].astype(f32)
    mine = jnp.where(there, (other & 3) * ROWS + ROWS - 1, -1)
    row = jnp.sum(jnp.where(iota((GROUP, CELLS), 0) == mine, rows, 0.0), axis=0, keepdims=True)
    row = jnp.broadcast_to(row, (8, CELLS))
    return row + pltpu.roll(row, CELLS - CORNER, 1) + pltpu.roll(row, CELLS - 2 * CORNER, 1)


def nest_kernel(
    wait, holder_ref, corner_ref, owner_ref, got_ref, s_ref, left_ref, right_ref, before_ref, after_ref, skin_ref,
    next_any, out_any, wx_ref, wide_ref, next_ref, out_ref, state_ref, force_ref, flux_ref, z_ref, sems,
):
    wide_ref[...] = jnp.zeros_like(wide_ref)
    flux_ref[...] = jnp.zeros_like(flux_ref)
    corners = [corner_of(got_ref, step) for step in CORNERS]
    group = pl.multiple_of((holder_ref[0] >> 2) * GROUP, 16)
    got = got_ref[pl.ds(group, GROUP), :]
    wait(1)
    ix, iy = lax.axis_index("gx"), lax.axis_index("gy")
    cx, cy = corner_ref[0], corner_ref[1]
    x0, y0 = ix * TX - HALO, iy * TY - HALO
    px, qy = cx + first_x_of(ix), cy + first_y_of(iy)
    lane = iota((ROWS_X, CELLS), 1)
    row = iota((ROWS_X, CELLS), 0)
    weight = hat(row + x0, cx, (lane & (WP - 1)) + px)
    for f in range(F):
        wx_ref[f * ROWS_X : (f + 1) * ROWS_X, :] = jnp.where(lane >> 5 == ((f + ix) & 3), weight, 0.0).astype(bf16)
    weight_last = relax_coef / diffuse_coef * hat(row + x0, cx, jnp.full_like(row, WP) + px).astype(bf16).astype(f32)
    inside = (row + x0 >= 0) & (row + x0 < GX * TX) & (lane + y0 >= 0) & (lane + y0 < GY * TY)
    mask = jnp.where(inside, diffuse_coef, 0.0)
    for now in range(2):
        state_ref[:, now, :PAD, :] = jnp.zeros((F, PAD, CELLS), f32)
        state_ref[:, now, PAD + ROWS_X :, :] = jnp.zeros((F, PAD, CELLS), f32)
    at = iota((CELLS, GROUP), 1) - (holder_ref[0] & 3) * ROWS
    weight_y = jnp.where((at >= 0) & (at < WQ), hat(iota((CELLS, GROUP), 0) + y0, cy, at + qy), 0.0).astype(bf16)
    lane = iota((CELLS, CELLS), 1)
    weight_c = hat(iota((CELLS, CELLS), 0) + y0, cy, qy + ((lane - qy) & (WP - 1))).astype(bf16)
    partial = dot(weight_y, got).astype(bf16)
    last = jnp.sum(
        jnp.where(iota((GROUP, CELLS), 0) == (holder_ref[0] & 3) * ROWS + WQ, got.astype(f32), 0.0), axis=0, keepdims=True
    )
    last = jnp.where(iota((8, CELLS), 1) >> 5 == iota((8, CELLS), 0), last, 0.0).astype(bf16)
    partial_last = dot_nt(last, weight_c).astype(bf16).astype(f32)
    force_ref[...] = dot_nt(wx_ref[...], partial)
    wait(2)
    column = column_of(owner_ref[...])
    number, owner = by_thirds(column)
    send = (iota((CAP * DEV, NB), 0) == rank_of(column, owner, number) * DEV + owner).astype(f32).astype(bf16)
    wait(4)
    left, right = unfolded(left_ref[...]), unfolded(right_ref[...])
    lane, sub = iota((8, CELLS), 1), iota((8, CELLS), 0)
    written = []
    for f in range(F):
        force = relax_coef / diffuse_coef * force_ref[f * ROWS_X : (f + 1) * ROWS_X, :] + weight_last * partial_last[f : f + 1, :]
        wide_ref[f, :, :TY] = s_ref[f]
        state_ref[f, 0, PAD : PAD + HALO, :] = before_ref[f * HALO : (f + 1) * HALO, :]
        state_ref[f, 0, PAD + HALO : PAD + HALO + TX, :] = widened(wide_ref[f], left, right, f)
        state_ref[f, 0, PAD + HALO + TX : PAD + ROWS_X, :] = after_ref[f * HALO : (f + 1) * HALO, :]
        for side, base in ((-1, PAD), (1, PAD + ROWS_X - 8)):
            tile = state_ref[f, 0, base : base + 8, :]
            for k, (dx, dy) in enumerate(CORNERS):
                for r in range(EDGE if dx == side else 0):
                    row = HALO - EDGE + r if dx < 0 else 8 - HALO + r
                    column = HALO - EDGE if dy < 0 else HALO + TY
                    at = FREE + (f * EDGE + r) * EDGE
                    moved = pltpu.roll(corners[k], (column - at) % CELLS, 1)
                    tile = jnp.where((sub == row) & (lane >= column) & (lane < column + EDGE), moved, tile)
            state_ref[f, 0, base : base + 8, :] = tile
        s = state_ref[f, 0, PAD : PAD + ROWS_X, :]
        for step in range(STEPS):
            now = step % 2
            beside = state_ref[f, now, PAD - 1 : PAD - 1 + ROWS_X, :] + state_ref[f, now, PAD + 1 : PAD + 1 + ROWS_X, :]
            beside = beside + (pltpu.roll(s, 1, 1) + pltpu.roll(s, CELLS - 1, 1))
            s = mask * ((1.0 - 4.0 * diffuse_coef - relax_coef) / diffuse_coef * s + beside + force)
            state_ref[f, 1 - now, PAD : PAD + ROWS_X, :] = s if step < STEPS - 1 else pltpu.roll(s, CELLS - HALO, 1)
        last_state = state_ref.at[f, STEPS % 2]
        next_ref[f] = last_state[PAD + HALO : PAD + HALO + TX, :TY]
    u, v, ta, qa = next_ref[0], next_ref[1], next_ref[2], next_ref[3]
    half = drag_coefficient * jnp.sqrt(1.0 + u * u + v * v)
    written.append(pltpu.make_async_copy(next_ref, next_any, sems.at[4]))
    written[0].start()
    wait(9)
    skin = skin_ref[...]
    flux = (half * (ta - skin), half * (qa - 0.5 * skin), half * u, half * v)
    rows = NB // CAP
    lane = iota((rows, CELLS), 1)
    blocks = []
    for f in range(F):
        flux_ref[f, :, :TY] = flux[f]
        m = [flux_ref[f, pl.ds(k, rows, stride=4), :] for k in range(4)]
        r1, r2, r3 = pltpu.roll(m[1], 96, 1), pltpu.roll(m[2], 64, 1), pltpu.roll(m[3], 32, 1)
        blocks.append(
            jnp.concatenate(
                [jnp.where(lane < 96, m[0], r1), jnp.where(lane < 64, r1, r2), jnp.where(lane < 32, r2, r3)], axis=0
            ).astype(bf16)
        )
    sent = dot(send, jnp.concatenate(blocks, axis=1))
    part = DEV // 4
    for c in range(4):
        for slot in range(CAP):
            for f in range(F):
                z_ref[pl.ds(c * part * CAP * F + slot * F + f, part, stride=CAP * F), :] = sent[
                    slot * DEV + c * part : slot * DEV + (c + 1) * part, f * CELLS : (f + 1) * CELLS
                ]
        written.append(write(z_ref, out_ref, out_any, sems.at[c], pl.ds(c * part * CAP * F, part * CAP * F)))
    for copy in written:
        copy.wait()


def hot_kernel(
    got_ref, kept_ref, owner_ref, hot_ref, give_ref, inverse_ref, cover_ref, back_ref, z_ref, slot_ref, row_ref
):
    column = column_of(owner_ref[...])
    number, owner = by_thirds(column)
    source = column_of(owner * CAP + rank_of(column, owner, number))
    back_ref[...] = (source == iota((NB, CAP * DEV), 1)).astype(f32).astype(bf16)
    slot_ref[...] = got_ref[...].astype(f32)
    slots = slot_ref[pl.ds(ROWS - 1, DEV, stride=ROWS), :].astype(i32)
    lane = iota((DEV, OCEAN * F), 1)
    for s in range(CAP):
        target = slots[:, s : s + 1] * F
        for f in range(F):
            z_ref[pl.ds(s * F + f, DEV, stride=CAP * F), :] = (lane == jnp.where(target < 0, -1, target + f)).astype(f32)
        row_ref[pl.ds(s, DEV, stride=CAP), :] = (lane == target).astype(f32)
    give_ref[...] = row_ref[...].astype(bf16)
    hot = jnp.swapaxes(z_ref[...], 0, 1)
    hot_ref[...] = hot.astype(bf16)
    count = jnp.sum(hot, axis=1, keepdims=True)
    inverse_ref[...] = jnp.broadcast_to(1.0 / jnp.maximum(count, 1.0), (OCEAN * F, CELLS))
    cover_ref[...] = jnp.where(count == 0.0, kept_ref[...], 0.0)


def top_kernel(scale_ref, marine_ref, out_ref):
    total = scale_ref[0, 0] * marine_ref[0]
    for k in range(1, marine_ref.shape[0]):
        total = total + scale_ref[0, k] * marine_ref[k]
    out_ref[: OCEAN * F, :] = total
    out_ref[OCEAN * F :, :] = jnp.full((8, CELLS), scale_ref[0, 0], f32)


def ocean_kernel(wait, got_ref, hot_ref, inverse_ref, cover_ref, top_ref, give_ref, forcing_ref, out_ref):
    wait(1)
    wait(0)
    sums = dot(hot_ref[...], got_ref[...])
    for k in (2, 3, 4, 5):
        wait(k)
    forcing = sums * inverse_ref[...] + cover_ref[...]
    forcing_ref[...] = forcing
    top = top_ref[: OCEAN * F, :] + top_ref[OCEAN * F : OCEAN * F + 1, :] * forcing
    back = dot(give_ref[...], jnp.concatenate(split3(top), axis=1))
    out_ref[...] = back[:, :CELLS] + back[:, CELLS : 2 * CELLS] + back[:, 2 * CELLS :]

def mix_kernel(scale_ref, forcing_ref, marine_ref, out_ref, high_ref, low_ref):
    layers = marine_ref.shape[0]
    n = 8 * layers

    @pl.when(pl.program_id(0) == 0)
    def _():
        spread = (iota((n, layers), 0) >> 3 == iota((n, layers), 1)).astype(f32).astype(bf16)
        same = (iota((n, n), 0) & 7) == (iota((n, n), 1) & 7)
        scale = scale_ref[...]
        high = scale.astype(bf16)
        low = (scale - high.astype(f32)).astype(bf16)
        for part, ref in ((high, high_ref), (low, low_ref)):
            wide = dot_nt(dot(spread, part).astype(bf16), spread)
            ref[...] = jnp.where(same, wide, 0.0).astype(bf16)

    groups = marine_ref.shape[1] // 8
    columns = []
    for g in range(groups):
        x = marine_ref[:, 8 * g : 8 * g + 8, :].reshape(n, CELLS)
        first = x[:8] + forcing_ref[8 * g : 8 * g + 8, :]
        columns.append(jnp.concatenate([first, x[8:]], axis=0))
    x = jnp.concatenate(columns, axis=1)
    high = x.astype(bf16)
    low = (x - high.astype(f32)).astype(bf16)
    y = dot(high_ref[...], high) + (dot(high_ref[...], low) + dot(low_ref[...], high))
    for g in range(groups):
        out_ref[:, 8 * g : 8 * g + 8, :] = y[:, g * CELLS : (g + 1) * CELLS].reshape(layers, 8, CELLS)


def skin_kernel(got_ref, back_ref, out_ref, tile_ref):
    x = dot(back_ref[...], jnp.concatenate(split3(got_ref[...]), axis=1))
    x = x[:, :CELLS] + x[:, CELLS : 2 * CELLS] + x[:, 2 * CELLS :]
    rows = NB // CAP
    t0, t1, t2 = x[:rows], x[rows : 2 * rows], x[2 * rows :]
    lane = iota((rows, CELLS), 1)
    tile_ref[pl.ds(0, rows, stride=4), :] = t0
    tile_ref[pl.ds(1, rows, stride=4), :] = pltpu.roll(jnp.where(lane < 64, t1, t0), 32, 1)
    tile_ref[pl.ds(2, rows, stride=4), :] = pltpu.roll(jnp.where(lane < 32, t2, t1), 64, 1)
    tile_ref[pl.ds(3, rows, stride=4), :] = pltpu.roll(t2, 96, 1)
    out_ref[...] = tile_ref[:, :TY]


MEMORY = {"h": pltpu.HBM, "v": pltpu.VMEM, "H": pltpu.HBM, "S": pltpu.HBM}
SPACES = {"h": pltpu.HBM, "v": pltpu.VMEM, "H": pltpu.HBM, "S": pltpu.HBM, "p": pltpu.VMEM, "s": pltpu.SMEM}


def call(kernel, ins, outs, args, shapes, scratch=(), copies=0, lazy=False):
    args = [pltpu.with_memory_space_constraint(a, MEMORY[c]) if c in MEMORY else a for c, a in zip(ins, args)]
    letters = ins + outs
    kinds = [(a.shape, a.dtype) for a in args] + list(shapes)
    moved = [k for k, c in enumerate(letters) if c in "HS"]
    own = len(scratch) + (1 if copies else 0)

    def body(*refs):
        arrays, rest = list(refs[: len(letters)]), refs[len(letters) :]
        sems = rest[-1]
        far = [arrays[k] for k in moved]
        for n, k in enumerate(moved):
            arrays[k] = rest[own + n]
        pending = {k: pltpu.make_async_copy(far[n], arrays[k], sems.at[n]) for n, k in enumerate(moved) if k < len(ins)}
        for copy in pending.values():
            copy.start()
        if lazy:
            kernel(lambda k: pending[k].wait(), *arrays, *rest[:own])
        else:
            for copy in pending.values():
                copy.wait()
            kernel(*arrays, *rest[:own])
        done = [pltpu.make_async_copy(arrays[k], far[n], sems.at[n]) for n, k in enumerate(moved) if k >= len(ins)]
        for copy in done:
            copy.start()
        for copy in done:
            copy.wait()

    return pl.pallas_call(
        body,
        out_shape=tuple(MEMORY[c](s, d) if c in MEMORY else jax.ShapeDtypeStruct(s, d) for c, (s, d) in zip(outs, shapes)),
        in_specs=[pl.BlockSpec(memory_space=SPACES[c]) for c in ins],
        out_specs=tuple(pl.BlockSpec(memory_space=SPACES[c]) for c in outs),
        scratch_shapes=[pltpu.VMEM(s, d) for s, d in scratch]
        + ([pltpu.SemaphoreType.DMA((copies,))] if copies else [])
        + [(pltpu.SMEM if letters[k] == "S" else pltpu.VMEM)(*kinds[k]) for k in moved]
        + [pltpu.SemaphoreType.DMA((max(1, len(moved)),))],
        compiler_params=pltpu.CompilerParams(vmem_limit_bytes=32 << 20),
    )(*args)


def shift(value, axis, by):
    n = lax.axis_size(axis)
    return lax.ppermute(value, axis, [(i, i + by) for i in range(n) if 0 <= i + by < n])


def exchange(value, rows):
    split = value.reshape(rows)
    return lax.all_to_all(split, ("gx", "gy"), split_axis=0, concat_axis=0, tiled=True).reshape(value.shape)


def by_block(value):
    return value.reshape(F, OCEAN, CELLS).transpose(1, 0, 2).reshape(OCEAN * F, CELLS)


def on_device(
    fine_atmospheric_values,
    fine_skin_heat,
    coarse_lowest_values,
    holder_flat,
    corner_offset,
    exchange_patch_holder,
    holder_patch_position,
    coarse_interface_exchange,
    marine_stratum_values,
    diffusion_solver_operator,
):
    owner = exchange_patch_holder.reshape(1, NB)
    place = holder_patch_position.reshape(1, NB)
    names, message, tile, strip = ((1, NB), i32), ((DEV * ROWS, CELLS), bf16), ((F, TX, TY), f32), ((TX, CELLS), f32)
    ends, fold, whole = ((F * HALO, CELLS), f32), ((FOLD, CELLS), f32), ((F, TX, CELLS), f32)
    windows, low, high, top, bottom = call(
        pack_kernel, "SHHHH", "hvvvv", (corner_offset, owner, place, coarse_lowest_values, fine_atmospheric_values),
        (message, fold, fold, ends, ends),
        (whole, ((F, PROW, 2 * CELLS), bf16), ((DEV * ROWS, CELLS), f32), message), 4, True,
    )
    got = exchange(windows, (DEV, ROWS // 4, 4, CELLS))
    left, right = shift(high, "gy", 1), shift(low, "gy", -1)
    before, after = shift(bottom, "gx", 1), shift(top, "gx", -1)
    holder, _ = lax.optimization_barrier((holder_flat, windows))
    holder = jnp.minimum(holder, DEV - 1)
    sent, strips = ((DEV * CAP * F, CELLS), bf16), ((F, TX, CELLS), f32)
    nest_next, flux = call(
        nest_kernel, "sSHvHvvvvH", "hh",
        (holder, corner_offset, owner, got, fine_atmospheric_values, left, right, before, after, fine_skin_heat), (tile, sent),
        (
            ((F * ROWS_X, CELLS), bf16), strips, tile, sent, ((F, 2, ROWS_X + 2 * PAD, CELLS), f32),
            ((F * ROWS_X, CELLS), f32), strips, ((DEV * CAP * F, CELLS), f32),
        ), 5, True,
    )
    got_flux = exchange(flux, (DEV, CAP, F, CELLS))
    layers = marine_stratum_values.shape[1]
    marine = marine_stratum_values.reshape(F, layers, OCEAN, CELLS).transpose(1, 2, 0, 3).reshape(layers, OCEAN * F, CELLS)
    marine_late, got_late, flux = lax.optimization_barrier((marine, got, flux))
    block = ((OCEAN * F, CELLS), f32)
    hot, give = ((OCEAN * F, DEV * CAP * F), bf16), ((DEV * CAP, OCEAN * F), bf16)
    hot, give, inverse, cover, back = call(
        hot_kernel, "vHH", "HHHHv", (got_late, by_block(coarse_interface_exchange), owner),
        (hot, give, block, block, ((NB, CAP * DEV), bf16)),
        (((DEV * CAP * F, OCEAN * F), f32), ((DEV * ROWS, CELLS), f32), ((DEV * CAP, OCEAN * F), f32)),
    )
    (layer0,) = call(top_kernel, "Sp", "H", (diffusion_solver_operator, marine_late), (((OCEAN * F + 8, CELLS), f32),))
    returned = ((DEV * CAP, CELLS), f32)
    forcing, skins = call(
        ocean_kernel, "HHHHHH", "HH", (got_flux, hot, inverse, cover, layer0, give), (block, returned),
        lazy=True,
    )
    arrived = exchange(skins, (DEV, 1, CAP * CELLS))
    part = 32
    refreshed = pl.pallas_call(
        mix_kernel,
        out_shape=jax.ShapeDtypeStruct((layers, OCEAN * F, CELLS), f32),
        grid=(OCEAN * F // part,),
        in_specs=[
            pl.BlockSpec((layers, layers), lambda g: (0, 0)),
            pl.BlockSpec((part, CELLS), lambda g: (g, 0)),
            pl.BlockSpec((layers, part, CELLS), lambda g: (0, g, 0)),
        ],
        out_specs=pl.BlockSpec((layers, part, CELLS), lambda g: (0, g, 0)),
        scratch_shapes=[pltpu.VMEM((8 * layers, 8 * layers), bf16)] * 2,
        compiler_params=pltpu.CompilerParams(vmem_limit_bytes=40 << 20),
    )(diffusion_solver_operator, forcing, marine)
    refreshed = refreshed.reshape(layers, OCEAN, F, CELLS).transpose(2, 0, 1, 3).reshape(marine_stratum_values.shape)
    (skin,) = call(skin_kernel, "vv", "p", (arrived, back), (((TX, TY), f32),), (((TX, CELLS), f32),))
    return (nest_next, refreshed, skin)


def solution(mesh):
    in_specs = (
        P(None, "gx", "gy"),
        P("gx", "gy"),
        P(None, "gx", "gy"),
        P(),
        P(),
        P(("gx", "gy"), None),
        P(("gx", "gy")),
        P(None, ("gx", "gy")),
        P(None, None, ("gx", "gy")),
        P(),
    )
    out_specs = (P(None, "gx", "gy"), P(None, None, ("gx", "gy")), P("gx", "gy"))
    return jax.shard_map(
        on_device, mesh=mesh, in_specs=in_specs, out_specs=out_specs, check_vma=False
    )
```

```python
import jax
import jax.numpy as jnp
from jax import lax
from jax.experimental import pallas as pl
from jax.experimental.pallas import tpu as pltpu
from jax.sharding import PartitionSpec as P

F = 4
CELLS = 128
OCEAN = 32
STEPS = 4
TX, TY = 192, 96
GX, GY = 8, 16
DEV = GX * GY
PC = 384
CAP = 3
BACK = 4
NB = 144
HALO = 4
ROWS_X = TX + 2 * HALO
PAD = 8
WP = 32
WQ = 18
ROWS = 20
GROUP = 4 * ROWS
PROW = 256
LEFT = tuple(
    i for i in range(GX) if i < GX - 1 and (4 * (TX * i + TX + 2) - 11) // 26 + 1 - (4 * (TX * i - 3) - 11) // 26 >= WP
)
f32, bf16, i32 = jnp.float32, jnp.bfloat16, jnp.int32

diffuse_coef = 0.24
relax_coef = 0.3
drag_coefficient = 0.5


def iota(shape, dim):
    return lax.broadcasted_iota(i32, shape, dim)


def first_x(i):
    return (4 * (TX * i - 3) - 11) // 26


def first_y(j):
    return (4 * (TY * j - 3) - 11) // 26


def first_y_of(j):
    return ((4 * TY * j + 3) * 2521 >> 16) - 1


def first_x_of(i):
    return ((4 * TX * i + 3) * 2521 >> 16) - 1


def dot(a, b):
    return jnp.dot(a, b, preferred_element_type=f32)


def dot_nt(a, b):
    return lax.dot_general(a, b, (((1,), (1,)), ((), ())), preferred_element_type=f32)


def split3(x):
    high = x.astype(bf16)
    rest = x - high.astype(f32)
    mid = rest.astype(bf16)
    return high, mid, (rest - mid.astype(f32)).astype(bf16)


def column_of(row):
    n = row.shape[1]
    return jnp.sum(jnp.where(iota((n, n), 0) == iota((n, n), 1), row, 0), axis=1, keepdims=True)


def fetch(pairs, sems):
    copies = [pltpu.make_async_copy(src, dst, sems.at[k]) for k, (src, dst) in enumerate(pairs)]
    for copy in copies:
        copy.start()
    return copies


def rank_of(column, row, number):
    return jnp.sum(jnp.where((column == row) & (iota((NB, NB), 0) < number), 1, 0), axis=0, keepdims=True)


def by_thirds(column):
    at = iota((1, NB), 1)
    third = (at >= NB // CAP).astype(i32) + (at >= 2 * (NB // CAP)).astype(i32)
    number = CAP * (at - third * (NB // CAP)) + third
    return number, jnp.sum(jnp.where(iota((NB, NB), 0) == number, column, 0), axis=0, keepdims=True)


PARTS = 3
EDGE = 3
CORNER = F * EDGE * EDGE
FREE = 16
CORNERS = ((-1, -1), (-1, 1), (1, -1), (1, 1))


def neighbour(step):
    x, y = lax.axis_index("gx") + step[0], lax.axis_index("gy") + step[1]
    there = (x >= 0) & (x < GX) & (y >= 0) & (y < GY)
    return jnp.where(there, x * GY + y, 0), there


def corner_rows(wide_ref):
    lane, sub = iota((8, CELLS), 1), iota((8, CELLS), 0)
    out = jnp.zeros((8, CELLS), f32)
    for f in range(F):
        for k, (dx, dy) in enumerate(CORNERS):
            for r in range(EDGE):
                row = r if dx < 0 else TX - EDGE + r
                column = 0 if dy < 0 else TY - EDGE
                at = FREE + (f * EDGE + r) * EDGE
                moved = pltpu.roll(jnp.broadcast_to(wide_ref[f, row : row + 1, :], (8, CELLS)), (at - column) % CELLS, 1)
                out = jnp.where((sub == k) & (lane >= at) & (lane < at + EDGE), moved, out)
    high, mid, low = (x.astype(f32) for x in split3(out))
    return high + pltpu.roll(mid, CORNER, 1) + pltpu.roll(low, 2 * CORNER, 1)


def pack_kernel(
    wait, corner_ref, owner_ref, place_ref, parent_ref, s_ref, out_any, low_ref, high_ref, top_ref, bottom_ref,
    wide_ref, pick_ref, z_ref, out_ref, sems,
):
    wait(0)
    cx, cy = corner_ref[0], corner_ref[1]
    base = pl.multiple_of(jnp.minimum(jnp.maximum(cx - 1, 0) // 16 * 16, PC - PROW), 16)
    row = iota((GY * ROWS, 1), 0)
    j = row * 3277 >> 16
    r = row - j * ROWS
    wanted = jnp.where(r < WQ, cy + first_y_of(j) + r, -1)
    pick_y = (wanted == iota((GY * ROWS, PC), 1)).astype(f32).astype(bf16)
    lane = iota((1, 2 * CELLS), 1)
    for f in range(F):
        i = (lane >> 7) * F + (((lane >> 5) - f) & 3)
        p = cx - base + first_x_of(i) + (lane & (WP - 1))
        pick_ref[f] = (iota((PROW, 2 * CELLS), 0) == p).astype(f32).astype(bf16)
    wait(1)
    wait(2)
    owner = owner_ref[...]
    rank = rank_of(column_of(owner), owner, iota((NB, NB), 1))
    named = iota((DEV, NB), 0) == owner
    slots = jnp.zeros((DEV, CELLS), f32)
    for s in range(CAP):
        value = jnp.sum(jnp.where(named & (rank == s), place_ref[...] + 1, 0).astype(f32), axis=1, keepdims=True) - 1.0
        slots = jnp.where(iota((DEV, CELLS), 1) == s, value, slots)
    wait(4)
    wide_ref[...] = jnp.zeros_like(wide_ref)
    for f in range(F):
        wide_ref[f, :, :TY] = s_ref[f]
    corners = corner_rows(wide_ref)
    for k, step in enumerate(CORNERS):
        other, there = neighbour(step)
        slots = slots + jnp.where(iota((DEV, CELLS), 0) == jnp.where(there, other, -1), corners[k : k + 1, :], 0.0)
    wait(3)
    parts = [parent_ref[f, pl.ds(base, PROW), :] for f in range(F)]
    windows = [dot(dot_nt(pick_y, parts[f]).astype(bf16), pick_ref[f]) for f in range(F)]
    j16 = iota((GY, PC), 0)
    q = iota((GY, PC), 1) - (cy + first_y_of(j16))
    inside = (q >= 0) & (q < WQ)
    lanes = iota((GY, CELLS), 1) >> 5
    erow = iota((8, PROW), 0)
    target = jnp.full((8, PROW), -1, i32)
    for k, i in enumerate(LEFT):
        target = jnp.where(erow == k, cx - base + first_x(i) + WP, target)
    pick_row = (target == iota((8, PROW), 1)).astype(f32).astype(bf16)
    left = [jnp.zeros((GY, CELLS), f32) for _ in LEFT]
    for f in range(F):
        rows = dot(pick_row, parts[f])
        for k in range(len(LEFT)):
            kept = jnp.where(inside, rows[k : k + 1, :], 0.0)
            folded = kept[:, :128] + kept[:, 128:256] + kept[:, 256:]
            folded = folded + pltpu.roll(folded, 64, 1)
            folded = folded + pltpu.roll(folded, 32, 1)
            left[k] = jnp.where(lanes == f, folded, left[k])
    copies = []
    size = 2 * GY * ROWS
    quarter = iota((GY * ROWS, CELLS), 1) >> 5
    for pair in range(GX // 2):
        for i in (2 * pair, 2 * pair + 1):
            tile = slice(i // F * CELLS, i // F * CELLS + CELLS)
            message = windows[0][:, tile]
            for f in range(1, F):
                message = jnp.where(quarter == (f + i) % F, windows[f][:, tile], message)
            z_ref[pl.ds(i * GY * ROWS, GY * ROWS), :] = message
            if i in LEFT:
                z_ref[pl.ds(i * GY * ROWS + WQ, GY, stride=ROWS), :] = left[LEFT.index(i)]
        z_ref[pl.ds(pair * size + ROWS - 1, 2 * GY, stride=ROWS), :] = slots[2 * GY * pair : 2 * GY * (pair + 1)]
        copies.append(write(z_ref, out_ref, out_any, sems.at[pair], pl.ds(pair * size, size)))
    strips(wide_ref, low_ref, high_ref, top_ref, bottom_ref)
    for copy in copies:
        copy.wait()


def write(z_ref, out_ref, out_any, sem, at):
    out_ref[at, :] = z_ref[at, :].astype(bf16)
    copy = pltpu.make_async_copy(out_ref.at[at, :], out_any.at[at, :], sem)
    copy.start()
    return copy


def hat(fine, anchor, coarse):
    centre = (fine.astype(f32) + 0.5) * (2.0 / 13.0) - 0.5 + anchor.astype(f32)
    return jnp.maximum(0.0, 1.0 - jnp.abs(centre - coarse.astype(f32)))


FOLD = TX // (CELLS // (F * HALO))


def strips(wide_ref, low_ref, high_ref, top_ref, bottom_ref):
    field = iota((TX, CELLS), 1) >> 2
    low, high = jnp.zeros((TX, CELLS), f32), jnp.zeros((TX, CELLS), f32)
    for f in range(F):
        s = wide_ref[f]
        low = jnp.where(field == f, s if f == 0 else pltpu.roll(s, HALO * f, 1), low)
        high = jnp.where(field == f, pltpu.roll(s, CELLS - TY + HALO + HALO * f, 1), high)
        top_ref[f * HALO : (f + 1) * HALO, :] = pltpu.roll(s[:8], HALO, 1)[:HALO]
        bottom_ref[f * HALO : (f + 1) * HALO, :] = pltpu.roll(s[TX - 8 :], HALO, 1)[HALO:]
    for strip, ref in ((low, low_ref), (high, high_ref)):
        packed = strip[:FOLD]
        for g in range(1, TX // FOLD):
            packed = packed + pltpu.roll(strip[g * FOLD : (g + 1) * FOLD], g * F * HALO, 1)
        ref[...] = packed


def unfolded(packed):
    n = F * HALO
    return jnp.concatenate([packed] + [pltpu.roll(packed, CELLS - g * n, 1) for g in range(1, TX // FOLD)], axis=0)


def widened(s, left, right, f):
    lane = iota(s.shape, 1)
    before = left if f == 0 else pltpu.roll(left, CELLS - HALO * f, 1)
    after = pltpu.roll(right, TY + HALO - HALO * f, 1)
    wide = jnp.where(lane < TY + HALO, pltpu.roll(s, HALO, 1), after)
    return jnp.where(lane < HALO, before, jnp.where(lane < TY + 2 * HALO, wide, 0.0))


def corner_of(got_ref, step):
    other, there = neighbour(step)
    rows = got_ref[pl.ds(pl.multiple_of((other >> 2) * GROUP, 16), GROUP), :].astype(f32)
    mine = jnp.where(there, (other & 3) * ROWS + ROWS - 1, -1)
    row = jnp.sum(jnp.where(iota((GROUP, CELLS), 0) == mine, rows, 0.0), axis=0, keepdims=True)
    row = jnp.broadcast_to(row, (8, CELLS))
    return row + pltpu.roll(row, CELLS - CORNER, 1) + pltpu.roll(row, CELLS - 2 * CORNER, 1)


def nest_kernel(
    wait, holder_ref, corner_ref, owner_ref, got_ref, s_ref, left_ref, right_ref, before_ref, after_ref, skin_ref,
    next_any, out_any, wx_ref, wide_ref, next_ref, out_ref, state_ref, force_ref, flux_ref, z_ref, sems,
):
    wide_ref[...] = jnp.zeros_like(wide_ref)
    flux_ref[...] = jnp.zeros_like(flux_ref)
    corners = [corner_of(got_ref, step) for step in CORNERS]
    group = pl.multiple_of((holder_ref[0] >> 2) * GROUP, 16)
    got = got_ref[pl.ds(group, GROUP), :]
    wait(1)
    ix, iy = lax.axis_index("gx"), lax.axis_index("gy")
    cx, cy = corner_ref[0], corner_ref[1]
    x0, y0 = ix * TX - HALO, iy * TY - HALO
    px, qy = cx + first_x_of(ix), cy + first_y_of(iy)
    lane = iota((ROWS_X, CELLS), 1)
    row = iota((ROWS_X, CELLS), 0)
    weight = hat(row + x0, cx, (lane & (WP - 1)) + px)
    for f in range(F):
        wx_ref[f * ROWS_X : (f + 1) * ROWS_X, :] = jnp.where(lane >> 5 == ((f + ix) & 3), weight, 0.0).astype(bf16)
    weight_last = relax_coef / diffuse_coef * hat(row + x0, cx, jnp.full_like(row, WP) + px).astype(bf16).astype(f32)
    inside = (row + x0 >= 0) & (row + x0 < GX * TX) & (lane + y0 >= 0) & (lane + y0 < GY * TY)
    mask = jnp.where(inside, diffuse_coef, 0.0)
    for now in range(2):
        state_ref[:, now, :PAD, :] = jnp.zeros((F, PAD, CELLS), f32)
        state_ref[:, now, PAD + ROWS_X :, :] = jnp.zeros((F, PAD, CELLS), f32)
    at = iota((CELLS, GROUP), 1) - (holder_ref[0] & 3) * ROWS
    weight_y = jnp.where((at >= 0) & (at < WQ), hat(iota((CELLS, GROUP), 0) + y0, cy, at + qy), 0.0).astype(bf16)
    lane = iota((CELLS, CELLS), 1)
    weight_c = hat(iota((CELLS, CELLS), 0) + y0, cy, qy + ((lane - qy) & (WP - 1))).astype(bf16)
    partial = dot(weight_y, got).astype(bf16)
    last = jnp.sum(
        jnp.where(iota((GROUP, CELLS), 0) == (holder_ref[0] & 3) * ROWS + WQ, got.astype(f32), 0.0), axis=0, keepdims=True
    )
    last = jnp.where(iota((8, CELLS), 1) >> 5 == iota((8, CELLS), 0), last, 0.0).astype(bf16)
    partial_last = dot_nt(last, weight_c).astype(bf16).astype(f32)
    force_ref[...] = dot_nt(wx_ref[...], partial)
    wait(2)
    column = column_of(owner_ref[...])
    number, owner = by_thirds(column)
    send = (iota((CAP * DEV, NB), 0) == rank_of(column, owner, number) * DEV + owner).astype(f32).astype(bf16)
    wait(4)
    left, right = unfolded(left_ref[...]), unfolded(right_ref[...])
    lane, sub = iota((8, CELLS), 1), iota((8, CELLS), 0)
    written = []
    for f in range(F):
        force = relax_coef / diffuse_coef * force_ref[f * ROWS_X : (f + 1) * ROWS_X, :] + weight_last * partial_last[f : f + 1, :]
        wide_ref[f, :, :TY] = s_ref[f]
        state_ref[f, 0, PAD : PAD + HALO, :] = before_ref[f * HALO : (f + 1) * HALO, :]
        state_ref[f, 0, PAD + HALO : PAD + HALO + TX, :] = widened(wide_ref[f], left, right, f)
        state_ref[f, 0, PAD + HALO + TX : PAD + ROWS_X, :] = after_ref[f * HALO : (f + 1) * HALO, :]
        for side, base in ((-1, PAD), (1, PAD + ROWS_X - 8)):
            tile = state_ref[f, 0, base : base + 8, :]
            for k, (dx, dy) in enumerate(CORNERS):
                for r in range(EDGE if dx == side else 0):
                    row = HALO - EDGE + r if dx < 0 else 8 - HALO + r
                    column = HALO - EDGE if dy < 0 else HALO + TY
                    at = FREE + (f * EDGE + r) * EDGE
                    moved = pltpu.roll(corners[k], (column - at) % CELLS, 1)
                    tile = jnp.where((sub == row) & (lane >= column) & (lane < column + EDGE), moved, tile)
            state_ref[f, 0, base : base + 8, :] = tile
        s = state_ref[f, 0, PAD : PAD + ROWS_X, :]
        for step in range(STEPS):
            now = step % 2
            beside = state_ref[f, now, PAD - 1 : PAD - 1 + ROWS_X, :] + state_ref[f, now, PAD + 1 : PAD + 1 + ROWS_X, :]
            beside = beside + (pltpu.roll(s, 1, 1) + pltpu.roll(s, CELLS - 1, 1))
            s = mask * ((1.0 - 4.0 * diffuse_coef - relax_coef) / diffuse_coef * s + beside + force)
            state_ref[f, 1 - now, PAD : PAD + ROWS_X, :] = s if step < STEPS - 1 else pltpu.roll(s, CELLS - HALO, 1)
        last_state = state_ref.at[f, STEPS % 2]
        next_ref[f] = last_state[PAD + HALO : PAD + HALO + TX, :TY]
    u, v, ta, qa = next_ref[0], next_ref[1], next_ref[2], next_ref[3]
    half = drag_coefficient * jnp.sqrt(1.0 + u * u + v * v)
    written.append(pltpu.make_async_copy(next_ref, next_any, sems.at[4]))
    written[0].start()
    wait(9)
    skin = skin_ref[...]
    flux = (half * (ta - skin), half * (qa - 0.5 * skin), half * u, half * v)
    rows = NB // CAP
    lane = iota((rows, CELLS), 1)
    blocks = []
    for f in range(F):
        flux_ref[f, :, :TY] = flux[f]
        m = [flux_ref[f, pl.ds(k, rows, stride=4), :] for k in range(4)]
        r1, r2, r3 = pltpu.roll(m[1], 96, 1), pltpu.roll(m[2], 64, 1), pltpu.roll(m[3], 32, 1)
        blocks.append(
            jnp.concatenate(
                [jnp.where(lane < 96, m[0], r1), jnp.where(lane < 64, r1, r2), jnp.where(lane < 32, r2, r3)], axis=0
            ).astype(bf16)
        )
    sent = dot(send, jnp.concatenate(blocks, axis=1))
    part = DEV // 4
    for c in range(4):
        for slot in range(CAP):
            for f in range(F):
                z_ref[pl.ds(c * part * CAP * F + slot * F + f, part, stride=CAP * F), :] = sent[
                    slot * DEV + c * part : slot * DEV + (c + 1) * part, f * CELLS : (f + 1) * CELLS
                ]
        written.append(write(z_ref, out_ref, out_any, sems.at[c], pl.ds(c * part * CAP * F, part * CAP * F)))
    for copy in written:
        copy.wait()


def hot_kernel(
    got_ref, kept_ref, owner_ref, hot_ref, give_ref, inverse_ref, cover_ref, back_ref, z_ref, slot_ref, row_ref
):
    column = column_of(owner_ref[...])
    number, owner = by_thirds(column)
    source = column_of(owner * BACK + rank_of(column, owner, number))
    back_ref[...] = (source == iota((NB, BACK * DEV), 1)).astype(f32).astype(bf16)
    slot_ref[...] = got_ref[...].astype(f32)
    slots = slot_ref[pl.ds(ROWS - 1, DEV, stride=ROWS), :].astype(i32)
    lane = iota((DEV, OCEAN * F), 1)
    row_ref[...] = jnp.zeros_like(row_ref)
    for s in range(CAP):
        target = slots[:, s : s + 1] * F
        for f in range(F):
            z_ref[pl.ds(s * F + f, DEV, stride=CAP * F), :] = (lane == jnp.where(target < 0, -1, target + f)).astype(f32)
        row_ref[pl.ds(s, DEV, stride=BACK), :] = (lane == target).astype(f32)
    give_ref[...] = row_ref[...].astype(bf16)
    hot = jnp.swapaxes(z_ref[...], 0, 1)
    hot_ref[...] = hot.astype(bf16)
    count = jnp.sum(hot, axis=1, keepdims=True)
    inverse_ref[...] = jnp.broadcast_to(1.0 / jnp.maximum(count, 1.0), (OCEAN * F, CELLS))
    cover_ref[...] = jnp.where(count == 0.0, kept_ref[...], 0.0)


def top_kernel(scale_ref, marine_ref, out_ref):
    total = scale_ref[0, 0] * marine_ref[0]
    for k in range(1, marine_ref.shape[0]):
        total = total + scale_ref[0, k] * marine_ref[k]
    out_ref[: OCEAN * F, :] = total
    out_ref[OCEAN * F :, :] = jnp.full((8, CELLS), scale_ref[0, 0], f32)


def ocean_kernel(wait, got_ref, hot_ref, inverse_ref, cover_ref, top_ref, give_ref, forcing_ref, out_ref):
    wait(1)
    wait(0)
    sums = dot(hot_ref[...], got_ref[...])
    for k in (2, 3, 4, 5):
        wait(k)
    forcing = sums * inverse_ref[...] + cover_ref[...]
    forcing_ref[...] = forcing
    top = top_ref[: OCEAN * F, :] + top_ref[OCEAN * F : OCEAN * F + 1, :] * forcing
    out_ref[...] = dot(give_ref[...], top.astype(bf16)).astype(bf16)

def mix_kernel(scale_ref, forcing_ref, marine_ref, out_ref, high_ref, low_ref):
    layers = marine_ref.shape[0]
    n = 8 * layers

    @pl.when(pl.program_id(0) == 0)
    def _():
        spread = (iota((n, layers), 0) >> 3 == iota((n, layers), 1)).astype(f32).astype(bf16)
        same = (iota((n, n), 0) & 7) == (iota((n, n), 1) & 7)
        scale = scale_ref[...]
        high = scale.astype(bf16)
        low = (scale - high.astype(f32)).astype(bf16)
        for part, ref in ((high, high_ref), (low, low_ref)):
            wide = dot_nt(dot(spread, part).astype(bf16), spread)
            ref[...] = jnp.where(same, wide, 0.0).astype(bf16)

    groups = marine_ref.shape[1] // 8
    columns = []
    for g in range(groups):
        x = marine_ref[:, 8 * g : 8 * g + 8, :].reshape(n, CELLS)
        first = x[:8] + forcing_ref[8 * g : 8 * g + 8, :]
        columns.append(jnp.concatenate([first, x[8:]], axis=0))
    x = jnp.concatenate(columns, axis=1)
    high = x.astype(bf16)
    low = (x - high.astype(f32)).astype(bf16)
    y = dot(high_ref[...], high) + (dot(high_ref[...], low) + dot(low_ref[...], high))
    for g in range(groups):
        out_ref[:, 8 * g : 8 * g + 8, :] = y[:, g * CELLS : (g + 1) * CELLS].reshape(layers, 8, CELLS)


def skin_kernel(got_ref, back_ref, out_ref, tile_ref):
    x = dot(back_ref[...], got_ref[...])
    rows = NB // CAP
    t0, t1, t2 = x[:rows], x[rows : 2 * rows], x[2 * rows :]
    lane = iota((rows, CELLS), 1)
    tile_ref[pl.ds(0, rows, stride=4), :] = t0
    tile_ref[pl.ds(1, rows, stride=4), :] = pltpu.roll(jnp.where(lane < 64, t1, t0), 32, 1)
    tile_ref[pl.ds(2, rows, stride=4), :] = pltpu.roll(jnp.where(lane < 32, t2, t1), 64, 1)
    tile_ref[pl.ds(3, rows, stride=4), :] = pltpu.roll(t2, 96, 1)
    out_ref[...] = tile_ref[:, :TY]


MEMORY = {"h": pltpu.HBM, "v": pltpu.VMEM, "H": pltpu.HBM, "S": pltpu.HBM}
SPACES = {"h": pltpu.HBM, "v": pltpu.VMEM, "H": pltpu.HBM, "S": pltpu.HBM, "p": pltpu.VMEM, "s": pltpu.SMEM}


def call(kernel, ins, outs, args, shapes, scratch=(), copies=0, lazy=False):
    args = [pltpu.with_memory_space_constraint(a, MEMORY[c]) if c in MEMORY else a for c, a in zip(ins, args)]
    letters = ins + outs
    kinds = [(a.shape, a.dtype) for a in args] + list(shapes)
    moved = [k for k, c in enumerate(letters) if c in "HS"]
    own = len(scratch) + (1 if copies else 0)

    def body(*refs):
        arrays, rest = list(refs[: len(letters)]), refs[len(letters) :]
        sems = rest[-1]
        far = [arrays[k] for k in moved]
        for n, k in enumerate(moved):
            arrays[k] = rest[own + n]
        pending = {k: pltpu.make_async_copy(far[n], arrays[k], sems.at[n]) for n, k in enumerate(moved) if k < len(ins)}
        for copy in pending.values():
            copy.start()
        if lazy:
            kernel(lambda k: pending[k].wait(), *arrays, *rest[:own])
        else:
            for copy in pending.values():
                copy.wait()
            kernel(*arrays, *rest[:own])
        done = [pltpu.make_async_copy(arrays[k], far[n], sems.at[n]) for n, k in enumerate(moved) if k >= len(ins)]
        for copy in done:
            copy.start()
        for copy in done:
            copy.wait()

    return pl.pallas_call(
        body,
        out_shape=tuple(MEMORY[c](s, d) if c in MEMORY else jax.ShapeDtypeStruct(s, d) for c, (s, d) in zip(outs, shapes)),
        in_specs=[pl.BlockSpec(memory_space=SPACES[c]) for c in ins],
        out_specs=tuple(pl.BlockSpec(memory_space=SPACES[c]) for c in outs),
        scratch_shapes=[pltpu.VMEM(s, d) for s, d in scratch]
        + ([pltpu.SemaphoreType.DMA((copies,))] if copies else [])
        + [(pltpu.SMEM if letters[k] == "S" else pltpu.VMEM)(*kinds[k]) for k in moved]
        + [pltpu.SemaphoreType.DMA((max(1, len(moved)),))],
        compiler_params=pltpu.CompilerParams(vmem_limit_bytes=32 << 20),
    )(*args)


def shift(value, axis, by):
    n = lax.axis_size(axis)
    return lax.ppermute(value, axis, [(i, i + by) for i in range(n) if 0 <= i + by < n])


def exchange(value, rows):
    split = value.reshape(rows)
    return lax.all_to_all(split, ("gx", "gy"), split_axis=0, concat_axis=0, tiled=True).reshape(value.shape)


def by_block(value):
    return value.reshape(F, OCEAN, CELLS).transpose(1, 0, 2).reshape(OCEAN * F, CELLS)


def on_device(
    fine_atmospheric_values,
    fine_skin_heat,
    coarse_lowest_values,
    holder_flat,
    corner_offset,
    exchange_patch_holder,
    holder_patch_position,
    coarse_interface_exchange,
    marine_stratum_values,
    diffusion_solver_operator,
):
    owner = exchange_patch_holder.reshape(1, NB)
    place = holder_patch_position.reshape(1, NB)
    names, message, tile, strip = ((1, NB), i32), ((DEV * ROWS, CELLS), bf16), ((F, TX, TY), f32), ((TX, CELLS), f32)
    ends, fold, whole = ((F * HALO, CELLS), f32), ((FOLD, CELLS), f32), ((F, TX, CELLS), f32)
    windows, low, high, top, bottom = call(
        pack_kernel, "SHHHH", "hvvvv", (corner_offset, owner, place, coarse_lowest_values, fine_atmospheric_values),
        (message, fold, fold, ends, ends),
        (whole, ((F, PROW, 2 * CELLS), bf16), ((DEV * ROWS, CELLS), f32), message), 4, True,
    )
    got = exchange(windows, (DEV, ROWS // 4, 4, CELLS))
    left, right = shift(high, "gy", 1), shift(low, "gy", -1)
    before, after = shift(bottom, "gx", 1), shift(top, "gx", -1)
    holder, _ = lax.optimization_barrier((holder_flat, windows))
    holder = jnp.minimum(holder, DEV - 1)
    sent, strips = ((DEV * CAP * F, CELLS), bf16), ((F, TX, CELLS), f32)
    nest_next, flux = call(
        nest_kernel, "sSHvHvvvvH", "hh",
        (holder, corner_offset, owner, got, fine_atmospheric_values, left, right, before, after, fine_skin_heat), (tile, sent),
        (
            ((F * ROWS_X, CELLS), bf16), strips, tile, sent, ((F, 2, ROWS_X + 2 * PAD, CELLS), f32),
            ((F * ROWS_X, CELLS), f32), strips, ((DEV * CAP * F, CELLS), f32),
        ), 5, True,
    )
    got_flux = exchange(flux, (DEV, CAP, F, CELLS))
    layers = marine_stratum_values.shape[1]
    marine = marine_stratum_values.reshape(F, layers, OCEAN, CELLS).transpose(1, 2, 0, 3).reshape(layers, OCEAN * F, CELLS)
    marine_late, got_late, flux = lax.optimization_barrier((marine, got, flux))
    block = ((OCEAN * F, CELLS), f32)
    hot, give = ((OCEAN * F, DEV * CAP * F), bf16), ((DEV * BACK, OCEAN * F), bf16)
    hot, give, inverse, cover, back = call(
        hot_kernel, "vHH", "HHHHv", (got_late, by_block(coarse_interface_exchange), owner),
        (hot, give, block, block, ((NB, BACK * DEV), bf16)),
        (((DEV * CAP * F, OCEAN * F), f32), ((DEV * ROWS, CELLS), f32), ((DEV * BACK, OCEAN * F), f32)),
    )
    (layer0,) = call(top_kernel, "Sp", "H", (diffusion_solver_operator, marine_late), (((OCEAN * F + 8, CELLS), f32),))
    returned = ((DEV * BACK, CELLS), bf16)
    forcing, skins = call(
        ocean_kernel, "HHHHHH", "HH", (got_flux, hot, inverse, cover, layer0, give), (block, returned),
        lazy=True,
    )
    arrived = exchange(skins, (DEV, BACK, CELLS))
    part = 32
    refreshed = pl.pallas_call(
        mix_kernel,
        out_shape=jax.ShapeDtypeStruct((layers, OCEAN * F, CELLS), f32),
        grid=(OCEAN * F // part,),
        in_specs=[
            pl.BlockSpec((layers, layers), lambda g: (0, 0)),
            pl.BlockSpec((part, CELLS), lambda g: (g, 0)),
            pl.BlockSpec((layers, part, CELLS), lambda g: (0, g, 0)),
        ],
        out_specs=pl.BlockSpec((layers, part, CELLS), lambda g: (0, g, 0)),
        scratch_shapes=[pltpu.VMEM((8 * layers, 8 * layers), bf16)] * 2,
        compiler_params=pltpu.CompilerParams(vmem_limit_bytes=40 << 20),
    )(diffusion_solver_operator, forcing, marine)
    refreshed = refreshed.reshape(layers, OCEAN, F, CELLS).transpose(2, 0, 1, 3).reshape(marine_stratum_values.shape)
    (skin,) = call(skin_kernel, "vv", "p", (arrived, back), (((TX, TY), f32),), (((TX, CELLS), f32),))
    return (nest_next, refreshed, skin)


def solution(mesh):
    in_specs = (
        P(None, "gx", "gy"),
        P("gx", "gy"),
        P(None, "gx", "gy"),
        P(),
        P(),
        P(("gx", "gy"), None),
        P(("gx", "gy")),
        P(None, ("gx", "gy")),
        P(None, None, ("gx", "gy")),
        P(),
    )
    out_specs = (P(None, "gx", "gy"), P(None, None, ("gx", "gy")), P("gx", "gy"))
    return jax.shard_map(
        on_device, mesh=mesh, in_specs=in_specs, out_specs=out_specs, check_vma=False
    )
```

```python
import jax
import jax.numpy as jnp
from jax import lax
from jax.experimental import pallas as pl
from jax.experimental.pallas import tpu as pltpu
from jax.sharding import PartitionSpec as P

F = 4
CELLS = 128
OCEAN = 32
STEPS = 4
TX, TY = 192, 96
GX, GY = 8, 16
DEV = GX * GY
PC = 384
CAP = 3
NB = 144
HALO = 4
ROWS_X = TX + 2 * HALO
PAD = 8
WP = 32
WQ = 18
ROWS = 20
GROUP = 4 * ROWS
PROW = 256
LEFT = tuple(
    i for i in range(GX) if i < GX - 1 and (4 * (TX * i + TX + 2) - 11) // 26 + 1 - (4 * (TX * i - 3) - 11) // 26 >= WP
)
f32, bf16, i32 = jnp.float32, jnp.bfloat16, jnp.int32

diffuse_coef = 0.24
relax_coef = 0.3
drag_coefficient = 0.5


def iota(shape, dim):
    return lax.broadcasted_iota(i32, shape, dim)


def first_x(i):
    return (4 * (TX * i - 3) - 11) // 26


def first_y(j):
    return (4 * (TY * j - 3) - 11) // 26


def first_y_of(j):
    return ((4 * TY * j + 3) * 2521 >> 16) - 1


def first_x_of(i):
    return ((4 * TX * i + 3) * 2521 >> 16) - 1


def dot(a, b):
    return jnp.dot(a, b, preferred_element_type=f32)


def dot_nt(a, b):
    return lax.dot_general(a, b, (((1,), (1,)), ((), ())), preferred_element_type=f32)


def split3(x):
    high = x.astype(bf16)
    rest = x - high.astype(f32)
    mid = rest.astype(bf16)
    return high, mid, (rest - mid.astype(f32)).astype(bf16)


def column_of(row):
    n = row.shape[1]
    return jnp.sum(jnp.where(iota((n, n), 0) == iota((n, n), 1), row, 0), axis=1, keepdims=True)


def fetch(pairs, sems):
    copies = [pltpu.make_async_copy(src, dst, sems.at[k]) for k, (src, dst) in enumerate(pairs)]
    for copy in copies:
        copy.start()
    return copies


def rank_of(column, row, number):
    return jnp.sum(jnp.where((column == row) & (iota((NB, NB), 0) < number), 1, 0), axis=0, keepdims=True)


def by_thirds(column):
    at = iota((1, NB), 1)
    third = (at >= NB // CAP).astype(i32) + (at >= 2 * (NB // CAP)).astype(i32)
    number = CAP * (at - third * (NB // CAP)) + third
    return number, jnp.sum(jnp.where(iota((NB, NB), 0) == number, column, 0), axis=0, keepdims=True)


PARTS = 3
EDGE = 3
CORNER = F * EDGE * EDGE
FREE = 16
CORNERS = ((-1, -1), (-1, 1), (1, -1), (1, 1))


def neighbour(step):
    x, y = lax.axis_index("gx") + step[0], lax.axis_index("gy") + step[1]
    there = (x >= 0) & (x < GX) & (y >= 0) & (y < GY)
    return jnp.where(there, x * GY + y, 0), there


def corner_rows(wide_ref):
    lane, sub = iota((8, CELLS), 1), iota((8, CELLS), 0)
    out = jnp.zeros((8, CELLS), f32)
    for f in range(F):
        for k, (dx, dy) in enumerate(CORNERS):
            for r in range(EDGE):
                row = r if dx < 0 else TX - EDGE + r
                column = 0 if dy < 0 else TY - EDGE
                at = FREE + (f * EDGE + r) * EDGE
                moved = pltpu.roll(jnp.broadcast_to(wide_ref[f, row : row + 1, :], (8, CELLS)), (at - column) % CELLS, 1)
                out = jnp.where((sub == k) & (lane >= at) & (lane < at + EDGE), moved, out)
    high, mid, low = (x.astype(f32) for x in split3(out))
    return high + pltpu.roll(mid, CORNER, 1) + pltpu.roll(low, 2 * CORNER, 1)


def pack_kernel(
    wait, corner_ref, owner_ref, place_ref, parent_ref, s_ref, out_any, low_ref, high_ref, top_ref, bottom_ref,
    wide_ref, pick_ref, z_ref, out_ref, sems,
):
    wait(0)
    cx, cy = corner_ref[0], corner_ref[1]
    base = pl.multiple_of(jnp.minimum(jnp.maximum(cx - 1, 0) // 16 * 16, PC - PROW), 16)
    row = iota((GY * ROWS, 1), 0)
    j = row * 3277 >> 16
    r = row - j * ROWS
    wanted = jnp.where(r < WQ, cy + first_y_of(j) + r, -1)
    pick_y = (wanted == iota((GY * ROWS, PC), 1)).astype(f32).astype(bf16)
    lane = iota((1, 2 * CELLS), 1)
    for f in range(F):
        i = (lane >> 7) * F + (((lane >> 5) - f) & 3)
        p = cx - base + first_x_of(i) + (lane & (WP - 1))
        pick_ref[f] = (iota((PROW, 2 * CELLS), 0) == p).astype(f32).astype(bf16)
    wait(1)
    wait(2)
    owner = owner_ref[...]
    rank = rank_of(column_of(owner), owner, iota((NB, NB), 1))
    named = iota((DEV, NB), 0) == owner
    slots = jnp.zeros((DEV, CELLS), f32)
    for s in range(CAP):
        value = jnp.sum(jnp.where(named & (rank == s), place_ref[...] + 1, 0).astype(f32), axis=1, keepdims=True) - 1.0
        slots = jnp.where(iota((DEV, CELLS), 1) == s, value, slots)
    wait(4)
    wide_ref[...] = jnp.zeros_like(wide_ref)
    for f in range(F):
        wide_ref[f, :, :TY] = s_ref[f]
    corners = corner_rows(wide_ref)
    for k, step in enumerate(CORNERS):
        other, there = neighbour(step)
        slots = slots + jnp.where(iota((DEV, CELLS), 0) == jnp.where(there, other, -1), corners[k : k + 1, :], 0.0)
    wait(3)
    parts = [parent_ref[f, pl.ds(base, PROW), :] for f in range(F)]
    windows = [dot(dot_nt(pick_y, parts[f]).astype(bf16), pick_ref[f]) for f in range(F)]
    j16 = iota((GY, PC), 0)
    q = iota((GY, PC), 1) - (cy + first_y_of(j16))
    inside = (q >= 0) & (q < WQ)
    lanes = iota((GY, CELLS), 1) >> 5
    erow = iota((8, PROW), 0)
    target = jnp.full((8, PROW), -1, i32)
    for k, i in enumerate(LEFT):
        target = jnp.where(erow == k, cx - base + first_x(i) + WP, target)
    pick_row = (target == iota((8, PROW), 1)).astype(f32).astype(bf16)
    left = [jnp.zeros((GY, CELLS), f32) for _ in LEFT]
    for f in range(F):
        rows = dot(pick_row, parts[f])
        for k in range(len(LEFT)):
            kept = jnp.where(inside, rows[k : k + 1, :], 0.0)
            folded = kept[:, :128] + kept[:, 128:256] + kept[:, 256:]
            folded = folded + pltpu.roll(folded, 64, 1)
            folded = folded + pltpu.roll(folded, 32, 1)
            left[k] = jnp.where(lanes == f, folded, left[k])
    copies = []
    size = 2 * GY * ROWS
    quarter = iota((GY * ROWS, CELLS), 1) >> 5
    for pair in range(GX // 2):
        for i in (2 * pair, 2 * pair + 1):
            tile = slice(i // F * CELLS, i // F * CELLS + CELLS)
            message = windows[0][:, tile]
            for f in range(1, F):
                message = jnp.where(quarter == (f + i) % F, windows[f][:, tile], message)
            z_ref[pl.ds(i * GY * ROWS, GY * ROWS), :] = message
            if i in LEFT:
                z_ref[pl.ds(i * GY * ROWS + WQ, GY, stride=ROWS), :] = left[LEFT.index(i)]
        z_ref[pl.ds(pair * size + ROWS - 1, 2 * GY, stride=ROWS), :] = slots[2 * GY * pair : 2 * GY * (pair + 1)]
        copies.append(write(z_ref, out_ref, out_any, sems.at[pair], pl.ds(pair * size, size)))
    strips(wide_ref, low_ref, high_ref, top_ref, bottom_ref)
    for copy in copies:
        copy.wait()


def write(z_ref, out_ref, out_any, sem, at):
    out_ref[at, :] = z_ref[at, :].astype(bf16)
    copy = pltpu.make_async_copy(out_ref.at[at, :], out_any.at[at, :], sem)
    copy.start()
    return copy


def hat(fine, anchor, coarse):
    centre = (fine.astype(f32) + 0.5) * (2.0 / 13.0) - 0.5 + anchor.astype(f32)
    return jnp.maximum(0.0, 1.0 - jnp.abs(centre - coarse.astype(f32)))


FOLD = TX // (CELLS // (F * HALO))


def strips(wide_ref, low_ref, high_ref, top_ref, bottom_ref):
    field = iota((TX, CELLS), 1) >> 2
    low, high = jnp.zeros((TX, CELLS), f32), jnp.zeros((TX, CELLS), f32)
    for f in range(F):
        s = wide_ref[f]
        low = jnp.where(field == f, s if f == 0 else pltpu.roll(s, HALO * f, 1), low)
        high = jnp.where(field == f, pltpu.roll(s, CELLS - TY + HALO + HALO * f, 1), high)
        top_ref[f * HALO : (f + 1) * HALO, :] = pltpu.roll(s[:8], HALO, 1)[:HALO]
        bottom_ref[f * HALO : (f + 1) * HALO, :] = pltpu.roll(s[TX - 8 :], HALO, 1)[HALO:]
    for strip, ref in ((low, low_ref), (high, high_ref)):
        packed = strip[:FOLD]
        for g in range(1, TX // FOLD):
            packed = packed + pltpu.roll(strip[g * FOLD : (g + 1) * FOLD], g * F * HALO, 1)
        ref[...] = packed


def unfolded(packed):
    n = F * HALO
    return jnp.concatenate([packed] + [pltpu.roll(packed, CELLS - g * n, 1) for g in range(1, TX // FOLD)], axis=0)


def widened(s, left, right, f):
    lane = iota(s.shape, 1)
    before = left if f == 0 else pltpu.roll(left, CELLS - HALO * f, 1)
    after = pltpu.roll(right, TY + HALO - HALO * f, 1)
    wide = jnp.where(lane < TY + HALO, pltpu.roll(s, HALO, 1), after)
    return jnp.where(lane < HALO, before, jnp.where(lane < TY + 2 * HALO, wide, 0.0))


def corner_of(got_ref, step):
    other, there = neighbour(step)
    rows = got_ref[pl.ds(pl.multiple_of((other >> 2) * GROUP, 16), GROUP), :].astype(f32)
    mine = jnp.where(there, (other & 3) * ROWS + ROWS - 1, -1)
    row = jnp.sum(jnp.where(iota((GROUP, CELLS), 0) == mine, rows, 0.0), axis=0, keepdims=True)
    row = jnp.broadcast_to(row, (8, CELLS))
    return row + pltpu.roll(row, CELLS - CORNER, 1) + pltpu.roll(row, CELLS - 2 * CORNER, 1)


def nest_kernel(
    wait, holder_ref, corner_ref, owner_ref, got_ref, s_ref, left_ref, right_ref, before_ref, after_ref, skin_ref,
    next_any, out_any, wx_ref, wide_ref, next_ref, out_ref, state_ref, force_ref, flux_ref, z_ref, sems,
):
    wide_ref[...] = jnp.zeros_like(wide_ref)
    flux_ref[...] = jnp.zeros_like(flux_ref)
    corners = [corner_of(got_ref, step) for step in CORNERS]
    group = pl.multiple_of((holder_ref[0] >> 2) * GROUP, 16)
    got = got_ref[pl.ds(group, GROUP), :]
    wait(1)
    ix, iy = lax.axis_index("gx"), lax.axis_index("gy")
    cx, cy = corner_ref[0], corner_ref[1]
    x0, y0 = ix * TX - HALO, iy * TY - HALO
    px, qy = cx + first_x_of(ix), cy + first_y_of(iy)
    lane = iota((ROWS_X, CELLS), 1)
    row = iota((ROWS_X, CELLS), 0)
    weight = hat(row + x0, cx, (lane & (WP - 1)) + px)
    for f in range(F):
        wx_ref[f * ROWS_X : (f + 1) * ROWS_X, :] = jnp.where(lane >> 5 == ((f + ix) & 3), weight, 0.0).astype(bf16)
    weight_last = relax_coef / diffuse_coef * hat(row + x0, cx, jnp.full_like(row, WP) + px).astype(bf16).astype(f32)
    inside = (row + x0 >= 0) & (row + x0 < GX * TX) & (lane + y0 >= 0) & (lane + y0 < GY * TY)
    mask = jnp.where(inside, diffuse_coef, 0.0)
    for now in range(2):
        state_ref[:, now, :PAD, :] = jnp.zeros((F, PAD, CELLS), f32)
        state_ref[:, now, PAD + ROWS_X :, :] = jnp.zeros((F, PAD, CELLS), f32)
    at = iota((CELLS, GROUP), 1) - (holder_ref[0] & 3) * ROWS
    weight_y = jnp.where((at >= 0) & (at < WQ), hat(iota((CELLS, GROUP), 0) + y0, cy, at + qy), 0.0).astype(bf16)
    lane = iota((CELLS, CELLS), 1)
    weight_c = hat(iota((CELLS, CELLS), 0) + y0, cy, qy + ((lane - qy) & (WP - 1))).astype(bf16)
    partial = dot(weight_y, got).astype(bf16)
    last = jnp.sum(
        jnp.where(iota((GROUP, CELLS), 0) == (holder_ref[0] & 3) * ROWS + WQ, got.astype(f32), 0.0), axis=0, keepdims=True
    )
    last = jnp.where(iota((8, CELLS), 1) >> 5 == iota((8, CELLS), 0), last, 0.0).astype(bf16)
    partial_last = dot_nt(last, weight_c).astype(bf16).astype(f32)
    force_ref[...] = dot_nt(wx_ref[...], partial)
    wait(2)
    column = column_of(owner_ref[...])
    number, owner = by_thirds(column)
    send = (iota((CAP * DEV, NB), 0) == rank_of(column, owner, number) * DEV + owner).astype(f32).astype(bf16)
    wait(4)
    left, right = unfolded(left_ref[...]), unfolded(right_ref[...])
    lane, sub = iota((8, CELLS), 1), iota((8, CELLS), 0)
    written = []
    for f in range(F):
        force = relax_coef / diffuse_coef * force_ref[f * ROWS_X : (f + 1) * ROWS_X, :] + weight_last * partial_last[f : f + 1, :]
        wide_ref[f, :, :TY] = s_ref[f]
        state_ref[f, 0, PAD : PAD + HALO, :] = before_ref[f * HALO : (f + 1) * HALO, :]
        state_ref[f, 0, PAD + HALO : PAD + HALO + TX, :] = widened(wide_ref[f], left, right, f)
        state_ref[f, 0, PAD + HALO + TX : PAD + ROWS_X, :] = after_ref[f * HALO : (f + 1) * HALO, :]
        for side, base in ((-1, PAD), (1, PAD + ROWS_X - 8)):
            tile = state_ref[f, 0, base : base + 8, :]
            for k, (dx, dy) in enumerate(CORNERS):
                for r in range(EDGE if dx == side else 0):
                    row = HALO - EDGE + r if dx < 0 else 8 - HALO + r
                    column = HALO - EDGE if dy < 0 else HALO + TY
                    at = FREE + (f * EDGE + r) * EDGE
                    moved = pltpu.roll(corners[k], (column - at) % CELLS, 1)
                    tile = jnp.where((sub == row) & (lane >= column) & (lane < column + EDGE), moved, tile)
            state_ref[f, 0, base : base + 8, :] = tile
        s = state_ref[f, 0, PAD : PAD + ROWS_X, :]
        for step in range(STEPS):
            now = step % 2
            beside = state_ref[f, now, PAD - 1 : PAD - 1 + ROWS_X, :] + state_ref[f, now, PAD + 1 : PAD + 1 + ROWS_X, :]
            beside = beside + (pltpu.roll(s, 1, 1) + pltpu.roll(s, CELLS - 1, 1))
            s = mask * ((1.0 - 4.0 * diffuse_coef - relax_coef) / diffuse_coef * s + beside + force)
            state_ref[f, 1 - now, PAD : PAD + ROWS_X, :] = s if step < STEPS - 1 else pltpu.roll(s, CELLS - HALO, 1)
        last_state = state_ref.at[f, STEPS % 2]
        next_ref[f] = last_state[PAD + HALO : PAD + HALO + TX, :TY]
    u, v, ta, qa = next_ref[0], next_ref[1], next_ref[2], next_ref[3]
    half = drag_coefficient * jnp.sqrt(1.0 + u * u + v * v)
    written.append(pltpu.make_async_copy(next_ref, next_any, sems.at[4]))
    written[0].start()
    wait(9)
    skin = skin_ref[...]
    flux = (half * (ta - skin), half * (qa - 0.5 * skin), half * u, half * v)
    rows = NB // CAP
    lane = iota((rows, CELLS), 1)
    blocks = []
    for f in range(F):
        flux_ref[f, :, :TY] = flux[f]
        m = [flux_ref[f, pl.ds(k, rows, stride=4), :] for k in range(4)]
        r1, r2, r3 = pltpu.roll(m[1], 96, 1), pltpu.roll(m[2], 64, 1), pltpu.roll(m[3], 32, 1)
        blocks.append(
            jnp.concatenate(
                [jnp.where(lane < 96, m[0], r1), jnp.where(lane < 64, r1, r2), jnp.where(lane < 32, r2, r3)], axis=0
            ).astype(bf16)
        )
    sent = dot(send, jnp.concatenate(blocks, axis=1))
    part = DEV // 4
    for c in range(4):
        for slot in range(CAP):
            for f in range(F):
                z_ref[pl.ds(c * part * CAP * F + slot * F + f, part, stride=CAP * F), :] = sent[
                    slot * DEV + c * part : slot * DEV + (c + 1) * part, f * CELLS : (f + 1) * CELLS
                ]
        written.append(write(z_ref, out_ref, out_any, sems.at[c], pl.ds(c * part * CAP * F, part * CAP * F)))
    for copy in written:
        copy.wait()


def hot_kernel(
    got_ref, kept_ref, owner_ref, hot_ref, give_ref, inverse_ref, cover_ref, back_ref, z_ref, slot_ref, row_ref
):
    column = column_of(owner_ref[...])
    number, owner = by_thirds(column)
    source = column_of(owner * CAP + rank_of(column, owner, number))
    back_ref[...] = (source == iota((NB, CAP * DEV), 1)).astype(f32).astype(bf16)
    slot_ref[...] = got_ref[...].astype(f32)
    slots = slot_ref[pl.ds(ROWS - 1, DEV, stride=ROWS), :].astype(i32)
    lane = iota((DEV, OCEAN * F), 1)
    for s in range(CAP):
        target = slots[:, s : s + 1] * F
        for f in range(F):
            z_ref[pl.ds(s * F + f, DEV, stride=CAP * F), :] = (lane == jnp.where(target < 0, -1, target + f)).astype(f32)
        row_ref[pl.ds(s, DEV, stride=CAP), :] = (lane == target).astype(f32)
    give_ref[...] = row_ref[...].astype(bf16)
    hot = jnp.swapaxes(z_ref[...], 0, 1)
    hot_ref[...] = hot.astype(bf16)
    count = jnp.sum(hot, axis=1, keepdims=True)
    inverse_ref[...] = jnp.broadcast_to(1.0 / jnp.maximum(count, 1.0), (OCEAN * F, CELLS))
    cover_ref[...] = jnp.where(count == 0.0, kept_ref[...], 0.0)


def top_kernel(scale_ref, marine_ref, out_ref):
    total = scale_ref[0, 0] * marine_ref[0]
    for k in range(1, marine_ref.shape[0]):
        total = total + scale_ref[0, k] * marine_ref[k]
    out_ref[: OCEAN * F, :] = total
    out_ref[OCEAN * F :, :] = jnp.full((8, CELLS), scale_ref[0, 0], f32)


def ocean_kernel(wait, got_ref, hot_ref, inverse_ref, cover_ref, top_ref, give_ref, forcing_ref, out_ref):
    wait(1)
    wait(0)
    sums = dot(hot_ref[...], got_ref[...])
    for k in (2, 3, 4, 5):
        wait(k)
    forcing = sums * inverse_ref[...] + cover_ref[...]
    forcing_ref[...] = forcing
    top = top_ref[: OCEAN * F, :] + top_ref[OCEAN * F : OCEAN * F + 1, :] * forcing
    back = dot(give_ref[...], jnp.concatenate(split3(top), axis=1))
    out_ref[...] = back[:, :CELLS] + back[:, CELLS : 2 * CELLS] + back[:, 2 * CELLS :]

def mix_kernel(scale_ref, forcing_ref, marine_ref, out_ref, high_ref, low_ref):
    layers = marine_ref.shape[0]
    n = 8 * layers

    @pl.when(pl.program_id(0) == 0)
    def _():
        spread = (iota((n, layers), 0) >> 3 == iota((n, layers), 1)).astype(f32).astype(bf16)
        same = (iota((n, n), 0) & 7) == (iota((n, n), 1) & 7)
        scale = scale_ref[...]
        high = scale.astype(bf16)
        low = (scale - high.astype(f32)).astype(bf16)
        for part, ref in ((high, high_ref), (low, low_ref)):
            wide = dot_nt(dot(spread, part).astype(bf16), spread)
            ref[...] = jnp.where(same, wide, 0.0).astype(bf16)

    groups = marine_ref.shape[1] // 8
    columns = []
    for g in range(groups):
        x = marine_ref[:, 8 * g : 8 * g + 8, :].reshape(n, CELLS)
        first = x[:8] + forcing_ref[8 * g : 8 * g + 8, :]
        columns.append(jnp.concatenate([first, x[8:]], axis=0))
    x = jnp.concatenate(columns, axis=1)
    high = x.astype(bf16)
    low = (x - high.astype(f32)).astype(bf16)
    y = dot(high_ref[...], high) + (dot(high_ref[...], low) + dot(low_ref[...], high))
    for g in range(groups):
        out_ref[:, 8 * g : 8 * g + 8, :] = y[:, g * CELLS : (g + 1) * CELLS].reshape(layers, 8, CELLS)


def skin_kernel(got_ref, back_ref, out_ref, tile_ref):
    x = dot(back_ref[...], jnp.concatenate(split3(got_ref[...]), axis=1))
    x = x[:, :CELLS] + x[:, CELLS : 2 * CELLS] + x[:, 2 * CELLS :]
    rows = NB // CAP
    t0, t1, t2 = x[:rows], x[rows : 2 * rows], x[2 * rows :]
    lane = iota((rows, CELLS), 1)
    tile_ref[pl.ds(0, rows, stride=4), :] = t0
    tile_ref[pl.ds(1, rows, stride=4), :] = pltpu.roll(jnp.where(lane < 64, t1, t0), 32, 1)
    tile_ref[pl.ds(2, rows, stride=4), :] = pltpu.roll(jnp.where(lane < 32, t2, t1), 64, 1)
    tile_ref[pl.ds(3, rows, stride=4), :] = pltpu.roll(t2, 96, 1)
    out_ref[...] = tile_ref[:, :TY]


MEMORY = {"h": pltpu.HBM, "v": pltpu.VMEM, "H": pltpu.HBM, "S": pltpu.HBM}
SPACES = {"h": pltpu.HBM, "v": pltpu.VMEM, "H": pltpu.HBM, "S": pltpu.HBM, "p": pltpu.VMEM, "s": pltpu.SMEM}


def call(kernel, ins, outs, args, shapes, scratch=(), copies=0, lazy=False):
    args = [pltpu.with_memory_space_constraint(a, MEMORY[c]) if c in MEMORY else a for c, a in zip(ins, args)]
    letters = ins + outs
    kinds = [(a.shape, a.dtype) for a in args] + list(shapes)
    moved = [k for k, c in enumerate(letters) if c in "HS"]
    own = len(scratch) + (1 if copies else 0)

    def body(*refs):
        arrays, rest = list(refs[: len(letters)]), refs[len(letters) :]
        sems = rest[-1]
        far = [arrays[k] for k in moved]
        for n, k in enumerate(moved):
            arrays[k] = rest[own + n]
        pending = {k: pltpu.make_async_copy(far[n], arrays[k], sems.at[n]) for n, k in enumerate(moved) if k < len(ins)}
        for copy in pending.values():
            copy.start()
        if lazy:
            kernel(lambda k: pending[k].wait(), *arrays, *rest[:own])
        else:
            for copy in pending.values():
                copy.wait()
            kernel(*arrays, *rest[:own])
        done = [pltpu.make_async_copy(arrays[k], far[n], sems.at[n]) for n, k in enumerate(moved) if k >= len(ins)]
        for copy in done:
            copy.start()
        for copy in done:
            copy.wait()

    return pl.pallas_call(
        body,
        out_shape=tuple(MEMORY[c](s, d) if c in MEMORY else jax.ShapeDtypeStruct(s, d) for c, (s, d) in zip(outs, shapes)),
        in_specs=[pl.BlockSpec(memory_space=SPACES[c]) for c in ins],
        out_specs=tuple(pl.BlockSpec(memory_space=SPACES[c]) for c in outs),
        scratch_shapes=[pltpu.VMEM(s, d) for s, d in scratch]
        + ([pltpu.SemaphoreType.DMA((copies,))] if copies else [])
        + [(pltpu.SMEM if letters[k] == "S" else pltpu.VMEM)(*kinds[k]) for k in moved]
        + [pltpu.SemaphoreType.DMA((max(1, len(moved)),))],
        compiler_params=pltpu.CompilerParams(vmem_limit_bytes=32 << 20),
    )(*args)


def shift(value, axis, by):
    n = lax.axis_size(axis)
    return lax.ppermute(value, axis, [(i, i + by) for i in range(n) if 0 <= i + by < n])


def exchange(value, rows):
    split = value.reshape(rows)
    return lax.all_to_all(split, ("gx", "gy"), split_axis=0, concat_axis=0, tiled=True).reshape(value.shape)


def by_block(value):
    return value.reshape(F, OCEAN, CELLS).transpose(1, 0, 2).reshape(OCEAN * F, CELLS)


def on_device(
    fine_atmospheric_values,
    fine_skin_heat,
    coarse_lowest_values,
    holder_flat,
    corner_offset,
    exchange_patch_holder,
    holder_patch_position,
    coarse_interface_exchange,
    marine_stratum_values,
    diffusion_solver_operator,
):
    owner = exchange_patch_holder.reshape(1, NB)
    place = holder_patch_position.reshape(1, NB)
    names, message, tile, strip = ((1, NB), i32), ((DEV * ROWS, CELLS), bf16), ((F, TX, TY), f32), ((TX, CELLS), f32)
    ends, fold, whole = ((F * HALO, CELLS), f32), ((FOLD, CELLS), f32), ((F, TX, CELLS), f32)
    windows, low, high, top, bottom = call(
        pack_kernel, "SHHHH", "hvvvv", (corner_offset, owner, place, coarse_lowest_values, fine_atmospheric_values),
        (message, fold, fold, ends, ends),
        (whole, ((F, PROW, 2 * CELLS), bf16), ((DEV * ROWS, CELLS), f32), message), 4, True,
    )
    got = exchange(windows, (DEV, ROWS // 4, 4, CELLS))
    left, right = shift(high, "gy", 1), shift(low, "gy", -1)
    before, after = shift(bottom, "gx", 1), shift(top, "gx", -1)
    holder = holder_flat
    sent, strips = ((DEV * CAP * F, CELLS), bf16), ((F, TX, CELLS), f32)
    nest_next, flux = call(
        nest_kernel, "sSHvHvvvvH", "hh",
        (holder, corner_offset, owner, got, fine_atmospheric_values, left, right, before, after, fine_skin_heat), (tile, sent),
        (
            ((F * ROWS_X, CELLS), bf16), strips, tile, sent, ((F, 2, ROWS_X + 2 * PAD, CELLS), f32),
            ((F * ROWS_X, CELLS), f32), strips, ((DEV * CAP * F, CELLS), f32),
        ), 5, True,
    )
    got_flux = exchange(flux, (DEV, CAP, F, CELLS))
    layers = marine_stratum_values.shape[1]
    marine = marine_stratum_values.reshape(F, layers, OCEAN, CELLS).transpose(1, 2, 0, 3).reshape(layers, OCEAN * F, CELLS)
    marine_late, got_late, flux = lax.optimization_barrier((marine, got, flux))
    block = ((OCEAN * F, CELLS), f32)
    hot, give = ((OCEAN * F, DEV * CAP * F), bf16), ((DEV * CAP, OCEAN * F), bf16)
    hot, give, inverse, cover, back = call(
        hot_kernel, "vHH", "HHHHv", (got_late, by_block(coarse_interface_exchange), owner),
        (hot, give, block, block, ((NB, CAP * DEV), bf16)),
        (((DEV * CAP * F, OCEAN * F), f32), ((DEV * ROWS, CELLS), f32), ((DEV * CAP, OCEAN * F), f32)),
    )
    (layer0,) = call(top_kernel, "Sp", "H", (diffusion_solver_operator, marine_late), (((OCEAN * F + 8, CELLS), f32),))
    returned = ((DEV * CAP, CELLS), f32)
    forcing, skins = call(
        ocean_kernel, "HHHHHH", "HH", (got_flux, hot, inverse, cover, layer0, give), (block, returned),
        lazy=True,
    )
    arrived = exchange(skins, (DEV, 1, CAP * CELLS))
    part = 32
    refreshed = pl.pallas_call(
        mix_kernel,
        out_shape=jax.ShapeDtypeStruct((layers, OCEAN * F, CELLS), f32),
        grid=(OCEAN * F // part,),
        in_specs=[
            pl.BlockSpec((layers, layers), lambda g: (0, 0)),
            pl.BlockSpec((part, CELLS), lambda g: (g, 0)),
            pl.BlockSpec((layers, part, CELLS), lambda g: (0, g, 0)),
        ],
        out_specs=pl.BlockSpec((layers, part, CELLS), lambda g: (0, g, 0)),
        scratch_shapes=[pltpu.VMEM((8 * layers, 8 * layers), bf16)] * 2,
        compiler_params=pltpu.CompilerParams(vmem_limit_bytes=40 << 20),
    )(diffusion_solver_operator, forcing, marine)
    refreshed = refreshed.reshape(layers, OCEAN, F, CELLS).transpose(2, 0, 1, 3).reshape(marine_stratum_values.shape)
    (skin,) = call(skin_kernel, "vv", "p", (arrived, back), (((TX, TY), f32),), (((TX, CELLS), f32),))
    return (nest_next, refreshed, skin)


def solution(mesh):
    in_specs = (
        P(None, "gx", "gy"),
        P("gx", "gy"),
        P(None, "gx", "gy"),
        P(),
        P(),
        P(("gx", "gy"), None),
        P(("gx", "gy")),
        P(None, ("gx", "gy")),
        P(None, None, ("gx", "gy")),
        P(),
    )
    out_specs = (P(None, "gx", "gy"), P(None, None, ("gx", "gy")), P("gx", "gy"))
    return jax.shard_map(
        on_device, mesh=mesh, in_specs=in_specs, out_specs=out_specs, check_vma=False
    )
```
